32 devices in a mesh: dp: 16 (over z, y, x), seq: 2 (over core).
Axes of the slice: x: 2, y: 2, z: 4, core: 2. Of those that a mesh axis runs over, the one named last changes fastest.
Arguments:
- hidden_in: bfloat16 [4, 8192, 768], P(None, ('dp', 'seq')), may hold values from -6 to 6
- slot_sizes: int32 [16, 4, 8], P('dp'), may hold values from 0 to 512, as said below
- live_lengths: int32 [16, 4, 8], P('dp'), may hold values from 0 to 512, as said below
- w_query: bfloat16 [768, 768], replicated, may hold values from -0.21875 to 0.21875
- w_key: bfloat16 [768, 768], replicated, may hold values from -0.21875 to 0.21875
- w_value: bfloat16 [768, 768], replicated, may hold values from -0.21875 to 0.21875
- query_down_factor: bfloat16 [768, 8], replicated, may hold values from -0.21875 to 0.21875
- down_value: bfloat16 [768, 8], replicated, may hold values from -0.21875 to 0.21875
- query_up_factor: bfloat16 [8, 768], replicated, may hold values from -0.75 to 0.75
- value_up_factor: bfloat16 [8, 768], replicated, may hold values from -0.75 to 0.75
- w_output: bfloat16 [768, 768], replicated, may hold values from -1.75 to 1.75
- attn_gain: float32 [768], replicated, may hold values from 0.5 to 1.5
- attn_shift: float32 [768], replicated, may hold values from -4 to 4
- w_expand: bfloat16 [768, 3072], replicated, may hold values from -0.21875 to 0.21875
- w_reduce: bfloat16 [3072, 768], replicated, may hold values from -0.109375 to 0.109375
- ffn_gain: float32 [768], replicated, may hold values from 0.5 to 1.5
- ffn_shift: float32 [768], replicated, may hold values from -4 to 4
- out_grad: bfloat16 [4, 8192, 768], P(None, ('dp', 'seq')), may hold values from -6 to 6
Outputs:
- layer_out: bfloat16 [4, 8192, 768], P(None, ('dp', 'seq'))
- input_grad: float32 [4, 8192, 768], P(None, ('dp', 'seq'))
- up_query_grad: float32 [8, 768], replicated
- up_value_grad: float32 [8, 768], replicated
The draws below stay inside these ranges and needn't reach their ends.
Inputs may be any that keep to these rules, and one draw needn't show every extreme that they name: `slot_sizes`: for each packed row the used slots come first, hold sizes 64, 128, 256 or 512 that sum to 512, the rest are 0; for each g one micro-batch holds a single item of 512 tokens. `live_lengths`: each entry lies between half of its slot's size (rounded up) and the size; 0 for unused slots; an item of 512 tokens is live throughout.
All inputs are finite; a program needn't handle non-finite values.
Results may differ from the reference program's by a relative error of at most 0.02.
Values may be sent and summed in bfloat16 or wider, within the bound.
A program may use at most 192 MiB of HBM per device.

```python
import math
import jax
import jax.numpy as jnp
from jax import lax

D = 768
HEADS = 12
HD = 64
FF = 3072
ADAPTER_RANK = 8
SLOTS = 8
MB = 4
GROUP = 512
UNIT = 64
ROWS = 8192
N_DP = 16


def pack_layout(key):
    subkeys = jax.random.split(key, 4)
    whole_batch = jax.random.randint(subkeys[0], (N_DP,), 0, MB)
    split_half = jax.random.randint(subkeys[1], (N_DP, MB, 2), 0, 2)
    split_quarter = jax.random.randint(subkeys[2], (N_DP, MB, 4), 0, 2)
    unit_index = jnp.arange(SLOTS, dtype=jnp.int32)
    halves = split_half[:, :, unit_index // 4]
    quarters = split_quarter[:, :, unit_index // 2]
    extent = jnp.where(halves == 0, 4, jnp.where(quarters == 0, 2, 1)).astype(jnp.int32)
    single = (jnp.arange(MB, dtype=jnp.int32)[None, :] == whole_batch[:, None])[:, :, None]
    extent = jnp.where(single, 8, extent).astype(jnp.int32)
    opens = (unit_index[None, None, :] % extent == 0).astype(jnp.int32)
    order = jnp.argsort(1 - opens, axis=-1, stable=True)
    extent = jnp.take_along_axis(extent, order, axis=-1)
    opens = jnp.take_along_axis(opens, order, axis=-1)
    sizes_out = (opens * extent * UNIT).astype(jnp.int32)
    trims = jax.random.randint(subkeys[3], sizes_out.shape, 0, sizes_out // 2 + 1)
    lives = sizes_out - jnp.where(sizes_out == GROUP, 0, trims)
    return (sizes_out, lives.astype(jnp.int32))


def draw_slot_sizes(key, part):
    return pack_layout(key)[0]


def draw_live_lengths(key, part):
    return pack_layout(key)[1]


def shard_levels(stream_key, dims, cuts, low, high):
    level = 1.0
    for dim, parts in cuts:
        heights = jax.random.uniform(jax.random.fold_in(jax.random.fold_in(stream_key, 6), dim), (parts,), jnp.float32, low / len(cuts), high / len(cuts))
        level = level * jnp.repeat(jnp.exp(heights), dims[dim] // parts).reshape((-1,) + (1,) * (len(dims) - 1 - dim))
    return level


def noise(stream_key, shape, deviation, bound, cuts=(), kind=jnp.bfloat16):
    result = jax.random.normal(stream_key, shape, jnp.float32) * deviation
    if len(cuts) > 0:
        result = shard_levels(stream_key, shape, cuts, -0.22, 0.18) * result
    return jnp.clip(result, min=-bound, max=bound).astype(kind)


def setup_inputs(seed: int = 0) -> dict:
    key_of = jax.random.split(jax.random.key(seed), 19)
    hidden_in = noise(key_of[0], (MB, ROWS, D), 1.0, 6.0, ((1, 32),))
    slot_sizes = draw_slot_sizes(jax.random.fold_in(key_of[18], 71), 0)
    live_lengths = draw_live_lengths(jax.random.fold_in(key_of[18], 71), 0)
    w_query = noise(key_of[3], (D, D), D ** -0.5, 0.21875)
    w_key = noise(key_of[4], (D, D), D ** -0.5, 0.21875)
    w_value = noise(key_of[5], (D, D), D ** -0.5, 0.21875)
    query_down_factor = noise(key_of[6], (D, ADAPTER_RANK), D ** -0.5, 0.21875)
    down_value = noise(key_of[7], (D, ADAPTER_RANK), D ** -0.5, 0.21875)
    query_up_factor = noise(key_of[8], (ADAPTER_RANK, D), (8 * ADAPTER_RANK) ** -0.5, 0.75)
    value_up_factor = noise(key_of[9], (ADAPTER_RANK, D), (8 * ADAPTER_RANK) ** -0.5, 0.75)
    w_output = noise(key_of[10], (D, D), (D // 64) ** -0.5, 1.75)
    attn_gain = jnp.clip(1.0 + 0.1 * jax.random.normal(key_of[11], (D,), jnp.float32), 0.5, 1.5)
    attn_shift = noise(key_of[12], (D,), 0.3, 4.0, (), jnp.float32)
    w_expand = noise(key_of[13], (D, FF), D ** -0.5, 0.21875)
    w_reduce = noise(key_of[14], (FF, D), FF ** -0.5, 0.109375)
    ffn_gain = jnp.clip(1.0 + 0.1 * jax.random.normal(key_of[15], (D,), jnp.float32), 0.5, 1.5)
    ffn_shift = noise(key_of[16], (D,), 0.3, 4.0, (), jnp.float32)
    out_grad = noise(key_of[17], (MB, ROWS, D), 1.0, 6.0, ((1, 32),))
    return {"hidden_in": hidden_in, "slot_sizes": slot_sizes, "live_lengths": live_lengths, "w_query": w_query, "w_key": w_key, "w_value": w_value, "query_down_factor": query_down_factor, "down_value": down_value, "query_up_factor": query_up_factor, "value_up_factor": value_up_factor, "w_output": w_output, "attn_gain": attn_gain, "attn_shift": attn_shift, "w_expand": w_expand, "w_reduce": w_reduce, "ffn_gain": ffn_gain, "ffn_shift": ffn_shift, "out_grad": out_grad}


MASK_FILL = -1e+30
NORM_EPS = 1e-05
ADAPTER_STRENGTH = 16.0

@jax.custom_vjp
def reduced_projection(v):
    return lax.optimization_barrier(v.astype(jnp.bfloat16)).astype(jnp.float32)

@jax.custom_vjp
def reduced_gradient(v):
    return v

def low_keep(v):
    return (reduced_projection(v), None)

def low_pass(kept, grad):
    return (grad,)

def back_keep(v):
    return (v, None)

def back_low(kept, grad):
    return (reduced_projection(grad),)
reduced_projection.defvjp(low_keep, low_pass)
reduced_gradient.defvjp(back_keep, back_low)

def matrix_product(left, right):
    return jnp.dot(left, right, precision=lax.Precision.HIGHEST)

def locate(size_table, live_table, positions):
    starts = jnp.cumsum(size_table, axis=-1) - size_table
    member = (starts[:, None, :] <= positions[None, :, None]).astype(jnp.int32)
    item_ids = lax.optimization_barrier(jnp.sum(member, axis=-1)) - 1
    slot_index = jnp.arange(size_table.shape[-1], dtype=jnp.int32)
    onehot = (item_ids[:, :, None] == slot_index[None, None, :]).astype(jnp.int32)
    item_start = lax.optimization_barrier(jnp.sum(onehot * starts[:, None, :], axis=-1))
    extent = lax.optimization_barrier(jnp.sum(onehot * live_table[:, None, :], axis=-1))
    return (item_ids, positions[None, :] - item_start < extent)

def layer_norm(resid, gain, shift):
    center = resid - lax.optimization_barrier(jnp.mean(resid, axis=-1, keepdims=True))
    spread = lax.optimization_barrier(jnp.mean(center * center, axis=-1, keepdims=True))
    return center * lax.rsqrt(spread + NORM_EPS) * gain + shift

def reference(hidden_in, slot_sizes, live_lengths, w_query, w_key, w_value, query_down_factor, down_value, query_up_factor, value_up_factor, w_output, attn_gain, attn_shift, w_expand, w_reduce, ffn_gain, ffn_shift, out_grad):
    query_weight_matrix = w_query.astype(jnp.float32)
    wk = w_key.astype(jnp.float32)
    value_weight_matrix = w_value.astype(jnp.float32)
    aq = query_down_factor.astype(jnp.float32)
    av = down_value.astype(jnp.float32)
    wo = w_output.astype(jnp.float32)
    wx = w_expand.astype(jnp.float32)
    wr = w_reduce.astype(jnp.float32)
    adapter_scale_factor = ADAPTER_STRENGTH / ADAPTER_RANK
    score_scale = 1.0 / math.sqrt(HD)
    seq_inputs = hidden_in.astype(jnp.float32).reshape(MB * N_DP, GROUP, D)
    seq_grads = out_grad.astype(jnp.float32).reshape(MB * N_DP, GROUP, D)
    size_rows = jnp.transpose(slot_sizes, (1, 0, 2)).reshape(MB * N_DP, SLOTS)
    live_rows = jnp.transpose(live_lengths, (1, 0, 2)).reshape(MB * N_DP, SLOTS)
    positions = jnp.arange(GROUP, dtype=jnp.int32)

    def per_sequence(totals, inputs):
        seq_input, seq_grad, size_row, live_row = inputs
        item_ids, key_live = locate(size_row[None], live_row[None], positions)
        allowed = (item_ids[0][:, None] == item_ids[0][None, :]) & key_live[0][None, :]

        def forward(sequence_input, query_bias_vector, value_bias_vector):
            narrow_query_rows = reduced_gradient(reduced_projection(matrix_product(sequence_input, aq)))
            narrow_value_rows = reduced_gradient(reduced_projection(matrix_product(sequence_input, av)))
            query_output = reduced_gradient(reduced_projection(matrix_product(sequence_input, query_weight_matrix) + adapter_scale_factor * matrix_product(narrow_query_rows, query_bias_vector)))
            keys = reduced_gradient(reduced_projection(matrix_product(sequence_input, wk)))
            value_output = reduced_gradient(reduced_projection(matrix_product(sequence_input, value_weight_matrix) + adapter_scale_factor * matrix_product(narrow_value_rows, value_bias_vector)))
            query_output = query_output.reshape(GROUP, HEADS, HD)
            keys = keys.reshape(GROUP, HEADS, HD)
            value_output = value_output.reshape(GROUP, HEADS, HD)
            scores = jnp.einsum('qhd,khd->hqk', query_output, keys, precision=lax.Precision.HIGHEST) * score_scale
            scores = reduced_gradient(scores)
            scores = jnp.where(allowed[None], scores, MASK_FILL)
            top = lax.optimization_barrier(jnp.max(scores, axis=-1, keepdims=True))
            expo = jnp.exp(scores - top)
            probs = reduced_projection(expo / lax.optimization_barrier(jnp.sum(expo, axis=-1, keepdims=True)))
            context = jnp.einsum('hqk,khd->qhd', probs, value_output, precision=lax.Precision.HIGHEST).reshape(GROUP, D)
            context = reduced_gradient(reduced_projection(context))
            attended = reduced_gradient(matrix_product(context, wo))
            hidden = layer_norm(sequence_input + attended, attn_gain, attn_shift)
            inner = reduced_gradient(matrix_product(reduced_projection(hidden), wx))
            active = reduced_projection(jax.nn.gelu(inner, approximate=False))
            branch = reduced_gradient(matrix_product(active, wr))
            return layer_norm(hidden + branch, ffn_gain, ffn_shift)
        seq_out, puller = jax.vjp(forward, seq_input, query_up_factor.astype(jnp.float32), value_up_factor.astype(jnp.float32))
        grad_in, grad_bq, grad_bv = puller(seq_grad)
        return ((totals[0] + grad_bq, totals[1] + grad_bv), (seq_out, grad_in))
    start_grads = (jnp.zeros((ADAPTER_RANK, D), jnp.float32), jnp.zeros((ADAPTER_RANK, D), jnp.float32))
    sums, outputs = lax.scan(per_sequence, start_grads, (seq_inputs, seq_grads, size_rows, live_rows))
    layer_out = outputs[0].reshape(MB, N_DP * GROUP, D).astype(jnp.bfloat16)
    input_grad = outputs[1].reshape(MB, N_DP * GROUP, D)
    return (layer_out, input_grad, sums[0], sums[1])
```

```python
import functools
import math

import jax
import jax.numpy as jnp
from jax import lax
from jax.experimental import pallas as pl
from jax.experimental.pallas import tpu as pltpu
from jax.sharding import PartitionSpec as P

HEADS = 12
HEAD = 64
NORM_EPS = 1e-05
ADAPTER_STRENGTH = 16.0
MASK_FILL = -1e30
LOG2_E = math.log2(math.e)
LN_2 = math.log(2.0)
CHUNK = 512
BF16 = jnp.bfloat16
F32 = jnp.float32
MESH = pl.DeviceIdType.MESH
VMEM = pltpu.VMEM
HBM_SPEC = pl.BlockSpec(memory_space=pl.ANY)
VMEM_SPEC = pl.BlockSpec(memory_space=pltpu.VMEM)
SMEM_SPEC = pl.BlockSpec(memory_space=pltpu.SMEM)


def dot(left, right, over_left, over_right):
    return lax.dot_general(
        left, right, (((over_left,), (over_right,)), ((), ())), preferred_element_type=F32
    )


def project_kernel(
    hidden, out_grad, wq, wk, wv, aq, av, bq, bv,
    qt_out, k_out, kt_out, v_out, vt_out, low_out, x_out, og_out, wq_out, wv_out,
    x_own, x_got, wq_s, wk_s, wv_s, qt_s, k_s, kt_s, v_s, vt_s, load, store, send, recv, own_sem,
):
    micro, tokens, width = hidden.shape
    rows = micro // 2
    place = lax.axis_index("seq")
    other = 1 - place
    loads = [
        pltpu.make_async_copy(hidden.at[pl.ds(rows * place, rows)], x_own, load.at[0]),
        pltpu.make_async_copy(wq, wq_s, load.at[1]),
        pltpu.make_async_copy(wk, wk_s, load.at[2]),
        pltpu.make_async_copy(wv, wv_s, load.at[3]),
    ]
    for copy in loads:
        copy.start()
    barrier = pltpu.get_barrier_semaphore()
    pl.semaphore_signal(barrier, inc=1, device_id={"seq": other}, device_id_type=MESH)
    pl.semaphore_wait(barrier, 1)
    x_copy = pltpu.make_async_remote_copy(
        src_ref=hidden.at[pl.ds(rows * other, rows)], dst_ref=x_got,
        send_sem=send.at[0], recv_sem=recv.at[0],
        device_id={"seq": other}, device_id_type=MESH,
    )
    x_copy.start()
    og_copy = pltpu.make_async_remote_copy(
        src_ref=out_grad.at[pl.ds(rows * other, rows)], dst_ref=og_out,
        send_sem=send.at[1], recv_sem=recv.at[1],
        device_id={"seq": other}, device_id_type=MESH,
    )
    og_copy.start()
    strength = ADAPTER_STRENGTH / aq.shape[0]
    for copy in loads:
        copy.wait()
    wq_s[...] = (
        (wq_s[...].astype(F32) + strength * dot(aq[...], bq[...], 0, 0))
        * (LOG2_E / math.sqrt(HEAD))
    ).astype(BF16)
    wv_s[...] = (
        wv_s[...].astype(F32) + strength * dot(av[...], bv[...], 0, 0)
    ).astype(BF16)
    stores = []

    def keep(source, target):
        copy = pltpu.make_async_copy(source, target, store.at[len(stores)])
        copy.start()
        stores.append(copy)

    keep(wq_s, wq_out)
    keep(wv_s, wv_out)
    for half in range(2):
        if half == 1:
            x_copy.wait_recv()
            keep(x_got, x_out)
        x = (x_own if half == 0 else x_got)[...].reshape(rows * tokens, width)
        span = slice(half * tokens, (half + 1) * tokens)
        qt = dot(wq_s[...], x, 0, 1).astype(BF16)
        keys = dot(x, wk_s[...], 1, 0).astype(BF16)
        vt = dot(wv_s[...], x, 0, 1).astype(BF16)
        kt = keys.T
        values = vt.T
        low_q = dot(aq[...], x, 1, 1)
        low_v = dot(av[...], x, 1, 1)
        low = jnp.concatenate([low_q, low_v], axis=0).astype(BF16)
        for row in range(rows):
            part = slice(row * tokens, (row + 1) * tokens)
            qt_s[row, :, span] = qt[:, part]
            k_s[row, span, :] = keys[part, :]
            vt_s[row, :, span] = vt[:, part]
            kt_s[row, :, span] = kt[:, part]
            v_s[row, span, :] = values[part, :]
            low_out[row, :, span] = low[:, part]
        keep(qt_s.at[:, :, span], qt_out.at[:, :, span])
        keep(k_s.at[:, span], k_out.at[:, span])
        keep(vt_s.at[:, :, span], vt_out.at[:, :, span])
        keep(kt_s.at[:, :, span], kt_out.at[:, :, span])
        keep(v_s.at[:, span], v_out.at[:, span])
    for copy in stores:
        copy.wait()
    x_copy.wait_send()
    og_copy.wait()


def layer_kernel(
    sizes, lives, place_ref, gain_one, shift_one, gain_two, shift_two,
    hidden, out_grad, x_in, og_in, qt_in, k_in, kt_in, v_in, vt_in, low_in, wo_in, wx_in, wr_in,
    lo_out, g_out, dqt_out, dk_out, dv_out, up_out,
    x_s, og_s, qt_s, k_s, kt_s, v_s, vt_s, low_s, wo_s, wx_s, wr_s,
    probs, score, ctx_s, inv_s, gctx_s, normed_s, back_s, acc_s, low16, slope_s, act_s, ds_s, do_s,
    rstd_s, kmask, qmask, lo_s, g_s, dqt_s, dk_s, dv_s,
    load, weight_load, store,
):
    rows, group, width = x_s.shape
    tokens = group // 2
    hidden_units = wx_s.shape[1]
    place = place_ref[0]
    slots = sizes.shape[1]
    pairs = HEADS // 2
    gain_one, shift_one, gain_two, shift_two = (
        part[...].reshape(1, width) for part in (gain_one, shift_one, gain_two, shift_two)
    )

    def row_loads(row):
        own = rows * place + row
        first = pl.ds(0, tokens)
        second = pl.ds(tokens, tokens)
        plan = [
            (qt_in.at[row], qt_s.at[row]),
            (k_in.at[row], k_s.at[row]),
            (vt_in.at[row], vt_s.at[row]),
            (hidden.at[own], x_s.at[row, first]),
            (x_in.at[row], x_s.at[row, second]),
            (out_grad.at[own], og_s.at[row, first]),
            (og_in.at[row], og_s.at[row, second]),
            (v_in.at[row], v_s.at[row]),
            (kt_in.at[row], kt_s.at[row]),
            (low_in.at[row], low_s.at[row]),
        ]
        return [
            pltpu.make_async_copy(source, target, load.at[row, index])
            for index, (source, target) in enumerate(plan)
        ]

    weight_loads = [
        pltpu.make_async_copy(source, target, weight_load.at[index])
        for index, (source, target) in enumerate([(wo_in, wo_s), (wx_in, wx_s), (wr_in, wr_s)])
    ]
    first_loads = row_loads(0)
    for copy in first_loads[:3]:
        copy.start()
    weight_loads[0].start()
    for copy in first_loads[3:5]:
        copy.start()
    weight_loads[1].start()
    weight_loads[2].start()
    for copy in first_loads[5:]:
        copy.start()
    for row in range(1, rows):
        for copy in row_loads(row):
            copy.start()

    def row_stores(row):
        plan = [
            (lo_s.at[row], lo_out.at[row]),
            (g_s.at[row], g_out.at[row]),
            (dqt_s.at[row], dqt_out.at[row]),
            (dk_s.at[row], dk_out.at[row]),
            (dv_s.at[row], dv_out.at[row]),
        ]
        return [
            pltpu.make_async_copy(source, target, store.at[row, index])
            for index, (source, target) in enumerate(plan)
        ]

    def paired(top, bottom_zero):
        zero = jnp.zeros_like(top)
        return jnp.concatenate([top, zero] if bottom_zero else [zero, top], axis=0)

    def attend_forward(row, spans):
        def scores(head):
            pair, odd = divmod(head, 2)
            lanes = slice(pair * 128, pair * 128 + 128)
            query = qt_s[row, head * HEAD:(head + 1) * HEAD, :]
            right = jnp.concatenate([paired(query, odd == 0), qmask[...]], axis=0)
            for a, b in spans:
                left = jnp.concatenate([k_s[row, a:b, lanes], kmask[a:b, :]], axis=1)
                score[head % 2, a:b, a:b] = dot(left, right[:, a:b], 1, 0)

        def weights(head):
            for a, b in spans:
                part = score[head % 2, a:b, a:b]
                top = jnp.max(part, axis=0, keepdims=True)
                probs[head, a:b, a:b] = jnp.exp2(part - top).astype(BF16)

        def contexts(head):
            values = vt_s[row, head * HEAD:(head + 1) * HEAD, :]
            left = jnp.concatenate([values, jnp.ones((16, group), BF16)], axis=0)
            for a, b in spans:
                total = dot(left[:, a:b], probs[head, a:b, a:b], 1, 0)
                inverse = 1.0 / total[HEAD:HEAD + 1]
                inv_s[head:head + 1, a:b] = inverse
                ctx_s[head * HEAD:(head + 1) * HEAD, a:b] = (total[:HEAD] * inverse).astype(BF16)

        for step in range(HEADS + 2):
            if step < HEADS:
                scores(step)
            if 0 <= step - 1 < HEADS:
                weights(step - 1)
            if 0 <= step - 2:
                contexts(step - 2)

    def attend_backward(row, spans):
        def score_grads(head):
            pair, odd = divmod(head, 2)
            lanes = slice(pair * 128, pair * 128 + 128)
            here = slice(head * HEAD, (head + 1) * HEAD)
            slot = head % 4
            grad = gctx_s[here, :] * inv_s[head:head + 1, :]
            short = grad.astype(BF16)
            do_s[slot] = short
            delta = -jnp.sum(grad * ctx_s[here, :].astype(F32), axis=0, keepdims=True)
            high = delta.astype(BF16).astype(F32)
            index = lax.broadcasted_iota(jnp.int32, (16, group), 0)
            extra = jnp.where(index == 0, high, jnp.where(index == 1, delta - high, 0.0))
            right = jnp.concatenate(
                [paired(short, odd == 0), extra.astype(BF16), jnp.zeros((112, group), BF16)], axis=0
            )
            for a, b in spans:
                left = jnp.concatenate(
                    [v_s[row, a:b, lanes], jnp.ones((b - a, 128), BF16)], axis=1
                )
                part = dot(left, right[:, a:b], 1, 0)
                ds_s[slot, a:b, a:b] = (probs[head, a:b, a:b].astype(F32) * part).astype(BF16)

        def grads(pair):
            lanes = slice(pair * 128, pair * 128 + 128)
            even, odd = 2 * pair, 2 * pair + 1
            for a, b in spans:
                for head in (even, odd):
                    here = slice(head * HEAD, (head + 1) * HEAD)
                    dqt_s[row, here, a:b] = (
                        dot(kt_s[row, here, a:b], ds_s[head % 4, a:b, a:b], 1, 0) * LN_2
                    ).astype(BF16)
                left = jnp.concatenate([ds_s[even % 4, a:b, a:b], ds_s[odd % 4, a:b, a:b]], axis=1)
                right = jnp.concatenate(
                    [
                        paired(qt_s[row, even * HEAD:even * HEAD + HEAD, a:b], True),
                        paired(qt_s[row, odd * HEAD:odd * HEAD + HEAD, a:b], False),
                    ],
                    axis=1,
                )
                dk_s[row, a:b, lanes] = (dot(left, right, 1, 1) * LN_2).astype(BF16)
                left = jnp.concatenate([probs[even, a:b, a:b], probs[odd, a:b, a:b]], axis=1)
                right = jnp.concatenate(
                    [paired(do_s[even % 4, :, a:b], True), paired(do_s[odd % 4, :, a:b], False)],
                    axis=1,
                )
                dv_s[row, a:b, lanes] = dot(left, right, 1, 1).astype(BF16)

        for step in range(pairs + 1):
            if step < pairs:
                score_grads(2 * step)
                score_grads(2 * step + 1)
            if step >= 1:
                grads(step - 1)

    def mean(value):
        return jnp.sum(value, axis=-1, keepdims=True) * (1.0 / width)

    def by_blocks(body, block=64):
        def step(index, carry):
            body(pl.ds(pl.multiple_of(index * block, block), block))
            return carry

        lax.fori_loop(0, group // block, step, 0)

    def one_row(row, carry):
        own = rows * place + row
        position = (lax.broadcasted_iota(jnp.int32, (group, 128), 0) + place * tokens) % group
        lane = lax.broadcasted_iota(jnp.int32, (1, 128), 1)
        low = jnp.full((1, 128), group, jnp.int32)
        high = low
        across = lax.broadcasted_iota(jnp.int32, (slots, group), 1)
        across = (across + place * tokens) % group
        line = lax.broadcasted_iota(jnp.int32, (slots, 1), 0)
        first = jnp.full((slots, 1), group, jnp.int32)
        last = first
        start = jnp.int32(0)
        crossing = jnp.int32(0)
        for slot in range(slots):
            size = sizes[own, slot]
            live = lives[own, slot]
            low = jnp.where(lane == slot, start, low)
            high = jnp.where(lane == slot, start + live, high)
            first = jnp.where(line == slot, start, first)
            last = jnp.where(line == slot, start + size, last)
            over = (start < tokens) & (start + size > tokens)
            crossing = jnp.where(over, 1, crossing)
            start = start + size
        dead = jnp.where((position >= low) & (position < high), 0.0, 1.0)
        kmask[...] = jnp.where(lane < slots, dead, 0.0).astype(BF16)
        within = jnp.where((across >= first) & (across < last), MASK_FILL, 0.0)
        qmask[...] = jnp.concatenate(
            [within, jnp.zeros((128 - slots, group), F32)], axis=0
        ).astype(BF16)

        loads = row_loads(row)
        for copy in loads[:3]:
            copy.wait()

        @pl.when(crossing == 1)
        def _():
            attend_forward(row, [(0, group)])

        @pl.when(crossing == 0)
        def _():
            attend_forward(row, [(0, tokens), (tokens, group)])

        @pl.when(row == 0)
        def _():
            weight_loads[0].wait()

        for copy in loads[3:5]:
            copy.wait()
        acc_s[...] = dot(ctx_s[...], wo_s[...], 0, 0)

        def norm_one(at):
            resid = x_s[row, at, :].astype(F32) + acc_s[at, :]
            center = resid - mean(resid)
            scaled = lax.rsqrt(mean(center * center) + NORM_EPS)
            normed = center * scaled
            normed_s[at, :] = normed
            rstd_s[at, :] = scaled
            low16[at, :] = (normed * gain_one + shift_one).astype(BF16)

        by_blocks(norm_one)

        @pl.when(row == 0)
        def _():
            weight_loads[1].wait()
            weight_loads[2].wait()

        chunks = hidden_units // CHUNK
        for step in range(chunks + 2):
            if step < chunks:
                at = slice(step * CHUNK, (step + 1) * CHUNK)
                score[step % 2] = dot(low16[...], wx_s[:, at], 1, 0)
            if 0 <= step - 1 < chunks:
                at = slice((step - 1) * CHUNK, step * CHUNK)
                inner = score[(step - 1) % 2]
                upto = 0.5 + 0.5 * lax.erf(inner * math.sqrt(0.5))
                bell = jnp.exp2(inner * inner * (-0.5 * LOG2_E)) * (1.0 / math.sqrt(2.0 * math.pi))
                act_s[(step - 1) % 2] = (inner * upto).astype(BF16)
                slope_s[:, at] = (upto + inner * bell).astype(BF16)
            if 0 <= step - 2:
                at = slice((step - 2) * CHUNK, (step - 1) * CHUNK)
                part = dot(act_s[(step - 2) % 2], wr_s[at, :], 1, 0)
                if step == 2:
                    acc_s[...] = part
                else:
                    acc_s[...] += part

        for copy in loads[5:7]:
            copy.wait()

        def norm_two(at):
            z = normed_s[at, :] * gain_one + shift_one + acc_s[at, :]
            center = z - mean(z)
            scaled = lax.rsqrt(mean(center * center) + NORM_EPS)
            normed = center * scaled
            lo_s[row, at, :] = (normed * gain_two + shift_two).astype(BF16)
            weighted = og_s[row, at, :].astype(F32) * gain_two
            grad = scaled * (weighted - mean(weighted) - normed * mean(weighted * normed))
            back_s[at, :] = grad
            low16[at, :] = grad.astype(BF16)

        by_blocks(norm_two)
        for step in range(chunks + 1):
            if step < chunks:
                at = slice(step * CHUNK, (step + 1) * CHUNK)
                part = dot(low16[...], wr_s[at, :], 1, 1)
                act_s[step % 2] = (part * slope_s[:, at].astype(F32)).astype(BF16)
            if step >= 1:
                at = slice((step - 1) * CHUNK, step * CHUNK)
                part = dot(act_s[(step - 1) % 2], wx_s[:, at], 1, 1)
                if step == 1:
                    acc_s[...] = part
                else:
                    acc_s[...] += part

        def norm_one_back(at):
            weighted = (back_s[at, :] + acc_s[at, :]) * gain_one
            normed = normed_s[at, :]
            grad = rstd_s[at, :] * (
                weighted - mean(weighted) - normed * mean(weighted * normed)
            )
            g_s[row, at, :] = grad.astype(BF16)

        by_blocks(norm_one_back)
        gctx_s[...] = dot(wo_s[...], g_s[row], 1, 1)
        for copy in loads[7:]:
            copy.wait()

        @pl.when(crossing == 1)
        def _():
            attend_backward(row, [(0, group)])

        @pl.when(crossing == 0)
        def _():
            attend_backward(row, [(0, tokens), (tokens, group)])

        for copy in row_stores(row):
            copy.start()
        from_q = dot(low_s[row], dqt_s[row], 1, 1) * (
            ADAPTER_STRENGTH / slots_rank / math.sqrt(HEAD) / LN_2
        )
        from_v = dot(low_s[row], dv_s[row], 1, 0) * (ADAPTER_STRENGTH / slots_rank)
        rank_line = lax.broadcasted_iota(jnp.int32, (2 * slots_rank, 1), 0)
        part = jnp.where(rank_line < slots_rank, from_q, from_v)
        up_out[...] = jnp.where(row == 0, part, up_out[...] + part)
        return carry

    slots_rank = low_s.shape[1] // 2
    lax.fori_loop(0, rows, one_row, 0)
    for row in range(rows):
        for copy in row_stores(row):
            copy.wait()


def partners():
    found = [("seq", 1)]
    bit = 1
    while bit < lax.axis_size("dp"):
        found.append(("dp", bit))
        bit *= 2
    return found


def finish_kernel(
    up, lo, grad, dqt, dk, dv, wq, wk, wv,
    lo_out, ig_out, upq_out, upv_out,
    total, got, grad_s, dqt_s, dk_s, dv_s, wq_s, wk_s, wv_s, res_s,
    load, store, send, recv, ar_send, ar_recv,
):
    rows, group, width = grad.shape
    tokens = group // 2
    place = lax.axis_index("seq")
    other = 1 - place
    plan = [
        (wq, wq_s), (wk, wk_s), (wv, wv_s),
        (dqt, dqt_s), (dk, dk_s), (dv, dv_s), (grad, grad_s),
    ]
    loads = [
        pltpu.make_async_copy(source, target, load.at[index])
        for index, (source, target) in enumerate(plan)
    ]
    for copy in loads:
        copy.start()
    barrier = pltpu.get_barrier_semaphore()
    rounds = []
    for axis, bit in partners():
        me = lax.axis_index(axis)
        rounds.append({axis: me + bit - 2 * bit * ((me // bit) % 2)})
    for partner in rounds:
        pl.semaphore_signal(barrier, inc=1, device_id=partner, device_id_type=MESH)
    pl.semaphore_wait(barrier, len(rounds))
    mine = pl.ds(rows * place, rows)
    lo_copy = pltpu.make_async_remote_copy(
        src_ref=lo.at[:, pl.ds(tokens, tokens)], dst_ref=lo_out.at[mine],
        send_sem=send.at[0], recv_sem=recv.at[0],
        device_id={"seq": other}, device_id_type=MESH,
    )
    reduces = [
        pltpu.make_async_remote_copy(
            src_ref=total.at[index], dst_ref=got.at[index],
            send_sem=ar_send.at[index], recv_sem=ar_recv.at[index],
            device_id=partner, device_id_type=MESH,
        )
        for index, partner in enumerate(rounds)
    ]
    total[0] = up[...]
    reduces[0].start()
    lo_copy.start()
    keep_lo = pltpu.make_async_copy(lo.at[:, pl.ds(0, tokens)], lo_out.at[mine], store.at[0])
    keep_lo.start()
    done = [0]

    def advance():
        index = done[0]
        if index == len(rounds):
            return
        reduces[index].wait_recv()
        total[index + 1] = total[index] + got[index]
        done[0] = index + 1
        if index + 1 < len(rounds):
            reduces[index + 1].start()

    for copy in loads:
        copy.wait()

    def piece(half, block):
        span = slice(half * tokens, (half + 1) * tokens)
        outs = slice(block * 256, block * 256 + 256)
        left_q = jnp.concatenate([dqt_s[row, :, span] for row in range(rows)], axis=1)
        left_k = dk_s[:, span, :].reshape(rows * tokens, width)
        left_v = dv_s[:, span, :].reshape(rows * tokens, width)
        value = dot(left_q, wq_s[outs, :], 0, 1)
        value += dot(left_k, wk_s[outs, :], 1, 1)
        value += dot(left_v, wv_s[outs, :], 1, 1)
        value += grad_s[:, span, outs].reshape(rows * tokens, 256).astype(F32)
        res_s[half, :, :, outs] = value.astype(BF16).reshape(rows, tokens, 256)

    blocks = width // 256
    for block in range(blocks):
        piece(1, block)
        advance()
    ig_copy = pltpu.make_async_remote_copy(
        src_ref=res_s.at[1], dst_ref=ig_out.at[mine],
        send_sem=send.at[1], recv_sem=recv.at[1],
        device_id={"seq": other}, device_id_type=MESH,
    )
    ig_copy.start()
    for block in range(blocks):
        piece(0, block)
        advance()
    keep_ig = pltpu.make_async_copy(res_s.at[0], ig_out.at[mine], store.at[1])
    keep_ig.start()
    for _ in range(len(rounds)):
        advance()
    last = total[len(rounds)]
    rank = up.shape[0] // 2
    upq_out[...] = last[:rank]
    upv_out[...] = last[rank:]
    for copy in reduces:
        copy.wait_send()
    keep_lo.wait()
    keep_ig.wait()
    lo_copy.wait()
    ig_copy.wait()


def shards(
    hidden_in, slot_sizes, live_lengths, w_query, w_key, w_value, query_down_factor, down_value,
    query_up_factor, value_up_factor, w_output, attn_gain, attn_shift, w_expand, w_reduce,
    ffn_gain, ffn_shift, out_grad,
):
    micro, tokens, width = hidden_in.shape
    rows = micro // 2
    group = 2 * tokens
    hidden_units = w_expand.shape[1]
    rank = query_down_factor.shape[1]
    shape = jax.ShapeDtypeStruct
    dma = pltpu.SemaphoreType.DMA
    wide = (rows, width, group)
    tall = (rows, group, width)
    mega = 2 ** 20
    qt, keys, kt, values, vt, low, x_got, og_got, wq_eff, wv_eff = pl.pallas_call(
        project_kernel,
        out_shape=[
            shape(wide, BF16), shape(tall, BF16), shape(wide, BF16), shape(tall, BF16),
            shape(wide, BF16), shape((rows, 2 * rank, group), BF16),
            shape((rows, tokens, width), BF16), shape((rows, tokens, width), BF16),
            shape((width, width), BF16), shape((width, width), BF16),
        ],
        in_specs=[HBM_SPEC] * 5 + [VMEM_SPEC] * 4,
        out_specs=[HBM_SPEC] * 5 + [VMEM_SPEC] + [HBM_SPEC] * 4,
        scratch_shapes=[
            VMEM((rows, tokens, width), BF16), VMEM((rows, tokens, width), BF16),
            VMEM((width, width), BF16), VMEM((width, width), BF16), VMEM((width, width), BF16),
            VMEM(wide, BF16), VMEM(tall, BF16), VMEM(wide, BF16), VMEM(tall, BF16),
            VMEM(wide, BF16),
            dma((4,)), dma((13,)), dma((2,)), dma((2,)), dma((1,)),
        ],
        compiler_params=pltpu.CompilerParams(
            collective_id=0, has_side_effects=True, vmem_limit_bytes=62 * mega
        ),
        name="project",
    )(
        hidden_in, out_grad, w_query, w_key, w_value, query_down_factor.T, down_value.T,
        query_up_factor, value_up_factor,
    )
    place = lax.axis_index("seq").astype(jnp.int32).reshape(1)
    lo, grad, dqt, dk, dv, up = pl.pallas_call(
        layer_kernel,
        out_shape=[
            shape(tall, BF16), shape(tall, BF16), shape(wide, BF16), shape(tall, BF16),
            shape(tall, BF16), shape((2 * rank, width), F32),
        ],
        in_specs=[SMEM_SPEC] * 3 + [VMEM_SPEC] * 4 + [HBM_SPEC] * 13,
        out_specs=[HBM_SPEC] * 5 + [VMEM_SPEC],
        scratch_shapes=[
            VMEM(tall, BF16), VMEM(tall, BF16), VMEM(wide, BF16), VMEM(tall, BF16),
            VMEM(wide, BF16), VMEM(tall, BF16), VMEM(wide, BF16),
            VMEM((rows, 2 * rank, group), BF16),
            VMEM((width, width), BF16), VMEM((width, hidden_units), BF16),
            VMEM((hidden_units, width), BF16),
            VMEM((HEADS, group, group), BF16), VMEM((2, group, group), F32),
            VMEM((width, group), BF16), VMEM((16, group), F32), VMEM((width, group), F32),
            VMEM((group, width), F32), VMEM((group, width), F32), VMEM((group, width), F32),
            VMEM((group, width), BF16), VMEM((group, hidden_units), BF16),
            VMEM((2, group, CHUNK), BF16), VMEM((4, group, group), BF16),
            VMEM((4, HEAD, group), BF16), VMEM((group, 1), F32),
            VMEM((group, 128), BF16), VMEM((128, group), BF16),
            VMEM(tall, BF16), VMEM(tall, BF16), VMEM(wide, BF16), VMEM(tall, BF16),
            VMEM(tall, BF16),
            dma((rows, 10)), dma((3,)), dma((rows, 5)),
        ],
        compiler_params=pltpu.CompilerParams(vmem_limit_bytes=62 * mega),
        name="layer",
    )(
        slot_sizes[0], live_lengths[0], place, attn_gain, attn_shift, ffn_gain, ffn_shift, hidden_in, out_grad, x_got, og_got,
        qt, keys, kt, values, vt, low, w_output, w_expand, w_reduce,
    )
    count = len(partners())
    layer_out, input_grad, up_query_grad, up_value_grad = pl.pallas_call(
        finish_kernel,
        out_shape=[
            shape((micro, tokens, width), BF16), shape((micro, tokens, width), BF16),
            shape((rank, width), F32), shape((rank, width), F32),
        ],
        in_specs=[VMEM_SPEC] + [HBM_SPEC] * 8,
        out_specs=[HBM_SPEC] * 2 + [VMEM_SPEC] * 2,
        scratch_shapes=[
            VMEM((count + 1, 2 * rank, width), F32), VMEM((count, 2 * rank, width), F32),
            VMEM(tall, BF16), VMEM(wide, BF16), VMEM(tall, BF16), VMEM(tall, BF16),
            VMEM((width, width), BF16), VMEM((width, width), BF16), VMEM((width, width), BF16),
            VMEM((2, rows, tokens, width), BF16),
            dma((7,)), dma((2,)), dma((2,)), dma((2,)), dma((count,)), dma((count,)),
        ],
        compiler_params=pltpu.CompilerParams(
            collective_id=1, has_side_effects=True, vmem_limit_bytes=62 * mega
        ),
        name="finish",
    )(up, lo, grad, dqt, dk, dv, wq_eff, w_key, wv_eff)
    return layer_out, input_grad.astype(F32), up_query_grad, up_value_grad


def solution(mesh):
    tokens = P(None, ("dp", "seq"), None)
    table = P("dp", None, None)
    in_specs = (tokens, table, table) + (P(),) * 14 + (tokens,)
    out_specs = (tokens, tokens, P(), P())
    return jax.shard_map(shards, mesh=mesh, in_specs=in_specs, out_specs=out_specs, check_vma=False)
```

```python
import functools
import math

import jax
import jax.numpy as jnp
from jax import lax
from jax.experimental import pallas as pl
from jax.experimental.pallas import tpu as pltpu
from jax.sharding import PartitionSpec as P

HEADS = 12
HEAD = 64
NORM_EPS = 1e-05
ADAPTER_STRENGTH = 16.0
MASK_FILL = -1e30
LOG2_E = math.log2(math.e)
LN_2 = math.log(2.0)
CHUNK = 512
BF16 = jnp.bfloat16
F32 = jnp.float32
MESH = pl.DeviceIdType.MESH
VMEM = pltpu.VMEM
HBM_SPEC = pl.BlockSpec(memory_space=pl.ANY)
VMEM_SPEC = pl.BlockSpec(memory_space=pltpu.VMEM)
SMEM_SPEC = pl.BlockSpec(memory_space=pltpu.SMEM)


def dot(left, right, over_left, over_right):
    return lax.dot_general(
        left, right, (((over_left,), (over_right,)), ((), ())), preferred_element_type=F32
    )


def exchange_kernel(
    hidden, out_grad, wq, wk, wv, aq, av, bq, bv,
    x_out, og_out, qt_out, k_out, vt_out, low_out, wq_out, wv_out,
    x_s, wq_s, wk_s, wv_s, qt_s, k_s, vt_s, load, store, send, recv,
):
    rows, tokens, width = x_s.shape
    place = lax.axis_index("seq")
    other = 1 - place
    loads = [
        pltpu.make_async_copy(source, target, load.at[index])
        for index, (source, target) in enumerate([
            (wq, wq_s), (hidden.at[pl.ds(rows * place, rows)], x_s), (wk, wk_s), (wv, wv_s),
        ])
    ]
    for copy in loads:
        copy.start()
    barrier = pltpu.get_barrier_semaphore()
    pl.semaphore_signal(barrier, inc=1, device_id={"seq": other}, device_id_type=MESH)
    pl.semaphore_wait(barrier, 1)
    remote = [
        pltpu.make_async_remote_copy(
            src_ref=source.at[pl.ds(rows * other, rows)], dst_ref=target,
            send_sem=send.at[index], recv_sem=recv.at[index],
            device_id={"seq": other}, device_id_type=MESH,
        )
        for index, (source, target) in enumerate([(hidden, x_out), (out_grad, og_out)])
    ]
    for copy in remote:
        copy.start()
    strength = ADAPTER_STRENGTH / aq.shape[0]
    stores = []

    def keep(source, target):
        copy = pltpu.make_async_copy(source, target, store.at[len(stores)])
        copy.start()
        stores.append(copy)

    loads[0].wait()
    wq_s[...] = (
        (wq_s[...].astype(F32) + strength * dot(aq[...], bq[...], 0, 0))
        * (LOG2_E / math.sqrt(HEAD))
    ).astype(BF16)
    keep(wq_s, wq_out)
    loads[1].wait()
    x = x_s[...].reshape(rows * tokens, width)
    qt = dot(wq_s[...], x, 0, 1).astype(BF16)
    for row in range(rows):
        qt_s[row] = qt[:, row * tokens:(row + 1) * tokens]
    keep(qt_s, qt_out)
    loads[3].wait()
    wv_s[...] = (
        wv_s[...].astype(F32) + strength * dot(av[...], bv[...], 0, 0)
    ).astype(BF16)
    keep(wv_s, wv_out)
    loads[2].wait()
    k_s[...] = dot(x, wk_s[...], 1, 0).astype(BF16).reshape(rows, tokens, width)
    keep(k_s, k_out)
    vt = dot(wv_s[...], x, 0, 1).astype(BF16)
    for row in range(rows):
        vt_s[row] = vt[:, row * tokens:(row + 1) * tokens]
    keep(vt_s, vt_out)
    low = jnp.concatenate([dot(aq[...], x, 1, 1), dot(av[...], x, 1, 1)], axis=0).astype(BF16)
    for row in range(rows):
        low_out[row] = low[:, row * tokens:(row + 1) * tokens]
    for copy in stores:
        copy.wait()
    for copy in remote:
        copy.wait()


def layer_kernel(
    sizes, lives, place_ref, gain_one, shift_one, gain_two, shift_two, low_in, aq, av,
    hidden, out_grad, x_in, og_in, qt_in, k_in, vt_in, wq_in, wk_in, wv_in, wo_in, wx_in, wr_in,
    lo_out, g_out, dqt_out, dk_out, dv_out, up_out,
    x_s, og_s, qt_s, k_s, vt_s, kt_s, v_s, low_s, wq_s, wk_s, wv_s, wo_s, wx_s, wr_s,
    probs, score, ctx_s, inv_s, gctx_s, normed_s, back_s, acc_s, low16, slope_s, act_s, ds_s, do_s,
    rstd_s, kmask, qmask, lo_s, g_s, dqt_s, dk_s, dv_s,
    load, store,
):
    rows, group, width = x_s.shape
    tokens = group // 2
    hidden_units = wx_s.shape[1]
    place = place_ref[0]
    slots = sizes.shape[1]
    pairs = HEADS // 2
    gain_one, shift_one, gain_two, shift_two = (
        part[...].reshape(1, width) for part in (gain_one, shift_one, gain_two, shift_two)
    )
    first = pl.ds(0, tokens)
    second = pl.ds(tokens, tokens)
    mine = pl.ds(rows * place, rows)
    loads = [
        pltpu.make_async_copy(source, target, load.at[index])
        for index, (source, target) in enumerate([
            (x_in, x_s.at[:, second]),
            (wk_in, wk_s),
            (wq_in, wq_s),
            (wv_in, wv_s),
            (qt_in, qt_s.at[:, :, first]),
            (k_in, k_s.at[:, first]),
            (vt_in, vt_s.at[:, :, first]),
            (wo_in, wo_s),
            (hidden.at[mine], x_s.at[:, first]),
            (wx_in, wx_s),
            (wr_in, wr_s),
            (out_grad.at[mine], og_s.at[:, first]),
            (og_in, og_s.at[:, second]),
        ])
    ]
    for copy in loads:
        copy.start()

    def row_stores(row):
        plan = [
            (lo_s.at[row], lo_out.at[row]),
            (g_s.at[row], g_out.at[row]),
            (dqt_s.at[row], dqt_out.at[row]),
            (dk_s.at[row], dk_out.at[row]),
            (dv_s.at[row], dv_out.at[row]),
        ]
        return [
            pltpu.make_async_copy(source, target, store.at[row, index])
            for index, (source, target) in enumerate(plan)
        ]

    loads[0].wait()
    loads[1].wait()
    x = x_s[:, tokens:, :].reshape(rows * tokens, width)
    k_s[:, tokens:, :] = dot(x, wk_s[...], 1, 0).astype(BF16).reshape(rows, tokens, width)
    low = jnp.concatenate([dot(aq[...], x, 1, 1), dot(av[...], x, 1, 1)], axis=0).astype(BF16)
    for row in range(rows):
        low_s[row, :, :tokens] = low_in[row]
        low_s[row, :, tokens:] = low[:, row * tokens:(row + 1) * tokens]
    for weight, target, copy in ((wq_s, qt_s, loads[2]), (wv_s, vt_s, loads[3])):
        copy.wait()
        part = dot(weight[...], x, 0, 1).astype(BF16)
        for row in range(rows):
            target[row, :, tokens:] = part[:, row * tokens:(row + 1) * tokens]
    for copy in loads[4:7]:
        copy.wait()

    def paired(top, bottom_zero):
        zero = jnp.zeros_like(top)
        return jnp.concatenate([top, zero] if bottom_zero else [zero, top], axis=0)

    def attend_forward(row, spans):
        def scores(head):
            pair, odd = divmod(head, 2)
            lanes = slice(pair * 128, pair * 128 + 128)
            query = qt_s[row, head * HEAD:(head + 1) * HEAD, :]
            right = jnp.concatenate([paired(query, odd == 0), qmask[...]], axis=0)
            for a, b in spans:
                left = jnp.concatenate([k_s[row, a:b, lanes], kmask[a:b, :]], axis=1)
                score[head % 2, a:b, a:b] = dot(left, right[:, a:b], 1, 0)

        def weights(head):
            for a, b in spans:
                part = score[head % 2, a:b, a:b]
                top = jnp.max(part, axis=0, keepdims=True)
                probs[head, a:b, a:b] = jnp.exp2(part - top).astype(BF16)

        def contexts(head):
            values = vt_s[row, head * HEAD:(head + 1) * HEAD, :]
            left = jnp.concatenate([values, jnp.ones((16, group), BF16)], axis=0)
            for a, b in spans:
                total = dot(left[:, a:b], probs[head, a:b, a:b], 1, 0)
                inverse = 1.0 / total[HEAD:HEAD + 1]
                inv_s[head:head + 1, a:b] = inverse
                ctx_s[head * HEAD:(head + 1) * HEAD, a:b] = (total[:HEAD] * inverse).astype(BF16)

        for step in range(HEADS + 2):
            if step < HEADS:
                scores(step)
            if 0 <= step - 1 < HEADS:
                weights(step - 1)
            if 0 <= step - 2:
                contexts(step - 2)

    def attend_backward(row, spans):
        def score_grads(head):
            pair, odd = divmod(head, 2)
            lanes = slice(pair * 128, pair * 128 + 128)
            here = slice(head * HEAD, (head + 1) * HEAD)
            slot = head % 4
            grad = gctx_s[here, :] * inv_s[head:head + 1, :]
            short = grad.astype(BF16)
            do_s[slot] = short
            delta = -jnp.sum(grad * ctx_s[here, :].astype(F32), axis=0, keepdims=True)
            high = delta.astype(BF16).astype(F32)
            index = lax.broadcasted_iota(jnp.int32, (16, group), 0)
            extra = jnp.where(index == 0, high, jnp.where(index == 1, delta - high, 0.0))
            right = jnp.concatenate(
                [paired(short, odd == 0), extra.astype(BF16), jnp.zeros((112, group), BF16)], axis=0
            )
            for a, b in spans:
                left = jnp.concatenate(
                    [v_s[a:b, lanes], jnp.ones((b - a, 128), BF16)], axis=1
                )
                part = dot(left, right[:, a:b], 1, 0)
                ds_s[slot, a:b, a:b] = (probs[head, a:b, a:b].astype(F32) * part).astype(BF16)

        def grads(pair):
            lanes = slice(pair * 128, pair * 128 + 128)
            even, odd = 2 * pair, 2 * pair + 1
            for a, b in spans:
                for head in (even, odd):
                    here = slice(head * HEAD, (head + 1) * HEAD)
                    dqt_s[row, here, a:b] = (
                        dot(kt_s[here, a:b], ds_s[head % 4, a:b, a:b], 1, 0) * LN_2
                    ).astype(BF16)
                left = jnp.concatenate([ds_s[even % 4, a:b, a:b], ds_s[odd % 4, a:b, a:b]], axis=1)
                right = jnp.concatenate(
                    [
                        paired(qt_s[row, even * HEAD:even * HEAD + HEAD, a:b], True),
                        paired(qt_s[row, odd * HEAD:odd * HEAD + HEAD, a:b], False),
                    ],
                    axis=1,
                )
                dk_s[row, a:b, lanes] = (dot(left, right, 1, 1) * LN_2).astype(BF16)
                left = jnp.concatenate([probs[even, a:b, a:b], probs[odd, a:b, a:b]], axis=1)
                right = jnp.concatenate(
                    [paired(do_s[even % 4, :, a:b], True), paired(do_s[odd % 4, :, a:b], False)],
                    axis=1,
                )
                dv_s[row, a:b, lanes] = dot(left, right, 1, 1).astype(BF16)

        for step in range(pairs + 1):
            if step < pairs:
                score_grads(2 * step)
                score_grads(2 * step + 1)
            if step >= 1:
                grads(step - 1)

    def mean(value):
        return jnp.sum(value, axis=-1, keepdims=True) * (1.0 / width)

    def weave(main, side):
        for index, step in enumerate(main):
            step()
            for part in side[index * len(side) // len(main):(index + 1) * len(side) // len(main)]:
                part()

    chunks = hidden_units // CHUNK
    piece = 32

    def feed_forward(row):
        def blocks(half, body):
            start = half * tokens
            return [
                functools.partial(body, slice(at, at + piece))
                for at in range(start, start + tokens, piece)
            ]

        def span(half):
            return slice(half * tokens, (half + 1) * tokens)

        def attended(half):
            def step(at):
                acc_s[span(half), at] = dot(ctx_s[:, span(half)], wo_s[:, at], 0, 0)

            return [
                functools.partial(step, slice(at, at + 256)) for at in range(0, width, 256)
            ]

        def norm_one(at):
            resid = x_s[row, at, :].astype(F32) + acc_s[at, :]
            center = resid - mean(resid)
            scaled = lax.rsqrt(mean(center * center) + NORM_EPS)
            normed = center * scaled
            normed_s[at, :] = normed
            rstd_s[at, :] = scaled
            low16[at, :] = (normed * gain_one + shift_one).astype(BF16)

        def forward(half):
            here = span(half)

            def run(step):
                if step < chunks:
                    at = slice(step * CHUNK, (step + 1) * CHUNK)
                    score[step % 2, here, :] = dot(low16[here, :], wx_s[:, at], 1, 0)
                if 0 <= step - 1 < chunks:
                    at = slice((step - 1) * CHUNK, step * CHUNK)
                    inner = score[(step - 1) % 2, here, :]
                    upto = 0.5 + 0.5 * lax.erf(inner * math.sqrt(0.5))
                    bell = jnp.exp2(inner * inner * (-0.5 * LOG2_E)) * (
                        1.0 / math.sqrt(2.0 * math.pi)
                    )
                    act_s[(step - 1) % 2, here, :] = (inner * upto).astype(BF16)
                    slope_s[here, at] = (upto + inner * bell).astype(BF16)
                if 0 <= step - 2:
                    at = slice((step - 2) * CHUNK, (step - 1) * CHUNK)
                    part = dot(act_s[(step - 2) % 2, here, :], wr_s[at, :], 1, 0)
                    if step == 2:
                        acc_s[here, :] = part
                    else:
                        acc_s[here, :] += part

            return [functools.partial(run, step) for step in range(chunks + 2)]

        def norm_two(at):
            z = normed_s[at, :] * gain_one + shift_one + acc_s[at, :]
            center = z - mean(z)
            scaled = lax.rsqrt(mean(center * center) + NORM_EPS)
            normed = center * scaled
            lo_s[row, at, :] = (normed * gain_two + shift_two).astype(BF16)
            weighted = og_s[row, at, :].astype(F32) * gain_two
            grad = scaled * (weighted - mean(weighted) - normed * mean(weighted * normed))
            back_s[at, :] = grad
            low16[at, :] = grad.astype(BF16)

        def backward(half):
            here = span(half)

            def run(step):
                if step < chunks:
                    at = slice(step * CHUNK, (step + 1) * CHUNK)
                    part = dot(low16[here, :], wr_s[at, :], 1, 1)
                    act_s[step % 2, here, :] = (part * slope_s[here, at].astype(F32)).astype(BF16)
                if step >= 1:
                    at = slice((step - 1) * CHUNK, step * CHUNK)
                    part = dot(act_s[(step - 1) % 2, here, :], wx_s[:, at], 1, 1)
                    if step == 1:
                        acc_s[here, :] = part
                    else:
                        acc_s[here, :] += part

            return [functools.partial(run, step) for step in range(chunks + 1)]

        def norm_one_back(at):
            weighted = (back_s[at, :] + acc_s[at, :]) * gain_one
            normed = normed_s[at, :]
            grad = rstd_s[at, :] * (
                weighted - mean(weighted) - normed * mean(weighted * normed)
            )
            g_s[row, at, :] = grad.astype(BF16)

        def context_grad(half):
            def step(at):
                gctx_s[at, span(half)] = dot(wo_s[at, :], g_s[row, span(half), :], 1, 1)

            return [
                functools.partial(step, slice(at, at + 256)) for at in range(0, width, 256)
            ]

        def turn(half):
            def step(at):
                kt_s[at, span(half)] = k_s[row, span(half), at].T
                v_s[span(half), at] = vt_s[row, at, span(half)].T

            return [
                functools.partial(step, slice(at, at + 128)) for at in range(0, width, 128)
            ]

        weave(attended(0), [])
        weave(attended(1), blocks(0, norm_one))

        @pl.when(row == 0)
        def _():
            loads[9].wait()
            loads[10].wait()

        weave(forward(0), blocks(1, norm_one))

        @pl.when(row == 0)
        def _():
            loads[11].wait()
            loads[12].wait()

        weave(forward(1), blocks(0, norm_two))
        weave(backward(0), blocks(1, norm_two))
        weave(backward(1), blocks(0, norm_one_back) + turn(0) + turn(1))
        weave(context_grad(0), blocks(1, norm_one_back))
        weave(context_grad(1), [])

    def one_row(row, carry):
        own = rows * place + row
        position = (lax.broadcasted_iota(jnp.int32, (group, 128), 0) + place * tokens) % group
        lane = lax.broadcasted_iota(jnp.int32, (1, 128), 1)
        low = jnp.full((1, 128), group, jnp.int32)
        high = low
        across = lax.broadcasted_iota(jnp.int32, (slots, group), 1)
        across = (across + place * tokens) % group
        line = lax.broadcasted_iota(jnp.int32, (slots, 1), 0)
        first = jnp.full((slots, 1), group, jnp.int32)
        last = first
        start = jnp.int32(0)
        crossing = jnp.int32(0)
        for slot in range(slots):
            size = sizes[own, slot]
            live = lives[own, slot]
            low = jnp.where(lane == slot, start, low)
            high = jnp.where(lane == slot, start + live, high)
            first = jnp.where(line == slot, start, first)
            last = jnp.where(line == slot, start + size, last)
            over = (start < tokens) & (start + size > tokens)
            crossing = jnp.where(over, 1, crossing)
            start = start + size
        dead = jnp.where((position >= low) & (position < high), 0.0, 1.0)
        kmask[...] = jnp.where(lane < slots, dead, 0.0).astype(BF16)
        within = jnp.where((across >= first) & (across < last), MASK_FILL, 0.0)
        qmask[...] = jnp.concatenate(
            [within, jnp.zeros((128 - slots, group), F32)], axis=0
        ).astype(BF16)

        @pl.when(crossing == 1)
        def _():
            attend_forward(row, [(0, group)])

        @pl.when(crossing == 0)
        def _():
            attend_forward(row, [(0, tokens), (tokens, group)])

        @pl.when(row == 0)
        def _():
            loads[7].wait()
            loads[8].wait()

        feed_forward(row)

        @pl.when(crossing == 1)
        def _():
            attend_backward(row, [(0, group)])

        @pl.when(crossing == 0)
        def _():
            attend_backward(row, [(0, tokens), (tokens, group)])

        for copy in row_stores(row):
            copy.start()
        from_q = dot(low_s[row], dqt_s[row], 1, 1) * (
            ADAPTER_STRENGTH / slots_rank / math.sqrt(HEAD) / LN_2
        )
        from_v = dot(low_s[row], dv_s[row], 1, 0) * (ADAPTER_STRENGTH / slots_rank)
        rank_line = lax.broadcasted_iota(jnp.int32, (2 * slots_rank, 1), 0)
        part = jnp.where(rank_line < slots_rank, from_q, from_v)
        up_out[...] = jnp.where(row == 0, part, up_out[...] + part)
        return carry

    slots_rank = low_s.shape[1] // 2
    lax.fori_loop(0, rows, one_row, 0)
    for row in range(rows):
        for copy in row_stores(row):
            copy.wait()


def phases():
    found = [("seq", 1, 2)]
    stride, left = 1, lax.axis_size("dp")
    while left > 1:
        size = 4 if left % 4 == 0 else left if left < 4 else 2
        found.append(("dp", stride, size))
        stride, left = stride * size, left // size
    return found


def finish_kernel(
    up, lo, grad, dqt, dk, dv, wq, wk, wv,
    lo_out, ig_out, up_out,
    pair, got, lo_s, grad_s, dqt_s, dk_s, dv_s, wq_s, wk_s, wv_s, acc_s, res_s,
    load, store, send, recv, ar_send, ar_recv,
):
    rows, group, width = grad_s.shape
    tokens = group // 2
    place = lax.axis_index("seq")
    other = 1 - place
    plan = [
        (dqt, dqt_s), (wq, wq_s), (dk, dk_s), (wk, wk_s), (dv, dv_s), (wv, wv_s), (grad, grad_s),
        (lo, lo_s),
    ]
    loads = [
        pltpu.make_async_copy(source, target, load.at[index])
        for index, (source, target) in enumerate(plan)
    ]
    for copy in loads:
        copy.start()
    barrier = pltpu.get_barrier_semaphore()
    rounds = []
    greeted = 0
    for axis, stride, size in phases():
        me = lax.axis_index(axis)
        digit = (me // stride) % size
        others = []
        for step in range(1, size):
            theirs = (digit + step) % size
            others.append((theirs, {axis: me + (theirs - digit) * stride}))
        for _, device in others:
            pl.semaphore_signal(barrier, inc=1, device_id=device, device_id_type=MESH)
        greeted += len(others)
        rounds.append((size, digit, others))
    pl.semaphore_wait(barrier, greeted)
    mine = pl.ds(rows * place, rows)

    def copies(index):
        size, digit, others = rounds[index]
        buffer = pair if index == 0 else got.at[index - 1]
        sends = [
            pltpu.make_async_remote_copy(
                src_ref=buffer.at[digit], dst_ref=buffer.at[digit],
                send_sem=ar_send.at[index, step], recv_sem=ar_recv.at[index, digit],
                device_id=device, device_id_type=MESH,
            )
            for step, (_, device) in enumerate(others)
        ]
        arrivals = [
            pltpu.make_async_remote_copy(
                src_ref=buffer.at[theirs], dst_ref=buffer.at[theirs],
                send_sem=ar_send.at[index, step], recv_sem=ar_recv.at[index, theirs],
                device_id=device, device_id_type=MESH,
            )
            for step, (theirs, device) in enumerate(others)
        ]
        return sends, arrivals

    all_copies = [copies(index) for index in range(len(rounds))]

    def begin(index, value):
        digit = rounds[index][1]
        if index == 0:
            pair[digit] = value
        else:
            got[index - 1, digit] = value.astype(BF16)
        for copy in all_copies[index][0]:
            copy.start()

    def end(index):
        size = rounds[index][0]
        for copy in all_copies[index][1]:
            copy.wait_recv()
        buffer = pair if index == 0 else got.at[index - 1]
        value = buffer[0].astype(F32)
        for step in range(1, size):
            value = value + buffer[step].astype(F32)
        return value

    begin(0, up[...])
    done = [0]

    def advance():
        if done[0] < len(rounds):
            value = end(done[0])
            done[0] += 1
            if done[0] < len(rounds):
                begin(done[0], value)
            else:
                up_out[...] = value

    def from_q(half):
        span = slice(half * tokens, (half + 1) * tokens)
        left = jnp.concatenate([dqt_s[row, :, span] for row in range(rows)], axis=1)
        acc_s[...] = dot(left, wq_s[...], 0, 1)

    def from_k(half):
        left = dk_s[:, half * tokens:(half + 1) * tokens, :].reshape(rows * tokens, width)
        acc_s[...] += dot(left, wk_s[...], 1, 1)

    def from_v(half):
        span = slice(half * tokens, (half + 1) * tokens)
        left = dv_s[:, span, :].reshape(rows * tokens, width)
        value = acc_s[...] + dot(left, wv_s[...], 1, 1)
        value += grad_s[:, span, :].reshape(rows * tokens, width).astype(F32)
        res_s[half] = value.astype(BF16).reshape(rows, tokens, width)

    def sibling(source, target, index):
        return pltpu.make_async_remote_copy(
            src_ref=source, dst_ref=target, send_sem=send.at[index], recv_sem=recv.at[index],
            device_id={"seq": other}, device_id_type=MESH,
        )

    loads[0].wait()
    loads[1].wait()
    from_q(1)
    advance()
    loads[2].wait()
    loads[3].wait()
    from_k(1)
    for copy in loads[4:7]:
        copy.wait()
    from_v(1)
    ig_copy = sibling(res_s.at[1], ig_out.at[mine], 0)
    ig_copy.start()
    loads[7].wait()
    lo_copy = sibling(lo_s.at[:, pl.ds(tokens, tokens)], lo_out.at[mine], 1)
    lo_copy.start()
    keep_lo = pltpu.make_async_copy(lo_s.at[:, pl.ds(0, tokens)], lo_out.at[mine], store.at[0])
    keep_lo.start()
    from_q(0)
    advance()
    from_k(0)
    from_v(0)
    keep_ig = pltpu.make_async_copy(res_s.at[0], ig_out.at[mine], store.at[1])
    keep_ig.start()
    for _ in range(len(rounds)):
        advance()
    for sends, _ in all_copies:
        for copy in sends:
            copy.wait_send()
    keep_lo.wait()
    keep_ig.wait()
    lo_copy.wait()
    ig_copy.wait()


def widen_kernel(lo, ig, up, lo_out, ig_out, upq_out, upv_out, lo_s, ig_s, wide_s, load, store):
    micro = lo.shape[0]
    loads = [
        pltpu.make_async_copy(ig.at[index], ig_s.at[index], load.at[index])
        for index in range(micro)
    ]
    loads.append(pltpu.make_async_copy(lo, lo_s, load.at[micro]))
    for copy in loads:
        copy.start()
    stores = []
    for index in range(micro):
        loads[index].wait()
        wide_s[index] = ig_s[index].astype(F32)
        stores.append(pltpu.make_async_copy(wide_s.at[index], ig_out.at[index], store.at[index]))
        stores[-1].start()
    loads[micro].wait()
    stores.append(pltpu.make_async_copy(lo_s, lo_out, store.at[micro]))
    stores[-1].start()
    rank = upq_out.shape[0]
    upq_out[...] = up[:rank]
    upv_out[...] = up[rank:]
    for copy in stores:
        copy.wait()


def shards(
    hidden_in, slot_sizes, live_lengths, w_query, w_key, w_value, query_down_factor, down_value,
    query_up_factor, value_up_factor, w_output, attn_gain, attn_shift, w_expand, w_reduce,
    ffn_gain, ffn_shift, out_grad,
):
    micro, tokens, width = hidden_in.shape
    rows = micro // 2
    group = 2 * tokens
    hidden_units = w_expand.shape[1]
    rank = query_down_factor.shape[1]
    shape = jax.ShapeDtypeStruct
    dma = pltpu.SemaphoreType.DMA
    wide = (rows, width, group)
    tall = (rows, group, width)
    half_tall = (rows, tokens, width)
    half_wide = (rows, width, tokens)
    square = (width, width)
    limit = 62 * 2 ** 20
    down_q, down_v = query_down_factor.T, down_value.T
    x_got, og_got, qt, keys, vt, low, wq_eff, wv_eff = pl.pallas_call(
        exchange_kernel,
        out_shape=[
            shape(half_tall, BF16), shape(half_tall, BF16), shape(half_wide, BF16),
            shape(half_tall, BF16), shape(half_wide, BF16), shape((rows, 2 * rank, tokens), BF16),
            shape(square, BF16), shape(square, BF16),
        ],
        in_specs=[HBM_SPEC] * 5 + [VMEM_SPEC] * 4,
        out_specs=[HBM_SPEC] * 5 + [VMEM_SPEC] + [HBM_SPEC] * 2,
        scratch_shapes=[
            VMEM(half_tall, BF16), VMEM(square, BF16), VMEM(square, BF16), VMEM(square, BF16),
            VMEM(half_wide, BF16), VMEM(half_tall, BF16), VMEM(half_wide, BF16),
            dma((4,)), dma((5,)), dma((2,)), dma((2,)),
        ],
        compiler_params=pltpu.CompilerParams(
            collective_id=0, has_side_effects=True, vmem_limit_bytes=limit
        ),
        name="project",
    )(
        hidden_in, out_grad, w_query, w_key, w_value, down_q, down_v,
        query_up_factor, value_up_factor,
    )
    place = lax.axis_index("seq").astype(jnp.int32).reshape(1)
    lo, grad, dqt, dk, dv, up = pl.pallas_call(
        layer_kernel,
        out_shape=[
            shape(tall, BF16), shape(tall, BF16), shape(wide, BF16), shape(tall, BF16),
            shape(tall, BF16), shape((2 * rank, width), F32),
        ],
        in_specs=[SMEM_SPEC] * 3 + [VMEM_SPEC] * 7 + [HBM_SPEC] * 13,
        out_specs=[HBM_SPEC] * 5 + [VMEM_SPEC],
        scratch_shapes=[
            VMEM(tall, BF16), VMEM(tall, BF16), VMEM(wide, BF16), VMEM(tall, BF16),
            VMEM(wide, BF16), VMEM((width, group), BF16), VMEM((group, width), BF16),
            VMEM((rows, 2 * rank, group), BF16),
            VMEM(square, BF16), VMEM(square, BF16), VMEM(square, BF16),
            VMEM(square, BF16), VMEM((width, hidden_units), BF16),
            VMEM((hidden_units, width), BF16),
            VMEM((HEADS, group, group), BF16), VMEM((2, group, group), F32),
            VMEM((width, group), BF16), VMEM((16, group), F32), VMEM((width, group), F32),
            VMEM((group, width), F32), VMEM((group, width), F32), VMEM((group, width), F32),
            VMEM((group, width), BF16), VMEM((group, hidden_units), BF16),
            VMEM((2, group, CHUNK), BF16), VMEM((4, group, group), BF16),
            VMEM((4, HEAD, group), BF16), VMEM((group, 1), F32),
            VMEM((group, 128), BF16), VMEM((128, group), BF16),
            VMEM(tall, BF16), VMEM(tall, BF16), VMEM(wide, BF16), VMEM(tall, BF16),
            VMEM(tall, BF16),
            dma((13,)), dma((rows, 5)),
        ],
        compiler_params=pltpu.CompilerParams(vmem_limit_bytes=limit),
        name="layer",
    )(
        slot_sizes[0], live_lengths[0], place, attn_gain, attn_shift, ffn_gain, ffn_shift,
        low, down_q, down_v, hidden_in, out_grad, x_got, og_got,
        qt, keys, vt, wq_eff, w_key, wv_eff, w_output, w_expand, w_reduce,
    )
    count = len(phases())
    lo, ig, up = pl.pallas_call(
        finish_kernel,
        out_shape=[
            shape((micro, tokens, width), BF16), shape((micro, tokens, width), BF16),
            shape((2 * rank, width), F32),
        ],
        in_specs=[VMEM_SPEC] + [HBM_SPEC] * 8,
        out_specs=[HBM_SPEC] * 2 + [VMEM_SPEC],
        scratch_shapes=[
            VMEM((2, 2 * rank, width), F32), VMEM((count - 1, 4, 2 * rank, width), BF16),
            VMEM(tall, BF16),
            VMEM(tall, BF16), VMEM(wide, BF16), VMEM(tall, BF16), VMEM(tall, BF16),
            VMEM(square, BF16), VMEM(square, BF16), VMEM(square, BF16),
            VMEM((rows * tokens, width), F32), VMEM((2, rows, tokens, width), BF16),
            dma((8,)), dma((2,)), dma((2,)), dma((2,)), dma((count, 3)), dma((count, 4)),
        ],
        compiler_params=pltpu.CompilerParams(
            collective_id=1, has_side_effects=True, vmem_limit_bytes=limit
        ),
        name="finish",
    )(up, lo, grad, dqt, dk, dv, wq_eff, w_key, wv_eff)
    return pl.pallas_call(
        widen_kernel,
        out_shape=[
            shape(lo.shape, BF16), shape(ig.shape, F32),
            shape((rank, width), F32), shape((rank, width), F32),
        ],
        in_specs=[HBM_SPEC] * 2 + [VMEM_SPEC],
        out_specs=[HBM_SPEC] * 2 + [VMEM_SPEC] * 2,
        scratch_shapes=[
            VMEM(lo.shape, BF16), VMEM(ig.shape, BF16), VMEM(ig.shape, F32),
            dma((micro + 1,)), dma((micro + 1,)),
        ],
        compiler_params=pltpu.CompilerParams(vmem_limit_bytes=limit),
        name="widen",
    )(lo, ig, up)


def solution(mesh):
    tokens = P(None, ("dp", "seq"), None)
    table = P("dp", None, None)
    in_specs = (tokens, table, table) + (P(),) * 14 + (tokens,)
    out_specs = (tokens, tokens, P(), P())
    return jax.shard_map(shards, mesh=mesh, in_specs=in_specs, out_specs=out_specs, check_vma=False)
```

```python
import functools
import math

import jax
import jax.numpy as jnp
from jax import lax
from jax.experimental import pallas as pl
from jax.experimental.pallas import tpu as pltpu
from jax.sharding import PartitionSpec as P

HEADS = 12
HEAD = 64
NORM_EPS = 1e-05
ADAPTER_STRENGTH = 16.0
MASK_FILL = -1e30
LOG2_E = math.log2(math.e)
LN_2 = math.log(2.0)
CHUNK = 512
BF16 = jnp.bfloat16
F32 = jnp.float32
MESH = pl.DeviceIdType.MESH
VMEM = pltpu.VMEM
HBM_SPEC = pl.BlockSpec(memory_space=pl.ANY)
VMEM_SPEC = pl.BlockSpec(memory_space=pltpu.VMEM)
SMEM_SPEC = pl.BlockSpec(memory_space=pltpu.SMEM)


def dot(left, right, over_left, over_right):
    return lax.dot_general(
        left, right, (((over_left,), (over_right,)), ((), ())), preferred_element_type=F32
    )


def exchange_kernel(
    hidden, out_grad, wq, wk, wv, aq_in, av_in, bq_in, bv_in,
    x_out, og_out, qt_out, k_out, vt_out, low_out, wq_out, wv_out,
    x_s, wq_s, wk_s, wv_s, aq, av, bq, bv, qt_s, k_s, vt_s, low_s, load, store, send, recv,
):
    rows, tokens, width = x_s.shape
    place = lax.axis_index("seq")
    other = 1 - place
    loads = [
        pltpu.make_async_copy(source, target, load.at[index])
        for index, (source, target) in enumerate([
            (wk, wk_s), (hidden.at[pl.ds(rows * place, rows)], x_s), (aq_in, aq), (bq_in, bq),
            (wq, wq_s), (av_in, av), (bv_in, bv), (wv, wv_s),
        ])
    ]
    for copy in loads:
        copy.start()
    barrier = pltpu.get_barrier_semaphore()
    pl.semaphore_signal(barrier, inc=1, device_id={"seq": other}, device_id_type=MESH)
    pl.semaphore_wait(barrier, 1)
    remote = [
        pltpu.make_async_remote_copy(
            src_ref=source.at[pl.ds(rows * other, rows)], dst_ref=target,
            send_sem=send.at[index], recv_sem=recv.at[index],
            device_id={"seq": other}, device_id_type=MESH,
        )
        for index, (source, target) in enumerate([(hidden, x_out), (out_grad, og_out)])
    ]
    for copy in remote:
        copy.start()
    strength = ADAPTER_STRENGTH / aq.shape[0]
    stores = []

    def keep(source, target):
        copy = pltpu.make_async_copy(source, target, store.at[len(stores)])
        copy.start()
        stores.append(copy)

    loads[0].wait()
    loads[1].wait()
    x = x_s[...].reshape(rows * tokens, width)
    k_s[...] = dot(x, wk_s[...], 1, 0).astype(BF16).reshape(rows, tokens, width)
    keep(k_s, k_out)
    for copy in loads[2:5]:
        copy.wait()
    wq_s[...] = (
        (wq_s[...].astype(F32) + strength * dot(aq[...], bq[...], 0, 0))
        * (LOG2_E / math.sqrt(HEAD))
    ).astype(BF16)
    keep(wq_s, wq_out)
    for copy in loads[5:8]:
        copy.wait()
    wv_s[...] = (
        wv_s[...].astype(F32) + strength * dot(av[...], bv[...], 0, 0)
    ).astype(BF16)
    keep(wv_s, wv_out)
    low = jnp.concatenate([dot(aq[...], x, 1, 1), dot(av[...], x, 1, 1)], axis=0).astype(BF16)
    for row in range(rows):
        low_s[row] = low[:, row * tokens:(row + 1) * tokens]
    keep(low_s, low_out)
    for weight, target, out in ((wq_s, qt_s, qt_out), (wv_s, vt_s, vt_out)):
        part = dot(weight[...], x, 0, 1).astype(BF16)
        for row in range(rows):
            target[row] = part[:, row * tokens:(row + 1) * tokens]
        keep(target, out)
    for copy in stores:
        copy.wait()
    for copy in remote:
        copy.wait()


def layer_kernel(
    sizes, lives, place_ref, *refs
):
    (
        gain_one, shift_one, gain_two, shift_two, low_in, aq_in, av_in,
        hidden, out_grad, x_in, og_in, qt_in, k_in, vt_in, wq_in, wk_in, wv_in,
        wo_in, wx_in, wr_in,
        lo_out, g_out, dqt_out, dk_out, dv_out, up_out,
        vec_s, aq, av, x_s, og_s, qt_s, k_s, vt_s, kt_s, v_s, low_s, wq_s, wk_s, wv_s,
        wo_s, wx_s, wr_s, probs, score, ctx_s, inv_s, gctx_s, normed_s, back_s, acc_s, low16,
        slope_s, act_s, ds_s, do_s, rstd_s, kmask, qmask, lo_s, g_s, dqt_s, dk_s, dv_s, up_s,
        load, store,
    ) = refs
    rows, group, width = x_s.shape
    tokens = group // 2
    hidden_units = wx_s.shape[1]
    place = place_ref[0]
    slots = sizes.shape[1]
    pairs = HEADS // 2
    first = pl.ds(0, tokens)
    second = pl.ds(tokens, tokens)
    mine = pl.ds(rows * place, rows)
    plan = [
        (x_in, x_s.at[:, second]),
        (wk_in, wk_s),
        (wq_in, wq_s),
        (wv_in, wv_s),
        (qt_in, qt_s.at[:, :, first]),
        (k_in, k_s.at[:, first]),
        (vt_in, vt_s.at[:, :, first]),
        (wo_in, wo_s),
        (hidden.at[mine], x_s.at[:, first]),
        (wx_in, wx_s),
        (wr_in, wr_s),
        (out_grad.at[mine], og_s.at[:, first]),
        (og_in, og_s.at[:, second]),
        (aq_in, aq),
        (av_in, av),
        (low_in, low_s.at[:, :, first]),
    ] + [
        (vector, vec_s.at[index])
        for index, vector in enumerate((gain_one, shift_one, gain_two, shift_two))
    ]
    loads = [
        pltpu.make_async_copy(source, target, load.at[index])
        for index, (source, target) in enumerate(plan)
    ]
    small = loads[13:]
    for copy in loads[:2] + small + loads[2:13]:
        copy.start()

    def row_stores(row):
        plan = [
            (lo_s.at[row], lo_out.at[row]),
            (g_s.at[row], g_out.at[row]),
            (dqt_s.at[row], dqt_out.at[row]),
            (dk_s.at[row], dk_out.at[row]),
            (dv_s.at[row], dv_out.at[row]),
        ]
        return [
            pltpu.make_async_copy(source, target, store.at[row, index])
            for index, (source, target) in enumerate(plan)
        ]

    def make_masks(row):
        own = rows * place + row
        position = (lax.broadcasted_iota(jnp.int32, (group, 128), 0) + place * tokens) % group
        lane = lax.broadcasted_iota(jnp.int32, (1, 128), 1)
        low_end = jnp.full((1, 128), group, jnp.int32)
        high_end = low_end
        across = lax.broadcasted_iota(jnp.int32, (slots, group), 1)
        across = (across + place * tokens) % group
        line = lax.broadcasted_iota(jnp.int32, (slots, 1), 0)
        begin = jnp.full((slots, 1), group, jnp.int32)
        last = begin
        start = jnp.int32(0)
        crossing = jnp.int32(0)
        for slot in range(slots):
            size = sizes[own, slot]
            live = lives[own, slot]
            low_end = jnp.where(lane == slot, start, low_end)
            high_end = jnp.where(lane == slot, start + live, high_end)
            begin = jnp.where(line == slot, start, begin)
            last = jnp.where(line == slot, start + size, last)
            over = (start < tokens) & (start + size > tokens)
            crossing = jnp.where(over, 1, crossing)
            start = start + size
        dead = jnp.where((position >= low_end) & (position < high_end), 0.0, 1.0)
        kmask[row] = jnp.where(lane < slots, dead, 0.0).astype(BF16)
        within = jnp.where((across >= begin) & (across < last), MASK_FILL, 0.0)
        qmask[row] = jnp.concatenate(
            [within, jnp.zeros((128 - slots, group), F32)], axis=0
        ).astype(BF16)
        return crossing

    crossings = [make_masks(row) for row in range(rows)]
    loads[0].wait()
    loads[1].wait()
    x = x_s[:, tokens:, :].reshape(rows * tokens, width)
    k_s[:, tokens:, :] = dot(x, wk_s[...], 1, 0).astype(BF16).reshape(rows, tokens, width)
    for copy in small:
        copy.wait()
    low = jnp.concatenate([dot(aq[...], x, 1, 1), dot(av[...], x, 1, 1)], axis=0).astype(BF16)
    for row in range(rows):
        low_s[row, :, tokens:] = low[:, row * tokens:(row + 1) * tokens]
    for weight, target, copy in ((wq_s, qt_s, loads[2]), (wv_s, vt_s, loads[3])):
        copy.wait()
        part = dot(weight[...], x, 0, 1).astype(BF16)
        for row in range(rows):
            target[row, :, tokens:] = part[:, row * tokens:(row + 1) * tokens]
    for copy in loads[4:7]:
        copy.wait()

    gain_one, shift_one, gain_two, shift_two = (
        vec_s[index].reshape(1, width) for index in range(4)
    )

    def paired(top, bottom_zero):
        zero = jnp.zeros_like(top)
        return jnp.concatenate([top, zero] if bottom_zero else [zero, top], axis=0)

    def attend_forward(row, spans):
        def scores(head):
            pair, odd = divmod(head, 2)
            lanes = slice(pair * 128, pair * 128 + 128)
            query = qt_s[row, head * HEAD:(head + 1) * HEAD, :]
            right = jnp.concatenate([paired(query, odd == 0), qmask[row]], axis=0)
            for a, b in spans:
                left = jnp.concatenate([k_s[row, a:b, lanes], kmask[row, a:b, :]], axis=1)
                score[head % 2, a:b, a:b] = dot(left, right[:, a:b], 1, 0)

        def weights(head):
            for a, b in spans:
                part = score[head % 2, a:b, a:b]
                top = jnp.max(part, axis=0, keepdims=True)
                probs[head, a:b, a:b] = jnp.exp2(part - top).astype(BF16)

        def contexts(head):
            values = vt_s[row, head * HEAD:(head + 1) * HEAD, :]
            left = jnp.concatenate([values, jnp.ones((16, group), BF16)], axis=0)
            for a, b in spans:
                total = dot(left[:, a:b], probs[head, a:b, a:b], 1, 0)
                inverse = 1.0 / total[HEAD:HEAD + 1]
                inv_s[head:head + 1, a:b] = inverse
                ctx_s[head * HEAD:(head + 1) * HEAD, a:b] = (total[:HEAD] * inverse).astype(BF16)

        for step in range(HEADS + 2):
            if step < HEADS:
                scores(step)
            if 0 <= step - 1 < HEADS:
                weights(step - 1)
            if 0 <= step - 2:
                contexts(step - 2)

    def attend_backward(row, spans):
        def score_grads(head):
            pair, odd = divmod(head, 2)
            lanes = slice(pair * 128, pair * 128 + 128)
            here = slice(head * HEAD, (head + 1) * HEAD)
            slot = head % 4
            grad = gctx_s[here, :] * inv_s[head:head + 1, :]
            short = grad.astype(BF16)
            do_s[slot] = short
            delta = -jnp.sum(grad * ctx_s[here, :].astype(F32), axis=0, keepdims=True)
            high = delta.astype(BF16).astype(F32)
            index = lax.broadcasted_iota(jnp.int32, (16, group), 0)
            extra = jnp.where(index == 0, high, jnp.where(index == 1, delta - high, 0.0))
            right = jnp.concatenate(
                [paired(short, odd == 0), extra.astype(BF16), jnp.zeros((112, group), BF16)], axis=0
            )
            for a, b in spans:
                left = jnp.concatenate(
                    [v_s[a:b, lanes], jnp.ones((b - a, 128), BF16)], axis=1
                )
                part = dot(left, right[:, a:b], 1, 0)
                ds_s[slot, a:b, a:b] = (probs[head, a:b, a:b].astype(F32) * part).astype(BF16)

        def grads(pair):
            even, odd = 2 * pair, 2 * pair + 1
            for a, b in spans:
                for head in (even, odd):
                    here = slice(head * HEAD, (head + 1) * HEAD)
                    dqt_s[row, here, a:b] = (
                        dot(kt_s[here, a:b], ds_s[head % 4, a:b, a:b], 1, 0) * LN_2
                    ).astype(BF16)
                lanes = slice(pair * 128, pair * 128 + 128)
                left = jnp.concatenate([ds_s[even % 4, a:b, a:b], ds_s[odd % 4, a:b, a:b]], axis=1)
                right = jnp.concatenate(
                    [
                        paired(qt_s[row, even * HEAD:even * HEAD + HEAD, a:b], True),
                        paired(qt_s[row, odd * HEAD:odd * HEAD + HEAD, a:b], False),
                    ],
                    axis=1,
                )
                dk_s[row, a:b, lanes] = (dot(left, right, 1, 1) * LN_2).astype(BF16)
                left = jnp.concatenate([probs[even, a:b, a:b], probs[odd, a:b, a:b]], axis=1)
                right = jnp.concatenate(
                    [paired(do_s[even % 4, :, a:b], True), paired(do_s[odd % 4, :, a:b], False)],
                    axis=1,
                )
                dv_s[row, a:b, lanes] = dot(left, right, 1, 1).astype(BF16)

        for step in range(pairs + 1):
            if step < pairs:
                score_grads(2 * step)
                score_grads(2 * step + 1)
            if step >= 1:
                grads(step - 1)

    def mean(value):
        return jnp.sum(value, axis=-1, keepdims=True) * (1.0 / width)

    def weave(main, side):
        for index, step in enumerate(main):
            step()
            for part in side[index * len(side) // len(main):(index + 1) * len(side) // len(main)]:
                part()

    chunks = hidden_units // CHUNK
    piece = 32

    def feed_forward(row):
        def blocks(half, body):
            start = half * tokens
            return [
                functools.partial(body, slice(at, at + piece))
                for at in range(start, start + tokens, piece)
            ]

        def span(half):
            return slice(half * tokens, (half + 1) * tokens)

        def attended(half):
            def step(at):
                acc_s[span(half), at] = dot(ctx_s[:, span(half)], wo_s[:, at], 0, 0)

            return [
                functools.partial(step, slice(at, at + 256)) for at in range(0, width, 256)
            ]

        def norm_one(at):
            resid = x_s[row, at, :].astype(F32) + acc_s[at, :]
            center = resid - mean(resid)
            scaled = lax.rsqrt(mean(center * center) + NORM_EPS)
            normed = center * scaled
            normed_s[at, :] = normed
            rstd_s[at, :] = scaled
            low16[at, :] = (normed * gain_one + shift_one).astype(BF16)

        def forward(half):
            here = span(half)

            def run(step):
                if step < chunks:
                    at = slice(step * CHUNK, (step + 1) * CHUNK)
                    score[step % 2, here, :] = dot(low16[here, :], wx_s[:, at], 1, 0)
                if 0 <= step - 1 < chunks:
                    at = slice((step - 1) * CHUNK, step * CHUNK)
                    inner = score[(step - 1) % 2, here, :]
                    upto = 0.5 + 0.5 * lax.erf(inner * math.sqrt(0.5))
                    bell = jnp.exp2(inner * inner * (-0.5 * LOG2_E)) * (
                        1.0 / math.sqrt(2.0 * math.pi)
                    )
                    act_s[(step - 1) % 2, here, :] = (inner * upto).astype(BF16)
                    slope_s[here, at] = (upto + inner * bell).astype(BF16)
                if 0 <= step - 2:
                    at = slice((step - 2) * CHUNK, (step - 1) * CHUNK)
                    part = dot(act_s[(step - 2) % 2, here, :], wr_s[at, :], 1, 0)
                    if step == 2:
                        acc_s[here, :] = part
                    else:
                        acc_s[here, :] += part

            return [functools.partial(run, step) for step in range(chunks + 2)]

        def norm_two(at):
            z = normed_s[at, :] * gain_one + shift_one + acc_s[at, :]
            center = z - mean(z)
            scaled = lax.rsqrt(mean(center * center) + NORM_EPS)
            normed = center * scaled
            lo_s[row, at, :] = (normed * gain_two + shift_two).astype(BF16)
            weighted = og_s[row, at, :].astype(F32) * gain_two
            grad = scaled * (weighted - mean(weighted) - normed * mean(weighted * normed))
            back_s[at, :] = grad
            low16[at, :] = grad.astype(BF16)

        def backward(half):
            here = span(half)

            def run(step):
                if step < chunks:
                    at = slice(step * CHUNK, (step + 1) * CHUNK)
                    part = dot(low16[here, :], wr_s[at, :], 1, 1)
                    act_s[step % 2, here, :] = (part * slope_s[here, at].astype(F32)).astype(BF16)
                if step >= 1:
                    at = slice((step - 1) * CHUNK, step * CHUNK)
                    part = dot(act_s[(step - 1) % 2, here, :], wx_s[:, at], 1, 1)
                    if step == 1:
                        acc_s[here, :] = part
                    else:
                        acc_s[here, :] += part

            return [functools.partial(run, step) for step in range(chunks + 1)]

        def norm_one_back(at):
            weighted = (back_s[at, :] + acc_s[at, :]) * gain_one
            normed = normed_s[at, :]
            grad = rstd_s[at, :] * (
                weighted - mean(weighted) - normed * mean(weighted * normed)
            )
            g_s[row, at, :] = grad.astype(BF16)

        def context_grad(half):
            def step(at):
                gctx_s[at, span(half)] = dot(wo_s[at, :], g_s[row, span(half), :], 1, 1)

            return [
                functools.partial(step, slice(at, at + 256)) for at in range(0, width, 256)
            ]

        def turn(half):
            def step(at):
                kt_s[at, span(half)] = k_s[row, span(half), at].T
                v_s[span(half), at] = vt_s[row, at, span(half)].T

            return [
                functools.partial(step, slice(at, at + 128)) for at in range(0, width, 128)
            ]

        weave(attended(0), [])
        weave(attended(1), blocks(0, norm_one))

        @pl.when(row == 0)
        def _():
            loads[9].wait()
            loads[10].wait()

        weave(forward(0), blocks(1, norm_one))

        @pl.when(row == 0)
        def _():
            loads[11].wait()
            loads[12].wait()

        weave(forward(1), blocks(0, norm_two))
        weave(backward(0), blocks(1, norm_two))
        weave(backward(1), blocks(0, norm_one_back) + turn(0) + turn(1))
        weave(context_grad(0), blocks(1, norm_one_back))
        weave(context_grad(1), [])

    def one_row(row, carry):
        crossing = jnp.where(row == 0, crossings[0], crossings[1])

        @pl.when(crossing == 1)
        def _():
            attend_forward(row, [(0, group)])

        @pl.when(crossing == 0)
        def _():
            attend_forward(row, [(0, tokens), (tokens, group)])

        @pl.when(row == 0)
        def _():
            loads[7].wait()
            loads[8].wait()

        feed_forward(row)
        for copy in row_stores(row)[:2]:
            copy.start()

        @pl.when(crossing == 1)
        def _():
            attend_backward(row, [(0, group)])

        @pl.when(crossing == 0)
        def _():
            attend_backward(row, [(0, tokens), (tokens, group)])

        for copy in row_stores(row)[2:]:
            copy.start()
        from_q = dot(low_s[row], dqt_s[row], 1, 1) * (
            ADAPTER_STRENGTH / slots_rank / math.sqrt(HEAD) / LN_2
        )
        from_v = dot(low_s[row], dv_s[row], 1, 0) * (ADAPTER_STRENGTH / slots_rank)
        rank_line = lax.broadcasted_iota(jnp.int32, (2 * slots_rank, 1), 0)
        part = jnp.where(rank_line < slots_rank, from_q, from_v)
        up_s[...] = jnp.where(row == 0, part, up_s[...] + part)
        return carry

    slots_rank = low_s.shape[1] // 2
    lax.fori_loop(0, rows, one_row, 0)
    keep_up = pltpu.make_async_copy(up_s, up_out, load.at[0])
    keep_up.start()
    for row in range(rows):
        for copy in row_stores(row):
            copy.wait()
    keep_up.wait()


def phases():
    found = [("seq", 1, 2)]
    stride, left = 1, lax.axis_size("dp")
    while left > 1:
        size = 4 if left % 4 == 0 else left if left < 4 else 2
        found.append(("dp", stride, size))
        stride, left = stride * size, left // size
    return found


def finish_kernel(
    up, lo, grad, dqt, dk, dv, wq, wk, wv,
    lo_out, ig_out, up_out,
    up_s, pair, got, grad_s, dqt_s, dk_s, dv_s, wq_s, wk_s, wv_s, acc_s, res_s,
    load, store, send, recv, ar_send, ar_recv,
):
    rows, group, width = grad_s.shape
    tokens = group // 2
    place = lax.axis_index("seq")
    other = 1 - place
    plan = [
        (dqt, dqt_s), (wq, wq_s), (dk, dk_s), (wk, wk_s), (dv, dv_s), (wv, wv_s),
        (grad, grad_s), (up, up_s),
    ]
    loads = [
        pltpu.make_async_copy(source, target, load.at[index])
        for index, (source, target) in enumerate(plan)
    ]
    for copy in loads[7:] + loads[:7]:
        copy.start()
    barrier = pltpu.get_barrier_semaphore()
    rounds = []
    greeted = 0
    for axis, stride, size in phases():
        me = lax.axis_index(axis)
        digit = (me // stride) % size
        others = []
        for step in range(1, size):
            theirs = (digit + step) % size
            others.append((theirs, {axis: me + (theirs - digit) * stride}))
        for _, device in others:
            pl.semaphore_signal(barrier, inc=1, device_id=device, device_id_type=MESH)
        greeted += len(others)
        rounds.append((size, digit, others))
    pl.semaphore_wait(barrier, greeted)
    mine = pl.ds(rows * place, rows)

    def copies(index):
        size, digit, others = rounds[index]
        buffer = pair if index == 0 else got.at[index - 1]
        sends = [
            pltpu.make_async_remote_copy(
                src_ref=buffer.at[digit], dst_ref=buffer.at[digit],
                send_sem=ar_send.at[index, step], recv_sem=ar_recv.at[index, digit],
                device_id=device, device_id_type=MESH,
            )
            for step, (_, device) in enumerate(others)
        ]
        arrivals = [
            pltpu.make_async_remote_copy(
                src_ref=buffer.at[theirs], dst_ref=buffer.at[theirs],
                send_sem=ar_send.at[index, step], recv_sem=ar_recv.at[index, theirs],
                device_id=device, device_id_type=MESH,
            )
            for step, (theirs, device) in enumerate(others)
        ]
        return sends, arrivals

    def sibling(source, target, index):
        return pltpu.make_async_remote_copy(
            src_ref=source, dst_ref=target, send_sem=send.at[index], recv_sem=recv.at[index],
            device_id={"seq": other}, device_id_type=MESH,
        )

    keep_up = pltpu.make_async_copy(up_s, up_out, store.at[0])
    all_copies = [copies(index) for index in range(len(rounds))]

    def begin(index, value):
        digit = rounds[index][1]
        if index == 0:
            pair[digit] = value
        else:
            got[index - 1, digit] = value.astype(BF16)
        for copy in all_copies[index][0]:
            copy.start()

    def end(index):
        size = rounds[index][0]
        for copy in all_copies[index][1]:
            copy.wait_recv()
        buffer = pair if index == 0 else got.at[index - 1]
        value = buffer[0].astype(F32)
        for step in range(1, size):
            value = value + buffer[step].astype(F32)
        return value

    loads[7].wait()
    begin(0, up_s[...])
    lo_copy = sibling(lo.at[:, pl.ds(tokens, tokens)], lo_out, 1)
    lo_copy.start()
    done = [0]

    def advance():
        if done[0] < len(rounds):
            value = end(done[0])
            done[0] += 1
            if done[0] < len(rounds):
                begin(done[0], value)
            else:
                up_s[...] = value
                keep_up.start()

    def from_q(half):
        span = slice(half * tokens, (half + 1) * tokens)
        left = jnp.concatenate([dqt_s[row, :, span] for row in range(rows)], axis=1)
        acc_s[...] = dot(left, wq_s[...], 0, 1)

    def part(source, weight, half):
        left = source[:, half * tokens:(half + 1) * tokens, :].reshape(rows * tokens, width)
        return dot(left, weight[...], 1, 1)

    def from_k(half):
        acc_s[...] += part(dk_s, wk_s, half)

    def from_v(half):
        span = slice(half * tokens, (half + 1) * tokens)
        value = acc_s[...] + part(dv_s, wv_s, half)
        value += grad_s[:, span, :].reshape(rows * tokens, width).astype(F32)
        res_s[half] = value.astype(BF16).reshape(rows, tokens, width)

    loads[0].wait()
    loads[1].wait()
    from_q(1)
    advance()
    loads[2].wait()
    loads[3].wait()
    from_k(1)
    for copy in loads[4:7]:
        copy.wait()
    from_v(1)
    ig_copy = sibling(res_s.at[1], ig_out.at[mine], 0)
    ig_copy.start()
    from_q(0)
    advance()
    from_k(0)
    from_v(0)
    keep_ig = pltpu.make_async_copy(res_s.at[0], ig_out.at[mine], store.at[1])
    keep_ig.start()
    for _ in range(len(rounds)):
        advance()
    for sends, _ in all_copies:
        for copy in sends:
            copy.wait_send()
    keep_up.wait()
    keep_ig.wait()
    lo_copy.wait()
    ig_copy.wait()


def widen_kernel(
    place_ref, lo, lo_got, ig, up, lo_out, ig_out, upq_out, upv_out,
    lo_s, ig_s, wide_s, up_s, load, store,
):
    micro, tokens, width = ig_s.shape
    rows = micro // 2
    place = place_ref[0]
    own = pl.ds(rows * place, rows)
    rest = pl.ds(rows * (1 - place), rows)
    rank = upq_out.shape[0]
    loads = [
        pltpu.make_async_copy(ig.at[index], ig_s.at[index], load.at[index])
        for index in range(micro)
    ] + [
        pltpu.make_async_copy(up, up_s, load.at[micro]),
        pltpu.make_async_copy(lo.at[:, pl.ds(0, tokens)], lo_s.at[0], load.at[micro + 1]),
        pltpu.make_async_copy(lo_got, lo_s.at[1], load.at[micro + 2]),
    ]
    for copy in loads:
        copy.start()
    widened = [
        pltpu.make_async_copy(wide_s.at[index], ig_out.at[index], store.at[index])
        for index in range(micro)
    ]
    for index in range(micro):
        loads[index].wait()
        wide_s[index] = ig_s[index].astype(F32)
        widened[index].start()
    stores = [
        pltpu.make_async_copy(up_s.at[pl.ds(0, rank)], upq_out, store.at[micro]),
        pltpu.make_async_copy(up_s.at[pl.ds(rank, rank)], upv_out, store.at[micro + 1]),
        pltpu.make_async_copy(lo_s.at[0], lo_out.at[own], store.at[micro + 2]),
        pltpu.make_async_copy(lo_s.at[1], lo_out.at[rest], store.at[micro + 3]),
    ]
    for copy in loads[micro:]:
        copy.wait()
    for copy in stores:
        copy.start()
    for copy in widened + stores:
        copy.wait()


def shards(
    hidden_in, slot_sizes, live_lengths, w_query, w_key, w_value, query_down_factor, down_value,
    query_up_factor, value_up_factor, w_output, attn_gain, attn_shift, w_expand, w_reduce,
    ffn_gain, ffn_shift, out_grad,
):
    micro, tokens, width = hidden_in.shape
    rows = micro // 2
    group = 2 * tokens
    hidden_units = w_expand.shape[1]
    rank = query_down_factor.shape[1]
    shape = jax.ShapeDtypeStruct
    dma = pltpu.SemaphoreType.DMA
    wide = (rows, width, group)
    tall = (rows, group, width)
    half_tall = (rows, tokens, width)
    half_wide = (rows, width, tokens)
    square = (width, width)
    limit = 62 * 2 ** 20
    down_q, down_v = query_down_factor.T, down_value.T
    x_got, og_got, qt, keys, vt, low, wq_eff, wv_eff = pl.pallas_call(
        exchange_kernel,
        out_shape=[
            shape(half_tall, BF16), shape(half_tall, BF16), shape(half_wide, BF16),
            shape(half_tall, BF16), shape(half_wide, BF16), shape((rows, 2 * rank, tokens), BF16),
            shape(square, BF16), shape(square, BF16),
        ],
        in_specs=[HBM_SPEC] * 9,
        out_specs=[HBM_SPEC] * 8,
        scratch_shapes=[
            VMEM(half_tall, BF16), VMEM(square, BF16), VMEM(square, BF16), VMEM(square, BF16),
            VMEM((rank, width), BF16), VMEM((rank, width), BF16),
            VMEM((rank, width), BF16), VMEM((rank, width), BF16),
            VMEM(half_wide, BF16), VMEM(half_tall, BF16), VMEM(half_wide, BF16),
            VMEM((rows, 2 * rank, tokens), BF16),
            dma((8,)), dma((6,)), dma((2,)), dma((2,)),
        ],
        compiler_params=pltpu.CompilerParams(
            collective_id=0, has_side_effects=True, vmem_limit_bytes=limit
        ),
        name="project",
    )(
        hidden_in, out_grad, w_query, w_key, w_value, down_q, down_v,
        query_up_factor, value_up_factor,
    )
    place = lax.axis_index("seq").astype(jnp.int32).reshape(1)
    lo, grad, dqt, dk, dv, up = pl.pallas_call(
        layer_kernel,
        out_shape=[
            shape(tall, BF16), shape(tall, BF16), shape(wide, BF16), shape(tall, BF16),
            shape(tall, BF16), shape((2 * rank, width), F32),
        ],
        in_specs=[SMEM_SPEC] * 3 + [HBM_SPEC] * 20,
        out_specs=[HBM_SPEC] * 6,
        scratch_shapes=[
            VMEM((4, width), F32), VMEM((rank, width), BF16), VMEM((rank, width), BF16),
            VMEM(tall, BF16), VMEM(tall, BF16), VMEM(wide, BF16), VMEM(tall, BF16),
            VMEM(wide, BF16), VMEM((width, group), BF16), VMEM((group, width), BF16),
            VMEM((rows, 2 * rank, group), BF16),
            VMEM(square, BF16), VMEM(square, BF16), VMEM(square, BF16),
            VMEM(square, BF16), VMEM((width, hidden_units), BF16),
            VMEM((hidden_units, width), BF16),
            VMEM((HEADS, group, group), BF16), VMEM((2, group, group), F32),
            VMEM((width, group), BF16), VMEM((16, group), F32), VMEM((width, group), F32),
            VMEM((group, width), F32), VMEM((group, width), F32), VMEM((group, width), F32),
            VMEM((group, width), BF16), VMEM((group, hidden_units), BF16),
            VMEM((2, group, CHUNK), BF16), VMEM((4, group, group), BF16),
            VMEM((4, HEAD, group), BF16), VMEM((group, 1), F32),
            VMEM((rows, group, 128), BF16), VMEM((rows, 128, group), BF16),
            VMEM(tall, BF16), VMEM(tall, BF16), VMEM(wide, BF16), VMEM(tall, BF16),
            VMEM(tall, BF16), VMEM((2 * rank, width), F32),
            dma((20,)), dma((rows, 5)),
        ],
        compiler_params=pltpu.CompilerParams(vmem_limit_bytes=limit),
        name="layer",
    )(
        slot_sizes[0], live_lengths[0], place, attn_gain, attn_shift, ffn_gain, ffn_shift,
        low, down_q, down_v, hidden_in, out_grad, x_got, og_got,
        qt, keys, vt, wq_eff, w_key, wv_eff, w_output, w_expand, w_reduce,
    )
    count = len(phases())
    lo_got, ig, up = pl.pallas_call(
        finish_kernel,
        out_shape=[
            shape(half_tall, BF16), shape((micro, tokens, width), BF16),
            shape((2 * rank, width), F32),
        ],
        in_specs=[HBM_SPEC] * 9,
        out_specs=[HBM_SPEC] * 3,
        scratch_shapes=[
            VMEM((2 * rank, width), F32),
            VMEM((2, 2 * rank, width), F32), VMEM((count - 1, 4, 2 * rank, width), BF16),
            VMEM(tall, BF16), VMEM(wide, BF16), VMEM(tall, BF16), VMEM(tall, BF16),
            VMEM(square, BF16), VMEM(square, BF16), VMEM(square, BF16),
            VMEM((rows * tokens, width), F32), VMEM((2, rows, tokens, width), BF16),
            dma((8,)), dma((2,)), dma((2,)), dma((2,)), dma((count, 3)), dma((count, 4)),
        ],
        compiler_params=pltpu.CompilerParams(
            collective_id=1, has_side_effects=True, vmem_limit_bytes=limit
        ),
        name="finish",
    )(up, lo, grad, dqt, dk, dv, wq_eff, w_key, wv_eff)
    return pl.pallas_call(
        widen_kernel,
        out_shape=[
            shape((micro, tokens, width), BF16), shape((micro, tokens, width), F32),
            shape((rank, width), F32), shape((rank, width), F32),
        ],
        in_specs=[SMEM_SPEC] + [HBM_SPEC] * 4,
        out_specs=[HBM_SPEC] * 4,
        scratch_shapes=[
            VMEM((2,) + half_tall, BF16), VMEM((micro, tokens, width), BF16),
            VMEM((micro, tokens, width), F32), VMEM((2 * rank, width), F32),
            dma((micro + 3,)), dma((micro + 4,)),
        ],
        compiler_params=pltpu.CompilerParams(vmem_limit_bytes=limit),
        name="widen",
    )(place, lo, lo_got, ig, up)


def solution(mesh):
    tokens = P(None, ("dp", "seq"), None)
    table = P("dp", None, None)
    in_specs = (tokens, table, table) + (P(),) * 14 + (tokens,)
    out_specs = (tokens, tokens, P(), P())
    return jax.shard_map(shards, mesh=mesh, in_specs=in_specs, out_specs=out_specs, check_vma=False)
```

```python
import functools
import math

import jax
import jax.numpy as jnp
from jax import lax
from jax.experimental import pallas as pl
from jax.experimental.pallas import tpu as pltpu
from jax.sharding import PartitionSpec as P

HEADS = 12
HEAD = 64
NORM_EPS = 1e-05
ADAPTER_STRENGTH = 16.0
MASK_FILL = -1e30
LOG2_E = math.log2(math.e)
LN_2 = math.log(2.0)
CHUNK = 512
BF16 = jnp.bfloat16
F32 = jnp.float32
MESH = pl.DeviceIdType.MESH
VMEM = pltpu.VMEM
HBM_SPEC = pl.BlockSpec(memory_space=pl.ANY)
VMEM_SPEC = pl.BlockSpec(memory_space=pltpu.VMEM)
SMEM_SPEC = pl.BlockSpec(memory_space=pltpu.SMEM)


def dot(left, right, over_left, over_right):
    return lax.dot_general(
        left, right, (((over_left,), (over_right,)), ((), ())), preferred_element_type=F32
    )


def exchange_kernel(
    hidden, out_grad, wq, wk, wv, aq_in, av_in, bq_in, bv_in,
    x_out, og_out, qt_out, k_out, vt_out, low_out, wq_out, wv_out,
    x_s, wq_s, wk_s, wv_s, delta_s, aq, av, bq, bv, qt_s, k_s, vt_s, low_s,
    load, store, send, recv,
):
    rows, tokens, width = x_s.shape
    place = lax.axis_index("seq")
    other = 1 - place
    loads = [
        pltpu.make_async_copy(source, target, load.at[index])
        for index, (source, target) in enumerate([
            (aq_in, aq), (bq_in, bq), (av_in, av), (bv_in, bv),
            (wk, wk_s), (hidden.at[pl.ds(rows * place, rows)], x_s), (wq, wq_s), (wv, wv_s),
        ])
    ]
    for copy in loads:
        copy.start()
    barrier = pltpu.get_barrier_semaphore()
    pl.semaphore_signal(barrier, inc=1, device_id={"seq": other}, device_id_type=MESH)
    pl.semaphore_wait(barrier, 1)
    remote = [
        pltpu.make_async_remote_copy(
            src_ref=source.at[pl.ds(rows * other, rows)], dst_ref=target,
            send_sem=send.at[index], recv_sem=recv.at[index],
            device_id={"seq": other}, device_id_type=MESH,
        )
        for index, (source, target) in enumerate([(hidden, x_out), (out_grad, og_out)])
    ]
    for copy in remote:
        copy.start()
    strength = ADAPTER_STRENGTH / aq.shape[0]
    stores = []

    def keep(source, target):
        copy = pltpu.make_async_copy(source, target, store.at[len(stores)])
        copy.start()
        stores.append(copy)

    for copy in loads[:4]:
        copy.wait()
    thirds = [slice(at, at + 256) for at in range(0, width, 256)]
    for at in thirds:
        delta_s[0, at, :] = dot(aq[:, at], bq[...], 0, 0) * strength
        delta_s[1, at, :] = dot(av[:, at], bv[...], 0, 0) * strength
    for copy in loads[4:]:
        copy.wait()
    x = x_s[...].reshape(rows * tokens, width)

    def fold(weight, index, scale, at):
        weight[at, :] = ((weight[at, :].astype(F32) + delta_s[index, at, :]) * scale).astype(BF16)

    def project(weight, target, at):
        part = dot(weight[:, at], x, 0, 1).astype(BF16)
        for row in range(rows):
            target[row, at, :] = part[:, row * tokens:(row + 1) * tokens]

    for at in thirds:
        k_s[:, :, at] = dot(x, wk_s[:, at], 1, 0).astype(BF16).reshape(rows, tokens, 256)
        fold(wq_s, 0, LOG2_E / math.sqrt(HEAD), at)
    keep(k_s, k_out)
    keep(wq_s, wq_out)
    for at in thirds:
        project(wq_s, qt_s, at)
        fold(wv_s, 1, 1.0, at)
    keep(qt_s, qt_out)
    keep(wv_s, wv_out)
    low = jnp.concatenate([dot(aq[...], x, 1, 1), dot(av[...], x, 1, 1)], axis=0).astype(BF16)
    for row in range(rows):
        low_s[row] = low[:, row * tokens:(row + 1) * tokens]
    keep(low_s, low_out)
    for at in thirds:
        project(wv_s, vt_s, at)
    keep(vt_s, vt_out)
    for copy in stores:
        copy.wait()
    for copy in remote:
        copy.wait()


def layer_kernel(
    sizes, lives, place_ref, *refs
):
    (
        gain_one, shift_one, gain_two, shift_two, low_in, aq_in, av_in,
        hidden, out_grad, x_in, og_in, qt_in, k_in, vt_in, wq_in, wk_in, wv_in,
        wo_in, wx_in, wr_in,
        lo_out, g_out, dqt_out, dk_out, dv_out, up_out,
        vec_s, aq, av, x_s, og_s, qt_s, k_s, vt_s, kt_s, v_s, low_s, wq_s, wk_s, wv_s,
        wo_s, wx_s, wr_s, probs, score, ctx_s, inv_s, gctx_s, normed_s, back_s, acc_s, low16,
        slope_s, act_s, ds_s, do_s, rstd_s, kmask, qmask, lo_s, g_s, dqt_s, dk_s, dv_s, up_s,
        load, store,
    ) = refs
    rows, group, width = x_s.shape
    tokens = group // 2
    hidden_units = wx_s.shape[1]
    place = place_ref[0]
    slots = sizes.shape[1]
    pairs = HEADS // 2
    first = pl.ds(0, tokens)
    second = pl.ds(tokens, tokens)
    mine = pl.ds(rows * place, rows)
    plan = [
        (x_in, x_s.at[:, second]),
        (wk_in, wk_s),
        (wq_in, wq_s),
        (wv_in, wv_s),
        (qt_in, qt_s.at[:, :, first]),
        (k_in, k_s.at[:, first]),
        (vt_in, vt_s.at[:, :, first]),
        (wo_in, wo_s),
        (hidden.at[mine], x_s.at[:, first]),
        (wx_in, wx_s),
        (wr_in, wr_s),
        (out_grad.at[mine], og_s.at[:, first]),
        (og_in, og_s.at[:, second]),
        (aq_in, aq),
        (av_in, av),
        (low_in, low_s.at[:, :, first]),
    ] + [
        (vector, vec_s.at[index])
        for index, vector in enumerate((gain_one, shift_one, gain_two, shift_two))
    ]
    loads = [
        pltpu.make_async_copy(source, target, load.at[index])
        for index, (source, target) in enumerate(plan)
    ]
    small = loads[13:]
    for copy in loads[:2] + small + loads[2:13]:
        copy.start()

    def row_stores(row):
        plan = [
            (lo_s.at[row], lo_out.at[row]),
            (g_s.at[row], g_out.at[row]),
        ]
        for at in (pl.ds(0, width // 2), pl.ds(width // 2, width // 2)):
            plan += [
                (dqt_s.at[row, at], dqt_out.at[row, at]),
                (dk_s.at[row, :, at], dk_out.at[row, :, at]),
                (dv_s.at[row, :, at], dv_out.at[row, :, at]),
            ]
        return [
            pltpu.make_async_copy(source, target, store.at[row, index])
            for index, (source, target) in enumerate(plan)
        ]

    def make_masks(row):
        own = rows * place + row
        position = (lax.broadcasted_iota(jnp.int32, (group, 128), 0) + place * tokens) % group
        lane = lax.broadcasted_iota(jnp.int32, (1, 128), 1)
        low_end = jnp.full((1, 128), group, jnp.int32)
        high_end = low_end
        across = lax.broadcasted_iota(jnp.int32, (slots, group), 1)
        across = (across + place * tokens) % group
        line = lax.broadcasted_iota(jnp.int32, (slots, 1), 0)
        begin = jnp.full((slots, 1), group, jnp.int32)
        last = begin
        start = jnp.int32(0)
        crossing = jnp.int32(0)
        for slot in range(slots):
            size = sizes[own, slot]
            live = lives[own, slot]
            low_end = jnp.where(lane == slot, start, low_end)
            high_end = jnp.where(lane == slot, start + live, high_end)
            begin = jnp.where(line == slot, start, begin)
            last = jnp.where(line == slot, start + size, last)
            over = (start < tokens) & (start + size > tokens)
            crossing = jnp.where(over, 1, crossing)
            start = start + size
        dead = jnp.where((position >= low_end) & (position < high_end), 0.0, 1.0)
        kmask[row] = jnp.where(lane < slots, dead, 0.0).astype(BF16)
        within = jnp.where((across >= begin) & (across < last), MASK_FILL, 0.0)
        qmask[row] = jnp.concatenate(
            [within, jnp.zeros((128 - slots, group), F32)], axis=0
        ).astype(BF16)
        return crossing

    crossings = [make_masks(row) for row in range(rows)]
    loads[0].wait()
    loads[1].wait()
    x = x_s[:, tokens:, :].reshape(rows * tokens, width)
    k_s[:, tokens:, :] = dot(x, wk_s[...], 1, 0).astype(BF16).reshape(rows, tokens, width)
    for copy in small:
        copy.wait()
    low = jnp.concatenate([dot(aq[...], x, 1, 1), dot(av[...], x, 1, 1)], axis=0).astype(BF16)
    for row in range(rows):
        low_s[row, :, tokens:] = low[:, row * tokens:(row + 1) * tokens]
    for weight, target, copy in ((wq_s, qt_s, loads[2]), (wv_s, vt_s, loads[3])):
        copy.wait()
        part = dot(weight[...], x, 0, 1).astype(BF16)
        for row in range(rows):
            target[row, :, tokens:] = part[:, row * tokens:(row + 1) * tokens]
    for copy in loads[4:7]:
        copy.wait()

    gain_one, shift_one, gain_two, shift_two = (
        vec_s[index].reshape(1, width) for index in range(4)
    )

    def paired(top, bottom_zero):
        zero = jnp.zeros_like(top)
        return jnp.concatenate([top, zero] if bottom_zero else [zero, top], axis=0)

    def attend_forward(row, spans):
        def scores(head):
            pair, odd = divmod(head, 2)
            lanes = slice(pair * 128, pair * 128 + 128)
            query = qt_s[row, head * HEAD:(head + 1) * HEAD, :]
            right = jnp.concatenate([paired(query, odd == 0), qmask[row]], axis=0)
            for a, b in spans:
                left = jnp.concatenate([k_s[row, a:b, lanes], kmask[row, a:b, :]], axis=1)
                score[head % 2, a:b, a:b] = dot(left, right[:, a:b], 1, 0)

        def weights(head):
            for a, b in spans:
                part = score[head % 2, a:b, a:b]
                top = jnp.max(part, axis=0, keepdims=True)
                probs[head, a:b, a:b] = jnp.exp2(part - top).astype(BF16)

        def contexts(head):
            values = vt_s[row, head * HEAD:(head + 1) * HEAD, :]
            left = jnp.concatenate([values, jnp.ones((16, group), BF16)], axis=0)
            for a, b in spans:
                total = dot(left[:, a:b], probs[head, a:b, a:b], 1, 0)
                inverse = 1.0 / total[HEAD:HEAD + 1]
                inv_s[head:head + 1, a:b] = inverse
                ctx_s[head * HEAD:(head + 1) * HEAD, a:b] = (total[:HEAD] * inverse).astype(BF16)

        for step in range(HEADS + 2):
            if step < HEADS:
                scores(step)
            if 0 <= step - 1 < HEADS:
                weights(step - 1)
            if 0 <= step - 2:
                contexts(step - 2)

    def attend_backward(row, spans):
        def score_grads(head):
            pair, odd = divmod(head, 2)
            lanes = slice(pair * 128, pair * 128 + 128)
            here = slice(head * HEAD, (head + 1) * HEAD)
            slot = head % 4
            grad = gctx_s[here, :] * inv_s[head:head + 1, :]
            short = grad.astype(BF16)
            do_s[slot] = short
            delta = -jnp.sum(grad * ctx_s[here, :].astype(F32), axis=0, keepdims=True)
            high = delta.astype(BF16).astype(F32)
            index = lax.broadcasted_iota(jnp.int32, (16, group), 0)
            extra = jnp.where(index == 0, high, jnp.where(index == 1, delta - high, 0.0))
            right = jnp.concatenate(
                [paired(short, odd == 0), extra.astype(BF16), jnp.zeros((112, group), BF16)], axis=0
            )
            for a, b in spans:
                left = jnp.concatenate(
                    [v_s[a:b, lanes], jnp.ones((b - a, 128), BF16)], axis=1
                )
                part = dot(left, right[:, a:b], 1, 0)
                ds_s[slot, a:b, a:b] = (probs[head, a:b, a:b].astype(F32) * part).astype(BF16)

        def grads(pair):
            even, odd = 2 * pair, 2 * pair + 1
            for a, b in spans:
                for head in (even, odd):
                    here = slice(head * HEAD, (head + 1) * HEAD)
                    dqt_s[row, here, a:b] = (
                        dot(kt_s[here, a:b], ds_s[head % 4, a:b, a:b], 1, 0) * LN_2
                    ).astype(BF16)
                lanes = slice(pair * 128, pair * 128 + 128)
                left = jnp.concatenate([ds_s[even % 4, a:b, a:b], ds_s[odd % 4, a:b, a:b]], axis=1)
                right = jnp.concatenate(
                    [
                        paired(qt_s[row, even * HEAD:even * HEAD + HEAD, a:b], True),
                        paired(qt_s[row, odd * HEAD:odd * HEAD + HEAD, a:b], False),
                    ],
                    axis=1,
                )
                dk_s[row, a:b, lanes] = (dot(left, right, 1, 1) * LN_2).astype(BF16)
                left = jnp.concatenate([probs[even, a:b, a:b], probs[odd, a:b, a:b]], axis=1)
                right = jnp.concatenate(
                    [paired(do_s[even % 4, :, a:b], True), paired(do_s[odd % 4, :, a:b], False)],
                    axis=1,
                )
                dv_s[row, a:b, lanes] = dot(left, right, 1, 1).astype(BF16)

        for step in range(pairs + 1):
            if step < pairs:
                score_grads(2 * step)
                score_grads(2 * step + 1)
            if step >= 1:
                grads(step - 1)
            if step == pairs // 2:
                for copy in row_stores(row)[2:5]:
                    copy.start()

    def mean(value):
        return jnp.sum(value, axis=-1, keepdims=True) * (1.0 / width)

    def weave(main, side):
        for index, step in enumerate(main):
            step()
            for part in side[index * len(side) // len(main):(index + 1) * len(side) // len(main)]:
                part()

    chunks = hidden_units // CHUNK
    piece = 32

    def feed_forward(row):
        def blocks(half, body):
            start = half * tokens
            return [
                functools.partial(body, slice(at, at + piece))
                for at in range(start, start + tokens, piece)
            ]

        def span(half):
            return slice(half * tokens, (half + 1) * tokens)

        def attended(half):
            def step(at):
                acc_s[span(half), at] = dot(ctx_s[:, span(half)], wo_s[:, at], 0, 0)

            return [
                functools.partial(step, slice(at, at + 256)) for at in range(0, width, 256)
            ]

        def norm_one(at):
            resid = x_s[row, at, :].astype(F32) + acc_s[at, :]
            center = resid - mean(resid)
            scaled = lax.rsqrt(mean(center * center) + NORM_EPS)
            normed = center * scaled
            normed_s[at, :] = normed
            rstd_s[at, :] = scaled
            low16[at, :] = (normed * gain_one + shift_one).astype(BF16)

        def forward(half):
            here = span(half)

            def run(step):
                if step < chunks:
                    at = slice(step * CHUNK, (step + 1) * CHUNK)
                    score[step % 2, here, :] = dot(low16[here, :], wx_s[:, at], 1, 0)
                if 0 <= step - 1 < chunks:
                    at = slice((step - 1) * CHUNK, step * CHUNK)
                    inner = score[(step - 1) % 2, here, :]
                    upto = 0.5 + 0.5 * lax.erf(inner * math.sqrt(0.5))
                    bell = jnp.exp2(inner * inner * (-0.5 * LOG2_E)) * (
                        1.0 / math.sqrt(2.0 * math.pi)
                    )
                    act_s[(step - 1) % 2, here, :] = (inner * upto).astype(BF16)
                    slope_s[here, at] = (upto + inner * bell).astype(BF16)
                if 0 <= step - 2:
                    at = slice((step - 2) * CHUNK, (step - 1) * CHUNK)
                    part = dot(act_s[(step - 2) % 2, here, :], wr_s[at, :], 1, 0)
                    if step == 2:
                        acc_s[here, :] = part
                    else:
                        acc_s[here, :] += part

            return [functools.partial(run, step) for step in range(chunks + 2)]

        def norm_two(at):
            z = normed_s[at, :] * gain_one + shift_one + acc_s[at, :]
            center = z - mean(z)
            scaled = lax.rsqrt(mean(center * center) + NORM_EPS)
            normed = center * scaled
            lo_s[row, at, :] = (normed * gain_two + shift_two).astype(BF16)
            weighted = og_s[row, at, :].astype(F32) * gain_two
            grad = scaled * (weighted - mean(weighted) - normed * mean(weighted * normed))
            back_s[at, :] = grad
            low16[at, :] = grad.astype(BF16)

        def backward(half):
            here = span(half)

            def run(step):
                if step < chunks:
                    at = slice(step * CHUNK, (step + 1) * CHUNK)
                    part = dot(low16[here, :], wr_s[at, :], 1, 1)
                    act_s[step % 2, here, :] = (part * slope_s[here, at].astype(F32)).astype(BF16)
                if step >= 1:
                    at = slice((step - 1) * CHUNK, step * CHUNK)
                    part = dot(act_s[(step - 1) % 2, here, :], wx_s[:, at], 1, 1)
                    if step == 1:
                        acc_s[here, :] = part
                    else:
                        acc_s[here, :] += part

            return [functools.partial(run, step) for step in range(chunks + 1)]

        def norm_one_back(at):
            weighted = (back_s[at, :] + acc_s[at, :]) * gain_one
            normed = normed_s[at, :]
            grad = rstd_s[at, :] * (
                weighted - mean(weighted) - normed * mean(weighted * normed)
            )
            g_s[row, at, :] = grad.astype(BF16)

        def context_grad(half):
            def step(at):
                gctx_s[at, span(half)] = dot(wo_s[at, :], g_s[row, span(half), :], 1, 1)

            return [
                functools.partial(step, slice(at, at + 256)) for at in range(0, width, 256)
            ]

        def turn(half):
            def step(at):
                kt_s[at, span(half)] = k_s[row, span(half), at].T
                v_s[span(half), at] = vt_s[row, at, span(half)].T

            return [
                functools.partial(step, slice(at, at + 128)) for at in range(0, width, 128)
            ]

        weave(attended(0), [])
        weave(attended(1), blocks(0, norm_one))

        weave(forward(0), blocks(1, norm_one))

        weave(forward(1), blocks(0, norm_two))
        weave(backward(0), blocks(1, norm_two))
        weave(backward(1), blocks(0, norm_one_back) + turn(0) + turn(1))
        weave(context_grad(0), blocks(1, norm_one_back))
        weave(context_grad(1), [])

    def one_row(row, carry):
        crossing = jnp.where(row == 0, crossings[0], crossings[1])

        @pl.when(crossing == 1)
        def _():
            attend_forward(row, [(0, group)])

        @pl.when(crossing == 0)
        def _():
            attend_forward(row, [(0, tokens), (tokens, group)])

        @pl.when(row == 0)
        def _():
            for copy in loads[7:13]:
                copy.wait()

        feed_forward(row)
        for copy in row_stores(row)[:2]:
            copy.start()

        @pl.when(crossing == 1)
        def _():
            attend_backward(row, [(0, group)])

        @pl.when(crossing == 0)
        def _():
            attend_backward(row, [(0, tokens), (tokens, group)])

        for copy in row_stores(row)[5:]:
            copy.start()
        from_q = dot(low_s[row], dqt_s[row], 1, 1) * (
            ADAPTER_STRENGTH / slots_rank / math.sqrt(HEAD) / LN_2
        )
        from_v = dot(low_s[row], dv_s[row], 1, 0) * (ADAPTER_STRENGTH / slots_rank)
        rank_line = lax.broadcasted_iota(jnp.int32, (2 * slots_rank, 1), 0)
        part = jnp.where(rank_line < slots_rank, from_q, from_v)
        up_s[...] = jnp.where(row == 0, part, up_s[...] + part)
        return carry

    slots_rank = low_s.shape[1] // 2
    lax.fori_loop(0, rows, one_row, 0)
    keep_up = pltpu.make_async_copy(up_s, up_out, load.at[0])
    keep_up.start()
    for row in range(rows):
        for copy in row_stores(row):
            copy.wait()
    keep_up.wait()


def phases():
    found = [("seq", 1, 2)]
    stride, left = 1, lax.axis_size("dp")
    while left > 1:
        size = 4 if left % 4 == 0 else left if left < 4 else 2
        found.append(("dp", stride, size))
        stride, left = stride * size, left // size
    return found


def finish_kernel(
    up, lo, grad, dqt, dk, dv, wq, wk, wv,
    lo_out, ig_out, up_out,
    up_s, pair, got, grad_s, dqt_s, dk_s, dv_s, wq_s, wk_s, wv_s, acc_s, res_s,
    load, store, send, recv, ar_send, ar_recv,
):
    rows, group, width = grad_s.shape
    tokens = group // 2
    place = lax.axis_index("seq")
    other = 1 - place
    plan = [
        (dqt, dqt_s), (wq, wq_s), (dk, dk_s), (wk, wk_s), (dv, dv_s), (wv, wv_s),
        (grad, grad_s), (up, up_s),
    ]
    loads = [
        pltpu.make_async_copy(source, target, load.at[index])
        for index, (source, target) in enumerate(plan)
    ]
    for copy in loads[7:] + loads[:7]:
        copy.start()
    barrier = pltpu.get_barrier_semaphore()
    rounds = []
    greeted = 0
    for axis, stride, size in phases():
        me = lax.axis_index(axis)
        digit = (me // stride) % size
        others = []
        for step in range(1, size):
            theirs = (digit + step) % size
            others.append((theirs, {axis: me + (theirs - digit) * stride}))
        for _, device in others:
            pl.semaphore_signal(barrier, inc=1, device_id=device, device_id_type=MESH)
        greeted += len(others)
        rounds.append((size, digit, others))
    pl.semaphore_wait(barrier, greeted)
    mine = pl.ds(rows * place, rows)

    def copies(index):
        size, digit, others = rounds[index]
        buffer = pair if index == 0 else got.at[index - 1]
        sends = [
            pltpu.make_async_remote_copy(
                src_ref=buffer.at[digit], dst_ref=buffer.at[digit],
                send_sem=ar_send.at[index, step], recv_sem=ar_recv.at[index, digit],
                device_id=device, device_id_type=MESH,
            )
            for step, (_, device) in enumerate(others)
        ]
        arrivals = [
            pltpu.make_async_remote_copy(
                src_ref=buffer.at[theirs], dst_ref=buffer.at[theirs],
                send_sem=ar_send.at[index, step], recv_sem=ar_recv.at[index, theirs],
                device_id=device, device_id_type=MESH,
            )
            for step, (theirs, device) in enumerate(others)
        ]
        return sends, arrivals

    def sibling(source, target, index):
        return pltpu.make_async_remote_copy(
            src_ref=source, dst_ref=target, send_sem=send.at[index], recv_sem=recv.at[index],
            device_id={"seq": other}, device_id_type=MESH,
        )

    keep_up = pltpu.make_async_copy(up_s, up_out, store.at[0])
    all_copies = [copies(index) for index in range(len(rounds))]

    def begin(index, value):
        digit = rounds[index][1]
        if index == 0:
            pair[digit] = value
        else:
            got[index - 1, digit] = value.astype(BF16)
        for copy in all_copies[index][0]:
            copy.start()

    def end(index):
        size = rounds[index][0]
        for copy in all_copies[index][1]:
            copy.wait_recv()
        buffer = pair if index == 0 else got.at[index - 1]
        value = buffer[0].astype(F32)
        for step in range(1, size):
            value = value + buffer[step].astype(F32)
        return value

    loads[7].wait()
    begin(0, up_s[...])
    lo_copy = sibling(lo.at[:, pl.ds(tokens, tokens)], lo_out, 1)
    lo_copy.start()
    done = [0]

    def advance():
        if done[0] < len(rounds):
            value = end(done[0])
            done[0] += 1
            if done[0] < len(rounds):
                begin(done[0], value)
            else:
                up_s[...] = value
                keep_up.start()

    def from_q(half):
        span = slice(half * tokens, (half + 1) * tokens)
        left = jnp.concatenate([dqt_s[row, :, span] for row in range(rows)], axis=1)
        acc_s[...] = dot(left, wq_s[...], 0, 1)

    def part(source, weight, half):
        left = source[:, half * tokens:(half + 1) * tokens, :].reshape(rows * tokens, width)
        return dot(left, weight[...], 1, 1)

    def from_k(half):
        acc_s[...] += part(dk_s, wk_s, half)

    def from_v(half):
        span = slice(half * tokens, (half + 1) * tokens)
        value = acc_s[...] + part(dv_s, wv_s, half)
        value += grad_s[:, span, :].reshape(rows * tokens, width).astype(F32)
        res_s[half] = value.astype(BF16).reshape(rows, tokens, width)

    loads[0].wait()
    loads[1].wait()
    from_q(1)
    advance()
    loads[2].wait()
    loads[3].wait()
    from_k(1)
    for copy in loads[4:7]:
        copy.wait()
    from_v(1)
    ig_copy = sibling(res_s.at[1], ig_out.at[mine], 0)
    ig_copy.start()
    advance()
    from_q(0)
    from_k(0)
    from_v(0)
    keep_ig = pltpu.make_async_copy(res_s.at[0], ig_out.at[mine], store.at[1])
    keep_ig.start()
    for _ in range(len(rounds)):
        advance()
    for sends, _ in all_copies:
        for copy in sends:
            copy.wait_send()
    keep_up.wait()
    keep_ig.wait()
    lo_copy.wait()
    ig_copy.wait()


def widen_kernel(
    place_ref, lo, lo_got, ig, up, lo_out, ig_out, upq_out, upv_out,
    lo_s, ig_s, wide_s, up_s, load, store,
):
    micro, tokens, width = ig_s.shape
    rows = micro // 2
    place = place_ref[0]
    own = pl.ds(rows * place, rows)
    rest = pl.ds(rows * (1 - place), rows)
    rank = upq_out.shape[0]
    loads = [
        pltpu.make_async_copy(ig.at[index], ig_s.at[index], load.at[index])
        for index in range(micro)
    ] + [
        pltpu.make_async_copy(up, up_s, load.at[micro]),
        pltpu.make_async_copy(lo.at[:, pl.ds(0, tokens)], lo_s.at[0], load.at[micro + 1]),
        pltpu.make_async_copy(lo_got, lo_s.at[1], load.at[micro + 2]),
    ]
    for copy in loads:
        copy.start()
    widened = [
        pltpu.make_async_copy(wide_s.at[index], ig_out.at[index], store.at[index])
        for index in range(micro)
    ]
    for index in range(micro):
        loads[index].wait()
        wide_s[index] = ig_s[index].astype(F32)
        widened[index].start()
    stores = [
        pltpu.make_async_copy(up_s.at[pl.ds(0, rank)], upq_out, store.at[micro]),
        pltpu.make_async_copy(up_s.at[pl.ds(rank, rank)], upv_out, store.at[micro + 1]),
        pltpu.make_async_copy(lo_s.at[0], lo_out.at[own], store.at[micro + 2]),
        pltpu.make_async_copy(lo_s.at[1], lo_out.at[rest], store.at[micro + 3]),
    ]
    for copy in loads[micro:]:
        copy.wait()
    for copy in stores:
        copy.start()
    for copy in widened + stores:
        copy.wait()


def shards(
    hidden_in, slot_sizes, live_lengths, w_query, w_key, w_value, query_down_factor, down_value,
    query_up_factor, value_up_factor, w_output, attn_gain, attn_shift, w_expand, w_reduce,
    ffn_gain, ffn_shift, out_grad,
):
    micro, tokens, width = hidden_in.shape
    rows = micro // 2
    group = 2 * tokens
    hidden_units = w_expand.shape[1]
    rank = query_down_factor.shape[1]
    shape = jax.ShapeDtypeStruct
    dma = pltpu.SemaphoreType.DMA
    wide = (rows, width, group)
    tall = (rows, group, width)
    half_tall = (rows, tokens, width)
    half_wide = (rows, width, tokens)
    square = (width, width)
    limit = 62 * 2 ** 20
    down_q, down_v = query_down_factor.T, down_value.T
    x_got, og_got, qt, keys, vt, low, wq_eff, wv_eff = pl.pallas_call(
        exchange_kernel,
        out_shape=[
            shape(half_tall, BF16), shape(half_tall, BF16), shape(half_wide, BF16),
            shape(half_tall, BF16), shape(half_wide, BF16), shape((rows, 2 * rank, tokens), BF16),
            shape(square, BF16), shape(square, BF16),
        ],
        in_specs=[HBM_SPEC] * 9,
        out_specs=[HBM_SPEC] * 8,
        scratch_shapes=[
            VMEM(half_tall, BF16), VMEM(square, BF16), VMEM(square, BF16), VMEM(square, BF16),
            VMEM((2, width, width), F32),
            VMEM((rank, width), BF16), VMEM((rank, width), BF16),
            VMEM((rank, width), BF16), VMEM((rank, width), BF16),
            VMEM(half_wide, BF16), VMEM(half_tall, BF16), VMEM(half_wide, BF16),
            VMEM((rows, 2 * rank, tokens), BF16),
            dma((8,)), dma((6,)), dma((2,)), dma((2,)),
        ],
        compiler_params=pltpu.CompilerParams(
            collective_id=0, has_side_effects=True, vmem_limit_bytes=limit
        ),
        name="project",
    )(
        hidden_in, out_grad, w_query, w_key, w_value, down_q, down_v,
        query_up_factor, value_up_factor,
    )
    place = lax.axis_index("seq").astype(jnp.int32).reshape(1)
    lo, grad, dqt, dk, dv, up = pl.pallas_call(
        layer_kernel,
        out_shape=[
            shape(tall, BF16), shape(tall, BF16), shape(wide, BF16), shape(tall, BF16),
            shape(tall, BF16), shape((2 * rank, width), F32),
        ],
        in_specs=[SMEM_SPEC] * 3 + [HBM_SPEC] * 20,
        out_specs=[HBM_SPEC] * 6,
        scratch_shapes=[
            VMEM((4, width), F32), VMEM((rank, width), BF16), VMEM((rank, width), BF16),
            VMEM(tall, BF16), VMEM(tall, BF16), VMEM(wide, BF16), VMEM(tall, BF16),
            VMEM(wide, BF16), VMEM((width, group), BF16), VMEM((group, width), BF16),
            VMEM((rows, 2 * rank, group), BF16),
            VMEM(square, BF16), VMEM(square, BF16), VMEM(square, BF16),
            VMEM(square, BF16), VMEM((width, hidden_units), BF16),
            VMEM((hidden_units, width), BF16),
            VMEM((HEADS, group, group), BF16), VMEM((2, group, group), F32),
            VMEM((width, group), BF16), VMEM((16, group), F32), VMEM((width, group), F32),
            VMEM((group, width), F32), VMEM((group, width), F32), VMEM((group, width), F32),
            VMEM((group, width), BF16), VMEM((group, hidden_units), BF16),
            VMEM((2, group, CHUNK), BF16), VMEM((4, group, group), BF16),
            VMEM((4, HEAD, group), BF16), VMEM((group, 1), F32),
            VMEM((rows, group, 128), BF16), VMEM((rows, 128, group), BF16),
            VMEM(tall, BF16), VMEM(tall, BF16), VMEM(wide, BF16), VMEM(tall, BF16),
            VMEM(tall, BF16), VMEM((2 * rank, width), F32),
            dma((20,)), dma((rows, 8)),
        ],
        compiler_params=pltpu.CompilerParams(vmem_limit_bytes=limit),
        name="layer",
    )(
        slot_sizes[0], live_lengths[0], place, attn_gain, attn_shift, ffn_gain, ffn_shift,
        low, down_q, down_v, hidden_in, out_grad, x_got, og_got,
        qt, keys, vt, wq_eff, w_key, wv_eff, w_output, w_expand, w_reduce,
    )
    count = len(phases())
    lo_got, ig, up = pl.pallas_call(
        finish_kernel,
        out_shape=[
            shape(half_tall, BF16), shape((micro, tokens, width), BF16),
            shape((2 * rank, width), F32),
        ],
        in_specs=[HBM_SPEC] * 9,
        out_specs=[HBM_SPEC] * 3,
        scratch_shapes=[
            VMEM((2 * rank, width), F32),
            VMEM((2, 2 * rank, width), F32), VMEM((count - 1, 4, 2 * rank, width), BF16),
            VMEM(tall, BF16), VMEM(wide, BF16), VMEM(tall, BF16), VMEM(tall, BF16),
            VMEM(square, BF16), VMEM(square, BF16), VMEM(square, BF16),
            VMEM((rows * tokens, width), F32), VMEM((2, rows, tokens, width), BF16),
            dma((8,)), dma((2,)), dma((2,)), dma((2,)), dma((count, 3)), dma((count, 4)),
        ],
        compiler_params=pltpu.CompilerParams(
            collective_id=1, has_side_effects=True, vmem_limit_bytes=limit
        ),
        name="finish",
    )(up, lo, grad, dqt, dk, dv, wq_eff, w_key, wv_eff)
    return pl.pallas_call(
        widen_kernel,
        out_shape=[
            shape((micro, tokens, width), BF16), shape((micro, tokens, width), F32),
            shape((rank, width), F32), shape((rank, width), F32),
        ],
        in_specs=[SMEM_SPEC] + [HBM_SPEC] * 4,
        out_specs=[HBM_SPEC] * 4,
        scratch_shapes=[
            VMEM((2,) + half_tall, BF16), VMEM((micro, tokens, width), BF16),
            VMEM((micro, tokens, width), F32), VMEM((2 * rank, width), F32),
            dma((micro + 3,)), dma((micro + 4,)),
        ],
        compiler_params=pltpu.CompilerParams(vmem_limit_bytes=limit),
        name="widen",
    )(place, lo, lo_got, ig, up)


def solution(mesh):
    tokens = P(None, ("dp", "seq"), None)
    table = P("dp", None, None)
    in_specs = (tokens, table, table) + (P(),) * 14 + (tokens,)
    out_specs = (tokens, tokens, P(), P())
    return jax.shard_map(shards, mesh=mesh, in_specs=in_specs, out_specs=out_specs, check_vma=False)
```

```python
import functools
import math

import jax
import jax.numpy as jnp
from jax import lax
from jax.experimental import pallas as pl
from jax.experimental.pallas import tpu as pltpu
from jax.sharding import PartitionSpec as P

HEADS = 12
HEAD = 64
NORM_EPS = 1e-05
ADAPTER_STRENGTH = 16.0
MASK_FILL = -1e30
LOG2_E = math.log2(math.e)
LN_2 = math.log(2.0)
CHUNK = 512
BF16 = jnp.bfloat16
F32 = jnp.float32
MESH = pl.DeviceIdType.MESH
VMEM = pltpu.VMEM
HBM_SPEC = pl.BlockSpec(memory_space=pl.ANY)
VMEM_SPEC = pl.BlockSpec(memory_space=pltpu.VMEM)
SMEM_SPEC = pl.BlockSpec(memory_space=pltpu.SMEM)


def dot(left, right, over_left, over_right):
    return lax.dot_general(
        left, right, (((over_left,), (over_right,)), ((), ())), preferred_element_type=F32
    )


def exchange_kernel(
    hidden, out_grad, wq, wk, wv, aq, av, bq, bv,
    x_out, og_out, qt_out, k_out, vt_out, low_out, wq_out, wv_out, down_out,
    x_s, wq_s, wk_s, wv_s, delta_s, down_s, qt_s, k_s, vt_s, low_s,
    load, store, send, recv,
):
    rows, tokens, width = x_s.shape
    place = lax.axis_index("seq")
    other = 1 - place
    loads = [
        pltpu.make_async_copy(source, target, load.at[index])
        for index, (source, target) in enumerate([
            (wk, wk_s), (hidden.at[pl.ds(rows * place, rows)], x_s), (wq, wq_s), (wv, wv_s),
        ])
    ]
    for copy in loads[:2]:
        copy.start()
    barrier = pltpu.get_barrier_semaphore()
    pl.semaphore_signal(barrier, inc=1, device_id={"seq": other}, device_id_type=MESH)
    pl.semaphore_wait(barrier, 1)
    remote = [
        pltpu.make_async_remote_copy(
            src_ref=source.at[pl.ds(rows * other, rows)], dst_ref=target,
            send_sem=send.at[index], recv_sem=recv.at[index],
            device_id={"seq": other}, device_id_type=MESH,
        )
        for index, (source, target) in enumerate([(hidden, x_out), (out_grad, og_out)])
    ]
    for copy in remote:
        copy.start()
    strength = ADAPTER_STRENGTH / aq.shape[0]
    stores = []

    def keep(source, target):
        copy = pltpu.make_async_copy(source, target, store.at[len(stores)])
        copy.start()
        stores.append(copy)

    for copy in loads[2:]:
        copy.start()
    thirds = [slice(at, at + 256) for at in range(0, width, 256)]
    for at in thirds:
        delta_s[0, at, :] = dot(aq[:, at], bq[...], 0, 0) * strength
        delta_s[1, at, :] = dot(av[:, at], bv[...], 0, 0) * strength
    down_s[...] = jnp.concatenate(
        [aq[...].astype(F32), av[...].astype(F32)], axis=0
    ).astype(BF16)
    keep(down_s, down_out)
    for copy in loads[:2]:
        copy.wait()
    x = x_s[...].reshape(rows * tokens, width)

    def fold(weight, index, scale, at):
        weight[at, :] = ((weight[at, :].astype(F32) + delta_s[index, at, :]) * scale).astype(BF16)

    def project(weight, target, at):
        part = dot(weight[:, at], x, 0, 1).astype(BF16)
        for row in range(rows):
            target[row, at, :] = part[:, row * tokens:(row + 1) * tokens]

    for at in thirds:
        k_s[:, :, at] = dot(x, wk_s[:, at], 1, 0).astype(BF16).reshape(rows, tokens, 256)
    for copy in loads[2:]:
        copy.wait()
    for at in thirds:
        fold(wq_s, 0, LOG2_E / math.sqrt(HEAD), at)
    keep(k_s, k_out)
    keep(wq_s, wq_out)
    for at in thirds:
        project(wq_s, qt_s, at)
        fold(wv_s, 1, 1.0, at)
    keep(qt_s, qt_out)
    keep(wv_s, wv_out)
    low = dot(down_s[...], x, 1, 1).astype(BF16)
    for row in range(rows):
        low_s[row] = low[:, row * tokens:(row + 1) * tokens]
    keep(low_s, low_out)
    for at in thirds:
        project(wv_s, vt_s, at)
    keep(vt_s, vt_out)
    for copy in stores:
        copy.wait()
    for copy in remote:
        copy.wait()


def layer_kernel(
    sizes, lives, place_ref, *refs
):
    (
        gain_one, shift_one, gain_two, shift_two, low_in, down_in,
        hidden, out_grad, x_in, og_in, qt_in, k_in, vt_in, wq_in, wk_in, wv_in,
        wo_in, wx_in, wr_in,
        lo_out, lo_send, g_out, dqt_out, dk_out, dv_out, up_out,
        vec_s, down_s, x_s, og_s, qt_s, k_s, vt_s, kt_s, v_s, low_s, wq_s, wk_s, wv_s,
        wo_s, wx_s, wr_s, probs, score, ctx_s, inv_s, gctx_s, normed_s, back_s, acc_s, low16,
        slope_s, act_s, ds_s, do_s, rstd_s, kmask, qmask, lo_s, g_s, dqt_s, dk_s, dv_s, up_s,
        load, store,
    ) = refs
    rows, group, width = x_s.shape
    tokens = group // 2
    hidden_units = wx_s.shape[1]
    place = place_ref[0]
    slots = sizes.shape[1]
    pairs = HEADS // 2
    first = pl.ds(0, tokens)
    second = pl.ds(tokens, tokens)
    mine = pl.ds(rows * place, rows)
    plan = [
        (x_in, x_s.at[:, second]),
        (wk_in, wk_s),
        (wq_in, wq_s),
        (wv_in, wv_s),
        (qt_in, qt_s.at[:, :, first]),
        (k_in, k_s.at[:, first]),
        (vt_in, vt_s.at[:, :, first]),
        (wo_in, wo_s),
        (hidden.at[mine], x_s.at[:, first]),
        (wx_in, wx_s),
        (wr_in, wr_s),
        (out_grad.at[mine], og_s.at[:, first]),
        (og_in, og_s.at[:, second]),
        (down_in, down_s),
        (low_in, low_s.at[:, :, first]),
    ] + [
        (vector, vec_s.at[index])
        for index, vector in enumerate((gain_one, shift_one, gain_two, shift_two))
    ]
    loads = [
        pltpu.make_async_copy(source, target, load.at[index])
        for index, (source, target) in enumerate(plan)
    ]
    small = loads[13:]
    for copy in loads[:2] + small + loads[2:13]:
        copy.start()

    def row_stores(row):
        plan = [
            (lo_s.at[row, first], lo_out.at[rows * place + row]),
            (lo_s.at[row, second], lo_send.at[row]),
            (g_s.at[row], g_out.at[row]),
        ]
        for at in (pl.ds(0, width // 2), pl.ds(width // 2, width // 2)):
            plan += [
                (dqt_s.at[row, at], dqt_out.at[row, at]),
                (dk_s.at[row, :, at], dk_out.at[row, :, at]),
                (dv_s.at[row, :, at], dv_out.at[row, :, at]),
            ]
        return [
            pltpu.make_async_copy(source, target, store.at[row, index])
            for index, (source, target) in enumerate(plan)
        ]

    def make_masks(row):
        own = rows * place + row
        position = (lax.broadcasted_iota(jnp.int32, (group, 128), 0) + place * tokens) % group
        lane = lax.broadcasted_iota(jnp.int32, (1, 128), 1)
        low_end = jnp.full((1, 128), group, jnp.int32)
        high_end = low_end
        across = lax.broadcasted_iota(jnp.int32, (slots, group), 1)
        across = (across + place * tokens) % group
        line = lax.broadcasted_iota(jnp.int32, (slots, 1), 0)
        begin = jnp.full((slots, 1), group, jnp.int32)
        last = begin
        start = jnp.int32(0)
        crossing = jnp.int32(0)
        for slot in range(slots):
            size = sizes[own, slot]
            live = lives[own, slot]
            low_end = jnp.where(lane == slot, start, low_end)
            high_end = jnp.where(lane == slot, start + live, high_end)
            begin = jnp.where(line == slot, start, begin)
            last = jnp.where(line == slot, start + size, last)
            over = (start < tokens) & (start + size > tokens)
            crossing = jnp.where(over, 1, crossing)
            start = start + size
        dead = jnp.where((position >= low_end) & (position < high_end), 0.0, 1.0)
        kmask[row] = jnp.where(lane < slots, dead, 0.0).astype(BF16)
        within = jnp.where((across >= begin) & (across < last), MASK_FILL, 0.0)
        qmask[row] = jnp.concatenate(
            [within, jnp.zeros((128 - slots, group), F32)], axis=0
        ).astype(BF16)
        return crossing

    crossings = [make_masks(row) for row in range(rows)]
    loads[0].wait()
    loads[1].wait()
    x = x_s[:, tokens:, :].reshape(rows * tokens, width)
    k_s[:, tokens:, :] = dot(x, wk_s[...], 1, 0).astype(BF16).reshape(rows, tokens, width)
    for copy in small:
        copy.wait()
    low = dot(down_s[...], x, 1, 1).astype(BF16)
    for row in range(rows):
        low_s[row, :, tokens:] = low[:, row * tokens:(row + 1) * tokens]
    for weight, target, copy in ((wq_s, qt_s, loads[2]), (wv_s, vt_s, loads[3])):
        copy.wait()
        part = dot(weight[...], x, 0, 1).astype(BF16)
        for row in range(rows):
            target[row, :, tokens:] = part[:, row * tokens:(row + 1) * tokens]
    for copy in loads[4:7]:
        copy.wait()

    gain_one, shift_one, gain_two, shift_two = (
        vec_s[index].reshape(1, width) for index in range(4)
    )

    def paired(top, bottom_zero):
        zero = jnp.zeros_like(top)
        return jnp.concatenate([top, zero] if bottom_zero else [zero, top], axis=0)

    def attend_forward(row, spans):
        def scores(head):
            pair, odd = divmod(head, 2)
            lanes = slice(pair * 128, pair * 128 + 128)
            query = qt_s[row, head * HEAD:(head + 1) * HEAD, :]
            right = jnp.concatenate([paired(query, odd == 0), qmask[row]], axis=0)
            for a, b in spans:
                left = jnp.concatenate([k_s[row, a:b, lanes], kmask[row, a:b, :]], axis=1)
                score[head % 2, a:b, a:b] = dot(left, right[:, a:b], 1, 0)

        def weights(head):
            for a, b in spans:
                part = score[head % 2, a:b, a:b]
                top = jnp.max(part, axis=0, keepdims=True)
                probs[head, a:b, a:b] = jnp.exp2(part - top).astype(BF16)

        def contexts(head):
            values = vt_s[row, head * HEAD:(head + 1) * HEAD, :]
            left = jnp.concatenate([values, jnp.ones((16, group), BF16)], axis=0)
            for a, b in spans:
                total = dot(left[:, a:b], probs[head, a:b, a:b], 1, 0)
                inverse = 1.0 / total[HEAD:HEAD + 1]
                inv_s[head:head + 1, a:b] = inverse
                ctx_s[head * HEAD:(head + 1) * HEAD, a:b] = (total[:HEAD] * inverse).astype(BF16)

        for step in range(HEADS + 2):
            if step < HEADS:
                scores(step)
            if 0 <= step - 1 < HEADS:
                weights(step - 1)
            if 0 <= step - 2:
                contexts(step - 2)

    def attend_backward(row, spans):
        def score_grads(head):
            pair, odd = divmod(head, 2)
            lanes = slice(pair * 128, pair * 128 + 128)
            here = slice(head * HEAD, (head + 1) * HEAD)
            slot = head % 4
            grad = gctx_s[here, :] * inv_s[head:head + 1, :]
            short = grad.astype(BF16)
            do_s[slot] = short
            delta = -jnp.sum(grad * ctx_s[here, :].astype(F32), axis=0, keepdims=True)
            high = delta.astype(BF16).astype(F32)
            index = lax.broadcasted_iota(jnp.int32, (16, group), 0)
            extra = jnp.where(index == 0, high, jnp.where(index == 1, delta - high, 0.0))
            right = jnp.concatenate(
                [paired(short, odd == 0), extra.astype(BF16), jnp.zeros((112, group), BF16)], axis=0
            )
            for a, b in spans:
                left = jnp.concatenate(
                    [v_s[a:b, lanes], jnp.ones((b - a, 128), BF16)], axis=1
                )
                part = dot(left, right[:, a:b], 1, 0)
                ds_s[slot, a:b, a:b] = (probs[head, a:b, a:b].astype(F32) * part).astype(BF16)

        def grads(pair):
            even, odd = 2 * pair, 2 * pair + 1
            for a, b in spans:
                for head in (even, odd):
                    here = slice(head * HEAD, (head + 1) * HEAD)
                    dqt_s[row, here, a:b] = (
                        dot(kt_s[here, a:b], ds_s[head % 4, a:b, a:b], 1, 0) * LN_2
                    ).astype(BF16)
                lanes = slice(pair * 128, pair * 128 + 128)
                left = jnp.concatenate([ds_s[even % 4, a:b, a:b], ds_s[odd % 4, a:b, a:b]], axis=1)
                right = jnp.concatenate(
                    [
                        paired(qt_s[row, even * HEAD:even * HEAD + HEAD, a:b], True),
                        paired(qt_s[row, odd * HEAD:odd * HEAD + HEAD, a:b], False),
                    ],
                    axis=1,
                )
                dk_s[row, a:b, lanes] = (dot(left, right, 1, 1) * LN_2).astype(BF16)
                left = jnp.concatenate([probs[even, a:b, a:b], probs[odd, a:b, a:b]], axis=1)
                right = jnp.concatenate(
                    [paired(do_s[even % 4, :, a:b], True), paired(do_s[odd % 4, :, a:b], False)],
                    axis=1,
                )
                dv_s[row, a:b, lanes] = dot(left, right, 1, 1).astype(BF16)

        for step in range(pairs + 1):
            if step < pairs:
                score_grads(2 * step)
                score_grads(2 * step + 1)
            if step >= 1:
                grads(step - 1)
            if step == pairs // 2:
                for copy in row_stores(row)[3:6]:
                    copy.start()

    def mean(value):
        return jnp.sum(value, axis=-1, keepdims=True) * (1.0 / width)

    def weave(main, side):
        for index, step in enumerate(main):
            step()
            for part in side[index * len(side) // len(main):(index + 1) * len(side) // len(main)]:
                part()

    chunks = hidden_units // CHUNK
    piece = 32

    def feed_forward(row):
        def blocks(half, body):
            start = half * tokens
            return [
                functools.partial(body, slice(at, at + piece))
                for at in range(start, start + tokens, piece)
            ]

        def span(half):
            return slice(half * tokens, (half + 1) * tokens)

        def attended(half):
            def step(at):
                acc_s[span(half), at] = dot(ctx_s[:, span(half)], wo_s[:, at], 0, 0)

            return [
                functools.partial(step, slice(at, at + 256)) for at in range(0, width, 256)
            ]

        def norm_one(at):
            resid = x_s[row, at, :].astype(F32) + acc_s[at, :]
            center = resid - mean(resid)
            scaled = lax.rsqrt(mean(center * center) + NORM_EPS)
            normed = center * scaled
            normed_s[at, :] = normed
            rstd_s[at, :] = scaled
            low16[at, :] = (normed * gain_one + shift_one).astype(BF16)

        def forward(half):
            here = span(half)

            def run(step):
                if step < chunks:
                    at = slice(step * CHUNK, (step + 1) * CHUNK)
                    score[step % 2, here, :] = dot(low16[here, :], wx_s[:, at], 1, 0)
                if 0 <= step - 1 < chunks:
                    at = slice((step - 1) * CHUNK, step * CHUNK)
                    inner = score[(step - 1) % 2, here, :]
                    upto = 0.5 + 0.5 * lax.erf(inner * math.sqrt(0.5))
                    bell = jnp.exp2(inner * inner * (-0.5 * LOG2_E)) * (
                        1.0 / math.sqrt(2.0 * math.pi)
                    )
                    act_s[(step - 1) % 2, here, :] = (inner * upto).astype(BF16)
                    slope_s[here, at] = (upto + inner * bell).astype(BF16)
                if 0 <= step - 2:
                    at = slice((step - 2) * CHUNK, (step - 1) * CHUNK)
                    part = dot(act_s[(step - 2) % 2, here, :], wr_s[at, :], 1, 0)
                    if step == 2:
                        acc_s[here, :] = part
                    else:
                        acc_s[here, :] += part

            return [functools.partial(run, step) for step in range(chunks + 2)]

        def norm_two(at):
            z = normed_s[at, :] * gain_one + shift_one + acc_s[at, :]
            center = z - mean(z)
            scaled = lax.rsqrt(mean(center * center) + NORM_EPS)
            normed = center * scaled
            lo_s[row, at, :] = (normed * gain_two + shift_two).astype(BF16)
            weighted = og_s[row, at, :].astype(F32) * gain_two
            grad = scaled * (weighted - mean(weighted) - normed * mean(weighted * normed))
            back_s[at, :] = grad
            low16[at, :] = grad.astype(BF16)

        def backward(half):
            here = span(half)

            def run(step):
                if step < chunks:
                    at = slice(step * CHUNK, (step + 1) * CHUNK)
                    part = dot(low16[here, :], wr_s[at, :], 1, 1)
                    act_s[step % 2, here, :] = (part * slope_s[here, at].astype(F32)).astype(BF16)
                if step >= 1:
                    at = slice((step - 1) * CHUNK, step * CHUNK)
                    part = dot(act_s[(step - 1) % 2, here, :], wx_s[:, at], 1, 1)
                    if step == 1:
                        acc_s[here, :] = part
                    else:
                        acc_s[here, :] += part

            return [functools.partial(run, step) for step in range(chunks + 1)]

        def norm_one_back(at):
            weighted = (back_s[at, :] + acc_s[at, :]) * gain_one
            normed = normed_s[at, :]
            grad = rstd_s[at, :] * (
                weighted - mean(weighted) - normed * mean(weighted * normed)
            )
            g_s[row, at, :] = grad.astype(BF16)

        def context_grad(half):
            def step(at):
                gctx_s[at, span(half)] = dot(wo_s[at, :], g_s[row, span(half), :], 1, 1)

            return [
                functools.partial(step, slice(at, at + 256)) for at in range(0, width, 256)
            ]

        def turn(half):
            def step(at):
                kt_s[at, span(half)] = k_s[row, span(half), at].T
                v_s[span(half), at] = vt_s[row, at, span(half)].T

            return [
                functools.partial(step, slice(at, at + 128)) for at in range(0, width, 128)
            ]

        weave(attended(0), [])
        weave(attended(1), blocks(0, norm_one))

        weave(forward(0), blocks(1, norm_one))

        weave(forward(1), blocks(0, norm_two))
        weave(backward(0), blocks(1, norm_two))
        weave(backward(1), blocks(0, norm_one_back) + turn(0) + turn(1))
        weave(context_grad(0), blocks(1, norm_one_back))
        weave(context_grad(1), [])

    def one_row(row, carry):
        crossing = jnp.where(row == 0, crossings[0], crossings[1])

        @pl.when(crossing == 1)
        def _():
            attend_forward(row, [(0, group)])

        @pl.when(crossing == 0)
        def _():
            attend_forward(row, [(0, tokens), (tokens, group)])

        @pl.when(row == 0)
        def _():
            for copy in loads[7:13]:
                copy.wait()

        feed_forward(row)
        for copy in row_stores(row)[:3]:
            copy.start()

        @pl.when(crossing == 1)
        def _():
            attend_backward(row, [(0, group)])

        @pl.when(crossing == 0)
        def _():
            attend_backward(row, [(0, tokens), (tokens, group)])

        for copy in row_stores(row)[6:]:
            copy.start()
        from_q = dot(low_s[row], dqt_s[row], 1, 1) * (
            ADAPTER_STRENGTH / slots_rank / math.sqrt(HEAD) / LN_2
        )
        from_v = dot(low_s[row], dv_s[row], 1, 0) * (ADAPTER_STRENGTH / slots_rank)
        rank_line = lax.broadcasted_iota(jnp.int32, (2 * slots_rank, 1), 0)
        part = jnp.where(rank_line < slots_rank, from_q, from_v)
        up_s[...] = jnp.where(row == 0, part, up_s[...] + part)
        return carry

    slots_rank = low_s.shape[1] // 2
    lax.fori_loop(0, rows, one_row, 0)
    keep_up = pltpu.make_async_copy(up_s, up_out, load.at[0])
    keep_up.start()
    for row in range(rows):
        for copy in row_stores(row):
            copy.wait()
    keep_up.wait()


def phases():
    found = [("seq", 1, 2)]
    stride, left = 1, lax.axis_size("dp")
    while left > 1:
        size = 4 if left % 4 == 0 else left if left < 4 else 2
        found.append(("dp", stride, size))
        stride, left = stride * size, left // size
    return found


def finish_kernel(
    up, lo, grad, dqt, dk, dv, wq, wk, wv,
    lo_out, ig_out, up_out,
    up_s, pair, got, grad_s, dqt_s, dk_s, dv_s, wq_s, wk_s, wv_s, acc_s, res_s,
    load, store, send, recv, ar_send, ar_recv,
):
    rows, group, width = grad_s.shape
    tokens = group // 2
    place = lax.axis_index("seq")
    other = 1 - place
    plan = [
        (dqt, dqt_s), (wq, wq_s), (dk, dk_s), (wk, wk_s), (dv, dv_s), (wv, wv_s),
        (grad, grad_s), (up, up_s),
    ]
    loads = [
        pltpu.make_async_copy(source, target, load.at[index])
        for index, (source, target) in enumerate(plan)
    ]
    for copy in loads[7:] + loads[:7]:
        copy.start()
    barrier = pltpu.get_barrier_semaphore()
    rounds = []
    greeted = 0
    for axis, stride, size in phases():
        me = lax.axis_index(axis)
        digit = (me // stride) % size
        others = []
        for step in range(1, size):
            theirs = (digit + step) % size
            others.append((theirs, {axis: me + (theirs - digit) * stride}))
        for _, device in others:
            pl.semaphore_signal(barrier, inc=1, device_id=device, device_id_type=MESH)
        greeted += len(others)
        rounds.append((size, digit, others))
    pl.semaphore_wait(barrier, greeted)
    mine = pl.ds(rows * place, rows)

    def copies(index):
        size, digit, others = rounds[index]
        buffer = pair if index == 0 else got.at[index - 1]
        sends = [
            pltpu.make_async_remote_copy(
                src_ref=buffer.at[digit], dst_ref=buffer.at[digit],
                send_sem=ar_send.at[index, step], recv_sem=ar_recv.at[index, digit],
                device_id=device, device_id_type=MESH,
            )
            for step, (_, device) in enumerate(others)
        ]
        arrivals = [
            pltpu.make_async_remote_copy(
                src_ref=buffer.at[theirs], dst_ref=buffer.at[theirs],
                send_sem=ar_send.at[index, step], recv_sem=ar_recv.at[index, theirs],
                device_id=device, device_id_type=MESH,
            )
            for step, (theirs, device) in enumerate(others)
        ]
        return sends, arrivals

    def sibling(source, target, index):
        return pltpu.make_async_remote_copy(
            src_ref=source, dst_ref=target, send_sem=send.at[index], recv_sem=recv.at[index],
            device_id={"seq": other}, device_id_type=MESH,
        )

    keep_up = pltpu.make_async_copy(up_s, up_out, store.at[0])
    all_copies = [copies(index) for index in range(len(rounds))]

    def begin(index, value):
        digit = rounds[index][1]
        if index == 0:
            pair[digit] = value
        else:
            got[index - 1, digit] = value.astype(BF16)
        for copy in all_copies[index][0]:
            copy.start()

    def end(index):
        size = rounds[index][0]
        for copy in all_copies[index][1]:
            copy.wait_recv()
        buffer = pair if index == 0 else got.at[index - 1]
        value = buffer[0].astype(F32)
        for step in range(1, size):
            value = value + buffer[step].astype(F32)
        return value

    loads[7].wait()
    begin(0, up_s[...])
    lo_copy = sibling(lo, lo_out, 1)
    lo_copy.start()
    done = [0]

    def advance():
        if done[0] < len(rounds):
            value = end(done[0])
            done[0] += 1
            if done[0] < len(rounds):
                begin(done[0], value)
            else:
                up_s[...] = value
                keep_up.start()

    def from_q(half):
        span = slice(half * tokens, (half + 1) * tokens)
        left = jnp.concatenate([dqt_s[row, :, span] for row in range(rows)], axis=1)
        acc_s[...] = dot(left, wq_s[...], 0, 1)

    def part(source, weight, half):
        left = source[:, half * tokens:(half + 1) * tokens, :].reshape(rows * tokens, width)
        return dot(left, weight[...], 1, 1)

    def from_k(half):
        acc_s[...] += part(dk_s, wk_s, half)

    def from_v(half):
        span = slice(half * tokens, (half + 1) * tokens)
        value = acc_s[...] + part(dv_s, wv_s, half)
        value += grad_s[:, span, :].reshape(rows * tokens, width).astype(F32)
        res_s[half] = value.astype(BF16).reshape(rows, tokens, width)

    loads[0].wait()
    loads[1].wait()
    from_q(1)
    advance()
    loads[2].wait()
    loads[3].wait()
    from_k(1)
    for copy in loads[4:7]:
        copy.wait()
    from_v(1)
    ig_copy = sibling(res_s.at[1], ig_out.at[mine], 0)
    ig_copy.start()
    advance()
    from_q(0)
    from_k(0)
    from_v(0)
    keep_ig = pltpu.make_async_copy(res_s.at[0], ig_out.at[mine], store.at[1])
    keep_ig.start()
    for _ in range(len(rounds)):
        advance()
    for sends, _ in all_copies:
        for copy in sends:
            copy.wait_send()
    keep_up.wait()
    keep_ig.wait()
    lo_copy.wait()
    ig_copy.wait()


def widen_kernel(
    place_ref, lo, lo_got, ig, up, lo_out, ig_out, upq_out, upv_out,
    lo_s, ig_s, wide_s, up_s, load, store,
):
    micro, tokens, width = ig_s.shape
    rows = micro // 2
    place = place_ref[0]
    rest = pl.ds(rows * (1 - place), rows)
    rank = upq_out.shape[0]
    loads = [
        pltpu.make_async_copy(ig.at[index], ig_s.at[index], load.at[index])
        for index in range(micro)
    ] + [
        pltpu.make_async_copy(up, up_s, load.at[micro]),
        pltpu.make_async_copy(lo_got, lo_s, load.at[micro + 1]),
    ]
    for copy in loads:
        copy.start()
    widened = [
        pltpu.make_async_copy(wide_s.at[index], ig_out.at[index], store.at[index])
        for index in range(micro)
    ]
    for index in range(micro):
        loads[index].wait()
        wide_s[index] = ig_s[index].astype(F32)
        widened[index].start()
    stores = [
        pltpu.make_async_copy(up_s.at[pl.ds(0, rank)], upq_out, store.at[micro]),
        pltpu.make_async_copy(up_s.at[pl.ds(rank, rank)], upv_out, store.at[micro + 1]),
        pltpu.make_async_copy(lo_s, lo_out.at[rest], store.at[micro + 2]),
    ]
    for copy in loads[micro:]:
        copy.wait()
    for copy in stores:
        copy.start()
    for copy in widened + stores:
        copy.wait()


def shards(
    hidden_in, slot_sizes, live_lengths, w_query, w_key, w_value, query_down_factor, down_value,
    query_up_factor, value_up_factor, w_output, attn_gain, attn_shift, w_expand, w_reduce,
    ffn_gain, ffn_shift, out_grad,
):
    micro, tokens, width = hidden_in.shape
    rows = micro // 2
    group = 2 * tokens
    hidden_units = w_expand.shape[1]
    rank = query_down_factor.shape[1]
    shape = jax.ShapeDtypeStruct
    dma = pltpu.SemaphoreType.DMA
    wide = (rows, width, group)
    tall = (rows, group, width)
    half_tall = (rows, tokens, width)
    half_wide = (rows, width, tokens)
    square = (width, width)
    limit = 62 * 2 ** 20
    down_q, down_v = query_down_factor.T, down_value.T
    x_got, og_got, qt, keys, vt, low, wq_eff, wv_eff, down = pl.pallas_call(
        exchange_kernel,
        out_shape=[
            shape(half_tall, BF16), shape(half_tall, BF16), shape(half_wide, BF16),
            shape(half_tall, BF16), shape(half_wide, BF16), shape((rows, 2 * rank, tokens), BF16),
            shape(square, BF16), shape(square, BF16), shape((2 * rank, width), BF16),
        ],
        in_specs=[HBM_SPEC] * 5 + [VMEM_SPEC] * 4,
        out_specs=[HBM_SPEC] * 9,
        scratch_shapes=[
            VMEM(half_tall, BF16), VMEM(square, BF16), VMEM(square, BF16), VMEM(square, BF16),
            VMEM((2, width, width), F32), VMEM((2 * rank, width), BF16),
            VMEM(half_wide, BF16), VMEM(half_tall, BF16), VMEM(half_wide, BF16),
            VMEM((rows, 2 * rank, tokens), BF16),
            dma((4,)), dma((7,)), dma((2,)), dma((2,)),
        ],
        compiler_params=pltpu.CompilerParams(
            collective_id=0, has_side_effects=True, vmem_limit_bytes=limit
        ),
        name="project",
    )(
        hidden_in, out_grad, w_query, w_key, w_value, down_q, down_v,
        query_up_factor, value_up_factor,
    )
    place = lax.axis_index("seq").astype(jnp.int32).reshape(1)
    lo, lo_send, grad, dqt, dk, dv, up = pl.pallas_call(
        layer_kernel,
        out_shape=[
            shape((micro, tokens, width), BF16), shape(half_tall, BF16), shape(tall, BF16),
            shape(wide, BF16), shape(tall, BF16), shape(tall, BF16), shape((2 * rank, width), F32),
        ],
        in_specs=[SMEM_SPEC] * 3 + [HBM_SPEC] * 19,
        out_specs=[HBM_SPEC] * 7,
        scratch_shapes=[
            VMEM((4, width), F32), VMEM((2 * rank, width), BF16),
            VMEM(tall, BF16), VMEM(tall, BF16), VMEM(wide, BF16), VMEM(tall, BF16),
            VMEM(wide, BF16), VMEM((width, group), BF16), VMEM((group, width), BF16),
            VMEM((rows, 2 * rank, group), BF16),
            VMEM(square, BF16), VMEM(square, BF16), VMEM(square, BF16),
            VMEM(square, BF16), VMEM((width, hidden_units), BF16),
            VMEM((hidden_units, width), BF16),
            VMEM((HEADS, group, group), BF16), VMEM((2, group, group), F32),
            VMEM((width, group), BF16), VMEM((16, group), F32), VMEM((width, group), F32),
            VMEM((group, width), F32), VMEM((group, width), F32), VMEM((group, width), F32),
            VMEM((group, width), BF16), VMEM((group, hidden_units), BF16),
            VMEM((2, group, CHUNK), BF16), VMEM((4, group, group), BF16),
            VMEM((4, HEAD, group), BF16), VMEM((group, 1), F32),
            VMEM((rows, group, 128), BF16), VMEM((rows, 128, group), BF16),
            VMEM(tall, BF16), VMEM(tall, BF16), VMEM(wide, BF16), VMEM(tall, BF16),
            VMEM(tall, BF16), VMEM((2 * rank, width), F32),
            dma((19,)), dma((rows, 9)),
        ],
        compiler_params=pltpu.CompilerParams(vmem_limit_bytes=limit),
        name="layer",
    )(
        slot_sizes[0], live_lengths[0], place, attn_gain, attn_shift, ffn_gain, ffn_shift,
        low, down, hidden_in, out_grad, x_got, og_got,
        qt, keys, vt, wq_eff, w_key, wv_eff, w_output, w_expand, w_reduce,
    )
    count = len(phases())
    lo_got, ig, up = pl.pallas_call(
        finish_kernel,
        out_shape=[
            shape(half_tall, BF16), shape((micro, tokens, width), BF16),
            shape((2 * rank, width), F32),
        ],
        in_specs=[HBM_SPEC] * 9,
        out_specs=[HBM_SPEC] * 3,
        scratch_shapes=[
            VMEM((2 * rank, width), F32),
            VMEM((2, 2 * rank, width), F32), VMEM((count - 1, 4, 2 * rank, width), BF16),
            VMEM(tall, BF16), VMEM(wide, BF16), VMEM(tall, BF16), VMEM(tall, BF16),
            VMEM(square, BF16), VMEM(square, BF16), VMEM(square, BF16),
            VMEM((rows * tokens, width), F32), VMEM((2, rows, tokens, width), BF16),
            dma((8,)), dma((2,)), dma((2,)), dma((2,)), dma((count, 3)), dma((count, 4)),
        ],
        compiler_params=pltpu.CompilerParams(
            collective_id=1, has_side_effects=True, vmem_limit_bytes=limit
        ),
        name="finish",
    )(up, lo_send, grad, dqt, dk, dv, wq_eff, w_key, wv_eff)
    return pl.pallas_call(
        widen_kernel,
        out_shape=[
            shape((micro, tokens, width), BF16), shape((micro, tokens, width), F32),
            shape((rank, width), F32), shape((rank, width), F32),
        ],
        in_specs=[SMEM_SPEC] + [HBM_SPEC] * 4,
        out_specs=[HBM_SPEC] * 4,
        scratch_shapes=[
            VMEM(half_tall, BF16), VMEM((micro, tokens, width), BF16),
            VMEM((micro, tokens, width), F32), VMEM((2 * rank, width), F32),
            dma((micro + 2,)), dma((micro + 3,)),
        ],
        input_output_aliases={1: 0},
        compiler_params=pltpu.CompilerParams(vmem_limit_bytes=limit),
        name="widen",
    )(place, lo, lo_got, ig, up)


def solution(mesh):
    tokens = P(None, ("dp", "seq"), None)
    table = P("dp", None, None)
    in_specs = (tokens, table, table) + (P(),) * 14 + (tokens,)
    out_specs = (tokens, tokens, P(), P())
    return jax.shard_map(shards, mesh=mesh, in_specs=in_specs, out_specs=out_specs, check_vma=False)
```

```python
import functools
import math

import jax
import jax.numpy as jnp
from jax import lax
from jax.experimental import pallas as pl
from jax.experimental.pallas import tpu as pltpu
from jax.sharding import PartitionSpec as P

HEADS = 12
HEAD = 64
NORM_EPS = 1e-05
ADAPTER_STRENGTH = 16.0
MASK_FILL = -1e30
LOG2_E = math.log2(math.e)
LN_2 = math.log(2.0)
CHUNK = 512
BF16 = jnp.bfloat16
F32 = jnp.float32
MESH = pl.DeviceIdType.MESH
VMEM = pltpu.VMEM
HBM_SPEC = pl.BlockSpec(memory_space=pl.ANY)
VMEM_SPEC = pl.BlockSpec(memory_space=pltpu.VMEM)
SMEM_SPEC = pl.BlockSpec(memory_space=pltpu.SMEM)


def dot(left, right, over_left, over_right):
    return lax.dot_general(
        left, right, (((over_left,), (over_right,)), ((), ())), preferred_element_type=F32
    )


def exchange_kernel(
    hidden, out_grad, wq, wk, wv, aq, av, bq, bv,
    x_out, og_out, qt_out, k_out, vt_out, low_out, wq_out, wv_out, down_out,
    x_s, wq_s, wk_s, wv_s, delta_s, down_s, qt_s, k_s, vt_s, low_s,
    load, store, send, recv,
):
    rows, tokens, width = x_s.shape
    place = lax.axis_index("seq")
    other = 1 - place
    loads = [
        pltpu.make_async_copy(source, target, load.at[index])
        for index, (source, target) in enumerate([
            (wk, wk_s), (hidden.at[pl.ds(rows * place, rows)], x_s), (wq, wq_s), (wv, wv_s),
        ])
    ]
    for copy in loads[:2]:
        copy.start()
    barrier = pltpu.get_barrier_semaphore()
    pl.semaphore_signal(barrier, inc=1, device_id={"seq": other}, device_id_type=MESH)
    pl.semaphore_wait(barrier, 1)
    remote = [
        pltpu.make_async_remote_copy(
            src_ref=source.at[pl.ds(rows * other, rows)], dst_ref=target,
            send_sem=send.at[index], recv_sem=recv.at[index],
            device_id={"seq": other}, device_id_type=MESH,
        )
        for index, (source, target) in enumerate([(hidden, x_out), (out_grad, og_out)])
    ]
    for copy in remote:
        copy.start()
    strength = ADAPTER_STRENGTH / aq.shape[0]
    stores = []

    def keep(source, target):
        copy = pltpu.make_async_copy(source, target, store.at[len(stores)])
        copy.start()
        stores.append(copy)

    for copy in loads[2:]:
        copy.start()
    thirds = [slice(at, at + 256) for at in range(0, width, 256)]
    for at in thirds:
        delta_s[0, at, :] = dot(aq[:, at], bq[...], 0, 0) * strength
        delta_s[1, at, :] = dot(av[:, at], bv[...], 0, 0) * strength
    down_s[...] = jnp.concatenate(
        [aq[...].astype(F32), av[...].astype(F32)], axis=0
    ).astype(BF16)
    keep(down_s, down_out)
    for copy in loads[:2]:
        copy.wait()
    x = x_s[...].reshape(rows * tokens, width)

    def fold(weight, index, scale, at):
        weight[at, :] = ((weight[at, :].astype(F32) + delta_s[index, at, :]) * scale).astype(BF16)

    def project(weight, target, at):
        part = dot(weight[:, at], x, 0, 1).astype(BF16)
        for row in range(rows):
            target[row, at, :] = part[:, row * tokens:(row + 1) * tokens]

    for at in thirds:
        k_s[:, :, at] = dot(x, wk_s[:, at], 1, 0).astype(BF16).reshape(rows, tokens, 256)
    for copy in loads[2:]:
        copy.wait()
    for at in thirds:
        fold(wq_s, 0, LOG2_E / math.sqrt(HEAD), at)
    keep(k_s, k_out)
    keep(wq_s, wq_out)
    for at in thirds:
        project(wq_s, qt_s, at)
        fold(wv_s, 1, 1.0, at)
    keep(qt_s, qt_out)
    keep(wv_s, wv_out)
    low = dot(down_s[...], x, 1, 1).astype(BF16)
    for row in range(rows):
        low_s[row] = low[:, row * tokens:(row + 1) * tokens]
    keep(low_s, low_out)
    for at in thirds:
        project(wv_s, vt_s, at)
    keep(vt_s, vt_out)
    for copy in stores:
        copy.wait()
    for copy in remote:
        copy.wait()


def layer_kernel(
    sizes, lives, place_ref, *refs
):
    (
        gain_one, shift_one, gain_two, shift_two, low_in, down_in,
        hidden, out_grad, x_in, og_in, qt_in, k_in, vt_in, wq_in, wk_in, wv_in,
        wo_in, wx_in, wr_in,
        lo_out, lo_send, g_out, dqt_out, dk_out, dv_out, up_out,
        vec_s, down_s, x_s, og_s, qt_s, k_s, vt_s, kt_s, v_s, low_s, wq_s, wk_s, wv_s,
        wo_s, wx_s, wr_s, probs, score, ctx_s, inv_s, gctx_s, normed_s, back_s, acc_s, low16,
        slope_s, act_s, ds_s, do_s, rstd_s, kmask, qmask, lo_s, g_s, dqt_s, dk_s, dv_s, up_s,
        load, store,
    ) = refs
    rows, group, width = x_s.shape
    tokens = group // 2
    hidden_units = wx_s.shape[1]
    place = place_ref[0]
    slots = sizes.shape[1]
    pairs = HEADS // 2
    first = pl.ds(0, tokens)
    second = pl.ds(tokens, tokens)
    mine = pl.ds(rows * place, rows)
    plan = [
        (x_in, x_s.at[:, second]),
        (wk_in, wk_s),
        (wq_in, wq_s),
        (wv_in, wv_s),
        (qt_in, qt_s.at[:, :, first]),
        (k_in, k_s.at[:, first]),
        (vt_in, vt_s.at[:, :, first]),
        (wo_in, wo_s),
        (hidden.at[mine], x_s.at[:, first]),
        (wx_in, wx_s),
        (wr_in, wr_s),
        (out_grad.at[mine], og_s.at[:, first]),
        (og_in, og_s.at[:, second]),
        (down_in, down_s),
        (low_in, low_s.at[:, :, first]),
    ] + [
        (vector, vec_s.at[index])
        for index, vector in enumerate((gain_one, shift_one, gain_two, shift_two))
    ]
    loads = [
        pltpu.make_async_copy(source, target, load.at[index])
        for index, (source, target) in enumerate(plan)
    ]
    small = loads[13:]
    for copy in loads[:2] + small + loads[2:13]:
        copy.start()

    def row_stores(row):
        plan = [
            (lo_s.at[row, first], lo_out.at[rows * place + row]),
            (lo_s.at[row, second], lo_send.at[row]),
            (g_s.at[row], g_out.at[row]),
        ]
        for at in (pl.ds(0, width // 2), pl.ds(width // 2, width // 2)):
            plan += [
                (dqt_s.at[row, at], dqt_out.at[row, at]),
                (dk_s.at[row, :, at], dk_out.at[row, :, at]),
                (dv_s.at[row, :, at], dv_out.at[row, :, at]),
            ]
        return [
            pltpu.make_async_copy(source, target, store.at[row, index])
            for index, (source, target) in enumerate(plan)
        ]

    def make_masks(row):
        own = rows * place + row
        position = (lax.broadcasted_iota(jnp.int32, (group, 128), 0) + place * tokens) % group
        lane = lax.broadcasted_iota(jnp.int32, (1, 128), 1)
        low_end = jnp.full((1, 128), group, jnp.int32)
        high_end = low_end
        across = lax.broadcasted_iota(jnp.int32, (slots, group), 1)
        across = (across + place * tokens) % group
        line = lax.broadcasted_iota(jnp.int32, (slots, 1), 0)
        begin = jnp.full((slots, 1), group, jnp.int32)
        last = begin
        start = jnp.int32(0)
        crossing = jnp.int32(0)
        for slot in range(slots):
            size = sizes[own, slot]
            live = lives[own, slot]
            low_end = jnp.where(lane == slot, start, low_end)
            high_end = jnp.where(lane == slot, start + live, high_end)
            begin = jnp.where(line == slot, start, begin)
            last = jnp.where(line == slot, start + size, last)
            over = (start < tokens) & (start + size > tokens)
            crossing = jnp.where(over, 1, crossing)
            start = start + size
        dead = jnp.where((position >= low_end) & (position < high_end), 0.0, 1.0)
        kmask[row] = jnp.where(lane < slots, dead, 0.0).astype(BF16)
        within = jnp.where((across >= begin) & (across < last), MASK_FILL, 0.0)
        qmask[row] = jnp.concatenate(
            [within, jnp.zeros((128 - slots, group), F32)], axis=0
        ).astype(BF16)
        return crossing

    crossings = [make_masks(row) for row in range(rows)]
    loads[0].wait()
    loads[1].wait()
    x = x_s[:, tokens:, :].reshape(rows * tokens, width)
    k_s[:, tokens:, :] = dot(x, wk_s[...], 1, 0).astype(BF16).reshape(rows, tokens, width)
    for copy in small:
        copy.wait()
    low = dot(down_s[...], x, 1, 1).astype(BF16)
    for row in range(rows):
        low_s[row, :, tokens:] = low[:, row * tokens:(row + 1) * tokens]
    for weight, target, copy in ((wq_s, qt_s, loads[2]), (wv_s, vt_s, loads[3])):
        copy.wait()
        part = dot(weight[...], x, 0, 1).astype(BF16)
        for row in range(rows):
            target[row, :, tokens:] = part[:, row * tokens:(row + 1) * tokens]
    for copy in loads[4:7]:
        copy.wait()

    gain_one, shift_one, gain_two, shift_two = (
        vec_s[index].reshape(1, width) for index in range(4)
    )

    def paired(top, bottom_zero):
        zero = jnp.zeros_like(top)
        return jnp.concatenate([top, zero] if bottom_zero else [zero, top], axis=0)

    def attend_forward(row, spans):
        def scores(head):
            pair, odd = divmod(head, 2)
            lanes = slice(pair * 128, pair * 128 + 128)
            query = qt_s[row, head * HEAD:(head + 1) * HEAD, :]
            right = jnp.concatenate([paired(query, odd == 0), qmask[row]], axis=0)
            for a, b in spans:
                left = jnp.concatenate([k_s[row, a:b, lanes], kmask[row, a:b, :]], axis=1)
                score[head % 2, a:b, a:b] = dot(left, right[:, a:b], 1, 0)

        def weights(head):
            for a, b in spans:
                part = score[head % 2, a:b, a:b]
                top = jnp.max(part, axis=0, keepdims=True)
                probs[head, a:b, a:b] = jnp.exp2(part - top).astype(BF16)

        def contexts(head):
            values = vt_s[row, head * HEAD:(head + 1) * HEAD, :]
            left = jnp.concatenate([values, jnp.ones((16, group), BF16)], axis=0)
            for a, b in spans:
                total = dot(left[:, a:b], probs[head, a:b, a:b], 1, 0)
                inverse = 1.0 / total[HEAD:HEAD + 1]
                inv_s[head:head + 1, a:b] = inverse
                ctx_s[head * HEAD:(head + 1) * HEAD, a:b] = (total[:HEAD] * inverse).astype(BF16)

        for step in range(HEADS + 2):
            if step < HEADS:
                scores(step)
            if 0 <= step - 1 < HEADS:
                weights(step - 1)
            if 0 <= step - 2:
                contexts(step - 2)

    def attend_backward(row, spans):
        def score_grads(head):
            pair, odd = divmod(head, 2)
            lanes = slice(pair * 128, pair * 128 + 128)
            here = slice(head * HEAD, (head + 1) * HEAD)
            slot = head % 4
            grad = gctx_s[here, :] * inv_s[head:head + 1, :]
            short = grad.astype(BF16)
            do_s[slot] = short
            delta = -jnp.sum(grad * ctx_s[here, :].astype(F32), axis=0, keepdims=True)
            high = delta.astype(BF16).astype(F32)
            index = lax.broadcasted_iota(jnp.int32, (16, group), 0)
            extra = jnp.where(index == 0, high, jnp.where(index == 1, delta - high, 0.0))
            right = jnp.concatenate(
                [paired(short, odd == 0), extra.astype(BF16), jnp.zeros((112, group), BF16)], axis=0
            )
            for a, b in spans:
                left = jnp.concatenate(
                    [v_s[a:b, lanes], jnp.ones((b - a, 128), BF16)], axis=1
                )
                part = dot(left, right[:, a:b], 1, 0)
                ds_s[slot, a:b, a:b] = (probs[head, a:b, a:b].astype(F32) * part).astype(BF16)

        def grads(pair):
            even, odd = 2 * pair, 2 * pair + 1
            for a, b in spans:
                for head in (even, odd):
                    here = slice(head * HEAD, (head + 1) * HEAD)
                    dqt_s[row, here, a:b] = (
                        dot(kt_s[here, a:b], ds_s[head % 4, a:b, a:b], 1, 0) * LN_2
                    ).astype(BF16)
                lanes = slice(pair * 128, pair * 128 + 128)
                left = jnp.concatenate([ds_s[even % 4, a:b, a:b], ds_s[odd % 4, a:b, a:b]], axis=1)
                right = jnp.concatenate(
                    [
                        paired(qt_s[row, even * HEAD:even * HEAD + HEAD, a:b], True),
                        paired(qt_s[row, odd * HEAD:odd * HEAD + HEAD, a:b], False),
                    ],
                    axis=1,
                )
                dk_s[row, a:b, lanes] = (dot(left, right, 1, 1) * LN_2).astype(BF16)
                left = jnp.concatenate([probs[even, a:b, a:b], probs[odd, a:b, a:b]], axis=1)
                right = jnp.concatenate(
                    [paired(do_s[even % 4, :, a:b], True), paired(do_s[odd % 4, :, a:b], False)],
                    axis=1,
                )
                dv_s[row, a:b, lanes] = dot(left, right, 1, 1).astype(BF16)

        for step in range(pairs + 1):
            if step < pairs:
                score_grads(2 * step)
                score_grads(2 * step + 1)
            if step >= 1:
                grads(step - 1)
            if step == pairs // 2:
                for copy in row_stores(row)[3:6]:
                    copy.start()

    def mean(value):
        return jnp.sum(value, axis=-1, keepdims=True) * (1.0 / width)

    def weave(main, side):
        for index, step in enumerate(main):
            step()
            for part in side[index * len(side) // len(main):(index + 1) * len(side) // len(main)]:
                part()

    chunks = hidden_units // CHUNK
    piece = 32

    def feed_forward(row):
        def blocks(half, body):
            start = half * tokens
            return [
                functools.partial(body, slice(at, at + piece))
                for at in range(start, start + tokens, piece)
            ]

        def span(half):
            return slice(half * tokens, (half + 1) * tokens)

        def attended(half):
            def step(at):
                acc_s[span(half), at] = dot(ctx_s[:, span(half)], wo_s[:, at], 0, 0)

            return [
                functools.partial(step, slice(at, at + 256)) for at in range(0, width, 256)
            ]

        def norm_one(at):
            resid = x_s[row, at, :].astype(F32) + acc_s[at, :]
            center = resid - mean(resid)
            scaled = lax.rsqrt(mean(center * center) + NORM_EPS)
            normed = center * scaled
            normed_s[at, :] = normed
            rstd_s[at, :] = scaled
            low16[at, :] = (normed * gain_one + shift_one).astype(BF16)

        def forward(half):
            here = span(half)

            def run(step):
                if step < chunks:
                    at = slice(step * CHUNK, (step + 1) * CHUNK)
                    score[step % 2, here, :] = dot(low16[here, :], wx_s[:, at], 1, 0)
                if 0 <= step - 1 < chunks:
                    at = slice((step - 1) * CHUNK, step * CHUNK)
                    inner = score[(step - 1) % 2, here, :]
                    upto = 0.5 + 0.5 * lax.erf(inner * math.sqrt(0.5))
                    bell = jnp.exp2(inner * inner * (-0.5 * LOG2_E)) * (
                        1.0 / math.sqrt(2.0 * math.pi)
                    )
                    act_s[(step - 1) % 2, here, :] = (inner * upto).astype(BF16)
                    slope_s[here, at] = (upto + inner * bell).astype(BF16)
                if 0 <= step - 2:
                    at = slice((step - 2) * CHUNK, (step - 1) * CHUNK)
                    part = dot(act_s[(step - 2) % 2, here, :], wr_s[at, :], 1, 0)
                    if step == 2:
                        acc_s[here, :] = part
                    else:
                        acc_s[here, :] += part

            return [functools.partial(run, step) for step in range(chunks + 2)]

        def norm_two(at):
            z = normed_s[at, :] * gain_one + shift_one + acc_s[at, :]
            center = z - mean(z)
            scaled = lax.rsqrt(mean(center * center) + NORM_EPS)
            normed = center * scaled
            lo_s[row, at, :] = (normed * gain_two + shift_two).astype(BF16)
            weighted = og_s[row, at, :].astype(F32) * gain_two
            grad = scaled * (weighted - mean(weighted) - normed * mean(weighted * normed))
            back_s[at, :] = grad
            low16[at, :] = grad.astype(BF16)

        def backward(half):
            here = span(half)

            def run(step):
                if step < chunks:
                    at = slice(step * CHUNK, (step + 1) * CHUNK)
                    part = dot(low16[here, :], wr_s[at, :], 1, 1)
                    act_s[step % 2, here, :] = (part * slope_s[here, at].astype(F32)).astype(BF16)
                if step >= 1:
                    at = slice((step - 1) * CHUNK, step * CHUNK)
                    part = dot(act_s[(step - 1) % 2, here, :], wx_s[:, at], 1, 1)
                    if step == 1:
                        acc_s[here, :] = part
                    else:
                        acc_s[here, :] += part

            return [functools.partial(run, step) for step in range(chunks + 1)]

        def norm_one_back(at):
            weighted = (back_s[at, :] + acc_s[at, :]) * gain_one
            normed = normed_s[at, :]
            grad = rstd_s[at, :] * (
                weighted - mean(weighted) - normed * mean(weighted * normed)
            )
            g_s[row, at, :] = grad.astype(BF16)

        def context_grad(half):
            def step(at):
                gctx_s[at, span(half)] = dot(wo_s[at, :], g_s[row, span(half), :], 1, 1)

            return [
                functools.partial(step, slice(at, at + 256)) for at in range(0, width, 256)
            ]

        def turn(half):
            def step(at):
                kt_s[at, span(half)] = k_s[row, span(half), at].T
                v_s[span(half), at] = vt_s[row, at, span(half)].T

            return [
                functools.partial(step, slice(at, at + 128)) for at in range(0, width, 128)
            ]

        weave(attended(0), [])
        weave(attended(1), blocks(0, norm_one))

        weave(forward(0), blocks(1, norm_one))

        weave(forward(1), blocks(0, norm_two))
        weave(backward(0), blocks(1, norm_two))
        weave(backward(1), blocks(0, norm_one_back) + turn(0) + turn(1))
        weave(context_grad(0), blocks(1, norm_one_back))
        weave(context_grad(1), [])

    def one_row(row, carry):
        crossing = jnp.where(row == 0, crossings[0], crossings[1])

        @pl.when(crossing == 1)
        def _():
            attend_forward(row, [(0, group)])

        @pl.when(crossing == 0)
        def _():
            attend_forward(row, [(0, tokens), (tokens, group)])

        @pl.when(row == 0)
        def _():
            for copy in loads[7:13]:
                copy.wait()

        feed_forward(row)
        for copy in row_stores(row)[:3]:
            copy.start()

        @pl.when(crossing == 1)
        def _():
            attend_backward(row, [(0, group)])

        @pl.when(crossing == 0)
        def _():
            attend_backward(row, [(0, tokens), (tokens, group)])

        for copy in row_stores(row)[6:]:
            copy.start()
        from_q = dot(low_s[row], dqt_s[row], 1, 1) * (
            ADAPTER_STRENGTH / slots_rank / math.sqrt(HEAD) / LN_2
        )
        from_v = dot(low_s[row], dv_s[row], 1, 0) * (ADAPTER_STRENGTH / slots_rank)
        rank_line = lax.broadcasted_iota(jnp.int32, (2 * slots_rank, 1), 0)
        part = jnp.where(rank_line < slots_rank, from_q, from_v)
        up_s[...] = jnp.where(row == 0, part, up_s[...] + part)
        return carry

    slots_rank = low_s.shape[1] // 2
    lax.fori_loop(0, rows, one_row, 0)
    keep_up = pltpu.make_async_copy(up_s, up_out, load.at[0])
    keep_up.start()
    for row in range(rows):
        for copy in row_stores(row):
            copy.wait()
    keep_up.wait()


def phases():
    found = [("seq", 1, 2)]
    stride, left = 1, lax.axis_size("dp")
    while left > 1:
        size = 4 if left % 4 == 0 else left if left < 4 else 2
        found.append(("dp", stride, size))
        stride, left = stride * size, left // size
    return found


def finish_kernel(
    up, lo, grad, dqt, dk, dv, wq, wk, wv,
    lo_out, ig_out, up_out,
    up_s, pair, got, grad_s, dqt_s, dk_s, dv_s, wq_s, wk_s, wv_s, acc_s, res_s,
    load, store, send, recv, ar_send, ar_recv,
):
    rows, group, width = grad_s.shape
    tokens = group // 2
    place = lax.axis_index("seq")
    other = 1 - place
    plan = [
        (dqt, dqt_s), (wq, wq_s), (dk, dk_s), (wk, wk_s), (dv, dv_s), (wv, wv_s),
        (grad, grad_s), (up, up_s),
    ]
    loads = [
        pltpu.make_async_copy(source, target, load.at[index])
        for index, (source, target) in enumerate(plan)
    ]
    for copy in loads[7:] + loads[:7]:
        copy.start()
    barrier = pltpu.get_barrier_semaphore()
    rounds = []
    greeted = 0
    for axis, stride, size in phases():
        me = lax.axis_index(axis)
        digit = (me // stride) % size
        others = []
        for step in range(1, size):
            theirs = (digit + step) % size
            others.append((theirs, {axis: me + (theirs - digit) * stride}))
        for _, device in others:
            pl.semaphore_signal(barrier, inc=1, device_id=device, device_id_type=MESH)
        greeted += len(others)
        rounds.append((size, digit, others))
    pl.semaphore_wait(barrier, greeted)
    mine = pl.ds(rows * place, rows)

    def buffer_of(index, half):
        return pair if index == 0 else got.at[index - 1, half]

    def copies(index, half):
        _, digit, others = rounds[index]
        buffer = buffer_of(index, half)
        sends = [
            pltpu.make_async_remote_copy(
                src_ref=buffer.at[digit], dst_ref=buffer.at[digit],
                send_sem=ar_send.at[index, half, step], recv_sem=ar_recv.at[index, half, digit],
                device_id=device, device_id_type=MESH,
            )
            for step, (_, device) in enumerate(others)
        ]
        arrivals = [
            pltpu.make_async_remote_copy(
                src_ref=buffer.at[theirs], dst_ref=buffer.at[theirs],
                send_sem=ar_send.at[index, half, step], recv_sem=ar_recv.at[index, half, theirs],
                device_id=device, device_id_type=MESH,
            )
            for step, (theirs, device) in enumerate(others)
        ]
        return sends, arrivals

    def sibling(source, target, index):
        return pltpu.make_async_remote_copy(
            src_ref=source, dst_ref=target, send_sem=send.at[index], recv_sem=recv.at[index],
            device_id={"seq": other}, device_id_type=MESH,
        )

    keep_up = pltpu.make_async_copy(up_s, up_out, store.at[0])
    last = len(rounds) - 1
    turns = [[(0, 0)]] + [[(1 + turn, 0), (last - turn, 1)] for turn in range(last)]
    all_copies = [[copies(index, half) for index, half in turn] for turn in turns]

    def begin(turn, values):
        for (index, half), value, (sends, _) in zip(turns[turn], values, all_copies[turn]):
            buffer_of(index, half)[rounds[index][1]] = value.astype(
                F32 if index == 0 else BF16
            )
            for copy in sends:
                copy.start()

    def end(turn):
        values = []
        for (index, half), (_, arrivals) in zip(turns[turn], all_copies[turn]):
            for copy in arrivals:
                copy.wait_recv()
            buffer = buffer_of(index, half)
            value = buffer[0].astype(F32)
            for step in range(1, rounds[index][0]):
                value = value + buffer[step].astype(F32)
            values.append(value)
        return values

    loads[7].wait()
    begin(0, [up_s[...]])
    lo_copy = sibling(lo, lo_out, 1)
    lo_copy.start()
    done = [0]

    def advance():
        if done[0] < len(turns):
            values = end(done[0])
            done[0] += 1
            if done[0] == 1:
                values = [values[0][:, :width // 2], values[0][:, width // 2:]]
            if done[0] < len(turns):
                begin(done[0], values)
            else:
                up_s[...] = jnp.concatenate(values, axis=1)
                keep_up.start()

    def from_q(half):
        span = slice(half * tokens, (half + 1) * tokens)
        left = jnp.concatenate([dqt_s[row, :, span] for row in range(rows)], axis=1)
        acc_s[...] = dot(left, wq_s[...], 0, 1)

    def part(source, weight, half):
        left = source[:, half * tokens:(half + 1) * tokens, :].reshape(rows * tokens, width)
        return dot(left, weight[...], 1, 1)

    def from_k(half):
        acc_s[...] += part(dk_s, wk_s, half)

    def from_v(half):
        span = slice(half * tokens, (half + 1) * tokens)
        value = acc_s[...] + part(dv_s, wv_s, half)
        value += grad_s[:, span, :].reshape(rows * tokens, width).astype(F32)
        res_s[half] = value.astype(BF16).reshape(rows, tokens, width)

    loads[0].wait()
    loads[1].wait()
    from_q(1)
    advance()
    loads[2].wait()
    loads[3].wait()
    from_k(1)
    for copy in loads[4:7]:
        copy.wait()
    from_v(1)
    ig_copy = sibling(res_s.at[1], ig_out.at[mine], 0)
    ig_copy.start()
    advance()
    from_q(0)
    from_k(0)
    from_v(0)
    keep_ig = pltpu.make_async_copy(res_s.at[0], ig_out.at[mine], store.at[1])
    keep_ig.start()
    for _ in range(len(rounds)):
        advance()
    for turn in all_copies:
        for sends, _ in turn:
            for copy in sends:
                copy.wait_send()
    keep_up.wait()
    keep_ig.wait()
    lo_copy.wait()
    ig_copy.wait()


def widen_kernel(
    place_ref, lo, lo_got, ig, up, lo_out, ig_out, upq_out, upv_out,
    lo_s, ig_s, wide_s, up_s, load, store,
):
    micro, tokens, width = ig_s.shape
    rows = micro // 2
    place = place_ref[0]
    rest = pl.ds(rows * (1 - place), rows)
    rank = upq_out.shape[0]
    loads = [
        pltpu.make_async_copy(ig.at[index], ig_s.at[index], load.at[index])
        for index in range(micro)
    ] + [
        pltpu.make_async_copy(up, up_s, load.at[micro]),
        pltpu.make_async_copy(lo_got, lo_s, load.at[micro + 1]),
    ]
    for copy in loads:
        copy.start()
    widened = [
        pltpu.make_async_copy(wide_s.at[index], ig_out.at[index], store.at[index])
        for index in range(micro)
    ]
    for index in range(micro):
        loads[index].wait()
        wide_s[index] = ig_s[index].astype(F32)
        widened[index].start()
    stores = [
        pltpu.make_async_copy(up_s.at[pl.ds(0, rank)], upq_out, store.at[micro]),
        pltpu.make_async_copy(up_s.at[pl.ds(rank, rank)], upv_out, store.at[micro + 1]),
        pltpu.make_async_copy(lo_s, lo_out.at[rest], store.at[micro + 2]),
    ]
    for copy in loads[micro:]:
        copy.wait()
    for copy in stores:
        copy.start()
    for copy in widened + stores:
        copy.wait()


def shards(
    hidden_in, slot_sizes, live_lengths, w_query, w_key, w_value, query_down_factor, down_value,
    query_up_factor, value_up_factor, w_output, attn_gain, attn_shift, w_expand, w_reduce,
    ffn_gain, ffn_shift, out_grad,
):
    micro, tokens, width = hidden_in.shape
    rows = micro // 2
    group = 2 * tokens
    hidden_units = w_expand.shape[1]
    rank = query_down_factor.shape[1]
    shape = jax.ShapeDtypeStruct
    dma = pltpu.SemaphoreType.DMA
    wide = (rows, width, group)
    tall = (rows, group, width)
    half_tall = (rows, tokens, width)
    half_wide = (rows, width, tokens)
    square = (width, width)
    limit = 62 * 2 ** 20
    down_q, down_v = query_down_factor.T, down_value.T
    x_got, og_got, qt, keys, vt, low, wq_eff, wv_eff, down = pl.pallas_call(
        exchange_kernel,
        out_shape=[
            shape(half_tall, BF16), shape(half_tall, BF16), shape(half_wide, BF16),
            shape(half_tall, BF16), shape(half_wide, BF16), shape((rows, 2 * rank, tokens), BF16),
            shape(square, BF16), shape(square, BF16), shape((2 * rank, width), BF16),
        ],
        in_specs=[HBM_SPEC] * 5 + [VMEM_SPEC] * 4,
        out_specs=[HBM_SPEC] * 9,
        scratch_shapes=[
            VMEM(half_tall, BF16), VMEM(square, BF16), VMEM(square, BF16), VMEM(square, BF16),
            VMEM((2, width, width), F32), VMEM((2 * rank, width), BF16),
            VMEM(half_wide, BF16), VMEM(half_tall, BF16), VMEM(half_wide, BF16),
            VMEM((rows, 2 * rank, tokens), BF16),
            dma((4,)), dma((7,)), dma((2,)), dma((2,)),
        ],
        compiler_params=pltpu.CompilerParams(
            collective_id=0, has_side_effects=True, vmem_limit_bytes=limit
        ),
        name="project",
    )(
        hidden_in, out_grad, w_query, w_key, w_value, down_q, down_v,
        query_up_factor, value_up_factor,
    )
    place = lax.axis_index("seq").astype(jnp.int32).reshape(1)
    lo, lo_send, grad, dqt, dk, dv, up = pl.pallas_call(
        layer_kernel,
        out_shape=[
            shape((micro, tokens, width), BF16), shape(half_tall, BF16), shape(tall, BF16),
            shape(wide, BF16), shape(tall, BF16), shape(tall, BF16), shape((2 * rank, width), F32),
        ],
        in_specs=[SMEM_SPEC] * 3 + [HBM_SPEC] * 19,
        out_specs=[HBM_SPEC] * 7,
        scratch_shapes=[
            VMEM((4, width), F32), VMEM((2 * rank, width), BF16),
            VMEM(tall, BF16), VMEM(tall, BF16), VMEM(wide, BF16), VMEM(tall, BF16),
            VMEM(wide, BF16), VMEM((width, group), BF16), VMEM((group, width), BF16),
            VMEM((rows, 2 * rank, group), BF16),
            VMEM(square, BF16), VMEM(square, BF16), VMEM(square, BF16),
            VMEM(square, BF16), VMEM((width, hidden_units), BF16),
            VMEM((hidden_units, width), BF16),
            VMEM((HEADS, group, group), BF16), VMEM((2, group, group), F32),
            VMEM((width, group), BF16), VMEM((16, group), F32), VMEM((width, group), F32),
            VMEM((group, width), F32), VMEM((group, width), F32), VMEM((group, width), F32),
            VMEM((group, width), BF16), VMEM((group, hidden_units), BF16),
            VMEM((2, group, CHUNK), BF16), VMEM((4, group, group), BF16),
            VMEM((4, HEAD, group), BF16), VMEM((group, 1), F32),
            VMEM((rows, group, 128), BF16), VMEM((rows, 128, group), BF16),
            VMEM(tall, BF16), VMEM(tall, BF16), VMEM(wide, BF16), VMEM(tall, BF16),
            VMEM(tall, BF16), VMEM((2 * rank, width), F32),
            dma((19,)), dma((rows, 9)),
        ],
        compiler_params=pltpu.CompilerParams(vmem_limit_bytes=limit),
        name="layer",
    )(
        slot_sizes[0], live_lengths[0], place, attn_gain, attn_shift, ffn_gain, ffn_shift,
        low, down, hidden_in, out_grad, x_got, og_got,
        qt, keys, vt, wq_eff, w_key, wv_eff, w_output, w_expand, w_reduce,
    )
    count = len(phases())
    lo_got, ig, up = pl.pallas_call(
        finish_kernel,
        out_shape=[
            shape(half_tall, BF16), shape((micro, tokens, width), BF16),
            shape((2 * rank, width), F32),
        ],
        in_specs=[HBM_SPEC] * 9,
        out_specs=[HBM_SPEC] * 3,
        scratch_shapes=[
            VMEM((2 * rank, width), F32),
            VMEM((2, 2 * rank, width), F32), VMEM((count - 1, 2, 4, 2 * rank, width // 2), BF16),
            VMEM(tall, BF16), VMEM(wide, BF16), VMEM(tall, BF16), VMEM(tall, BF16),
            VMEM(square, BF16), VMEM(square, BF16), VMEM(square, BF16),
            VMEM((rows * tokens, width), F32), VMEM((2, rows, tokens, width), BF16),
            dma((8,)), dma((2,)), dma((2,)), dma((2,)), dma((count, 2, 3)), dma((count, 2, 4)),
        ],
        compiler_params=pltpu.CompilerParams(
            collective_id=1, has_side_effects=True, vmem_limit_bytes=limit
        ),
        name="finish",
    )(up, lo_send, grad, dqt, dk, dv, wq_eff, w_key, wv_eff)
    return pl.pallas_call(
        widen_kernel,
        out_shape=[
            shape((micro, tokens, width), BF16), shape((micro, tokens, width), F32),
            shape((rank, width), F32), shape((rank, width), F32),
        ],
        in_specs=[SMEM_SPEC] + [HBM_SPEC] * 4,
        out_specs=[HBM_SPEC] * 4,
        scratch_shapes=[
            VMEM(half_tall, BF16), VMEM((micro, tokens, width), BF16),
            VMEM((micro, tokens, width), F32), VMEM((2 * rank, width), F32),
            dma((micro + 2,)), dma((micro + 3,)),
        ],
        input_output_aliases={1: 0},
        compiler_params=pltpu.CompilerParams(vmem_limit_bytes=limit),
        name="widen",
    )(place, lo, lo_got, ig, up)


def solution(mesh):
    tokens = P(None, ("dp", "seq"), None)
    table = P("dp", None, None)
    in_specs = (tokens, table, table) + (P(),) * 14 + (tokens,)
    out_specs = (tokens, tokens, P(), P())
    return jax.shard_map(shards, mesh=mesh, in_specs=in_specs, out_specs=out_specs, check_vma=False)
```
